32 devices in a mesh: dp: 8 (over z, x), mp: 4 (over y, core).
Axes of the slice: x: 2, y: 2, z: 4, core: 2. Of those that a mesh axis runs over, the one named last changes fastest.
Arguments:
- tokens: bfloat16 [16384, 768], P('dp'), may hold values from -6 to 6
- w_qkv: bfloat16 [3, 768, 768], P(None, None, 'mp'), may hold values from -0.21875 to 0.21875
- b_qv: float32 [2, 768], P(None, 'mp'), may hold values from -2 to 2
- w_out: bfloat16 [768, 768], P('mp'), may hold values from -0.875 to 0.875
- b_out: float32 [768], replicated, may hold values from -2 to 2
- norm1_gain: float32 [768], replicated, may hold values from 0.5 to 1.5
- norm1_shift: float32 [768], replicated, may hold values from -1.5 to 1.5
- w_in: bfloat16 [768, 3072], P(None, 'mp'), may hold values from -0.21875 to 0.21875
- b_in: float32 [3072], P('mp'), may hold values from -2 to 2
- w_back: bfloat16 [3072, 768], P('mp'), may hold values from -0.15625 to 0.15625
- b_back: float32 [768], replicated, may hold values from -1.5 to 1.5
- norm2_gain: float32 [768], replicated, may hold values from 0.5 to 1.5
- norm2_shift: float32 [768], replicated, may hold values from -0.4 to 0.4
- segment_ids: int32 [32, 512], P('dp'), may hold values from 0 to 15, never falling along the last dimension, each value on 1 to 64 neighbouring positions
- pair_ids: int32 [32, 8], P('dp'), may hold values from 0 to 255
Outputs:
- loss: float32 [], replicated
- layer_out: bfloat16 [16384, 768], P('dp')
- d_tokens: bfloat16 [16384, 768], P('dp')
- d_w_qkv: float32 [3, 768, 768], P(None, None, 'mp')
- d_b_qv: float32 [2, 768], P(None, 'mp')
- d_w_out: float32 [768, 768], P('mp')
- d_b_out: float32 [768], P('mp')
- d_norm1_gain: float32 [768], P('mp')
- d_norm1_shift: float32 [768], P('mp')
- d_w_in: float32 [768, 3072], P(None, 'mp')
- d_b_in: float32 [3072], P('mp')
- d_w_back: float32 [3072, 768], P('mp')
- d_b_back: float32 [768], P('mp')
- d_norm2_gain: float32 [768], P('mp')
- d_norm2_shift: float32 [768], P('mp')
The draws below stay inside these ranges and needn't reach their ends.
Inputs may be any that keep to these rules, and one draw needn't show every extreme that they name: `segment_ids`: in every row segment numbers never fall and each of the 16 texts has 1 to 64 positions.
All inputs are finite; a program needn't handle non-finite values.
Results may differ from the reference program's by a relative error of at most 0.02865.
Values may be sent and summed in bfloat16 or wider, within the bound.
No kernel may reach another device: no remote copies, remote signals or barrier semaphores. Data moves between devices by JAX's collectives and lax.ppermute only.
A program may use at most 128 MiB of HBM per device.

```python
import math
import jax
import jax.numpy as jnp
import numpy as np
from jax import lax

D = 768
HEAD_DIM = 64
FF = 3072
ROW_LEN = 512
SEGS = 16
SEG_MOST = 64
ROWS = 32
TOKENS = 16384
PAIRS = 8
PASSAGES = 256
N_MP = 4


def plant(array, rng, least, high):
    index_at = [jax.random.randint(jax.random.fold_in(rng, axis), (), 0, length) for axis, length in enumerate(array.shape)]
    longest = array.shape.index(max(array.shape))
    neighbour = index_at[:longest] + [(index_at[longest] + 1) % array.shape[longest]] + index_at[longest + 1:]
    return array.at[tuple(index_at)].set(least).at[tuple(neighbour)].set(high)


def shard_levels(rng, dims, shards, low, high):
    gain, own = 1.0, jax.random.fold_in(rng, 6)
    for position, parts in shards:
        heights = jnp.exp(jax.random.uniform(jax.random.fold_in(own, position), (parts,), jnp.float32, low / len(shards), high / len(shards)))
        gain = gain * jnp.repeat(heights, dims[position] // parts).reshape([-1 if axis == position else 1 for axis in range(len(dims))])
    return gain


def length_profile(amount, total, bound, slope):
    loads = [(1 << 20) // math.isqrt(standing ** slope) + 1 for standing in range(2, amount + 1)]
    rest, given = total - bound - (amount - 1), [1] * (amount - 1)
    while rest > 0:
        candidates = [i for i in range(amount - 1) if given[i] < bound]
        pool, remaining = sum([loads[i] for i in candidates]), rest
        for i in candidates:
            more = min(bound - given[i], max(1, remaining * loads[i] // pool), rest)
            given[i] = given[i] + more
            rest = rest - more
    return np.array([bound] + given)


def ragged_sizes(rng, count, total, most, lean):
    if count == 2:
        one = jax.random.randint(rng, (), max(1, total - most), min(most, total - 1) + 1)
        return jnp.stack([one, total - one])
    sizes = jnp.asarray(length_profile(count, total, most, lean), jnp.int32)
    couples = (count - 1) // 2
    giver, taker = sizes[1:1 + 2 * couples:2], sizes[2:2 + 2 * couples:2]
    room = jnp.minimum(giver - 1, most - taker)
    shifted = jax.random.randint(jax.random.fold_in(rng, 1), (couples,), 0, 1 << 20) % (room + 1)
    sizes = sizes.at[1:1 + 2 * couples:2].set(giver - shifted).at[2:2 + 2 * couples:2].set(taker + shifted)
    return sizes[jax.random.permutation(jax.random.fold_in(rng, 2), count)]


def bell_draw(key, shape, width, limit, split=(), kind=jnp.bfloat16):
    drawn = jax.random.normal(key, shape, jnp.float32) * width
    if len(split) > 0:
        drawn = shard_levels(key, shape, split, -0.22, 0.18) * drawn
    return jnp.clip(drawn, min=-limit, max=limit).astype(kind)


def setup_inputs(seed: int = 0) -> dict:
    streams_of = jax.random.split(jax.random.key(seed), 16)
    return {
        "tokens": bell_draw(streams_of[0], (TOKENS, D), 1.0, 6.0, ((0, 8),)),
        "w_qkv": bell_draw(streams_of[1], (3, D, D), D ** -0.5, 0.21875, ((2, 4),)),
        "b_qv": bell_draw(streams_of[2], (2, D), 0.3, 2.0, ((1, 4),), jnp.float32),
        "w_out": bell_draw(streams_of[3], (D, D), (D // 16) ** -0.5, 0.875, ((0, 4),)),
        "b_out": bell_draw(streams_of[4], (D,), 0.3, 2.0, (), jnp.float32),
        "norm1_gain": jnp.clip(1.0 + 0.1 * jax.random.normal(streams_of[5], (D,), jnp.float32), 0.5, 1.5),
        "norm1_shift": bell_draw(streams_of[6], (D,), 0.2, 1.5, (), jnp.float32),
        "w_in": bell_draw(streams_of[7], (D, FF), D ** -0.5, 0.21875, ((1, 4),)),
        "b_in": bell_draw(streams_of[8], (FF,), 0.3, 2.0, ((0, 4),), jnp.float32),
        "w_back": bell_draw(streams_of[9], (FF, D), (FF // 2) ** -0.5, 0.15625, ((0, 4),)),
        "b_back": bell_draw(streams_of[10], (D,), 0.2, 1.5, (), jnp.float32),
        "norm2_gain": jnp.clip(1.0 + 0.1 * jax.random.normal(streams_of[11], (D,), jnp.float32), 0.5, 1.5),
        "norm2_shift": bell_draw(streams_of[12], (D,), 0.05, 0.4, (), jnp.float32),
        "segment_ids": jax.vmap(lambda own: jnp.searchsorted(jnp.cumsum(ragged_sizes(own, SEGS, ROW_LEN, SEG_MOST, 1)), jnp.arange(ROW_LEN), side="right"))(jax.random.split(streams_of[13], ROWS)).reshape((ROWS, ROW_LEN)).astype(jnp.int32),
        "pair_ids": plant(jax.random.randint(streams_of[14], (ROWS, PAIRS), 0, PASSAGES), jax.random.fold_in(streams_of[14], 1), 0, PASSAGES - 1).astype(jnp.int32),
    }


@jax.custom_vjp
def low(v):
    return lax.optimization_barrier(v.astype(jnp.bfloat16)).astype(jnp.float32)

@jax.custom_vjp
def low_back(v):
    return v

def low_keep(v):
    return (low(v), None)

def low_pass(kept, grad):
    return (grad,)

def back_keep(v):
    return (v, None)

def back_low(kept, grad):
    return (low(grad),)
low.defvjp(low_keep, low_pass)
low_back.defvjp(back_keep, back_low)
norm_eps = 1e-06
inv_temp = 50.0
loss_scale = 8.0
highest = lax.Precision.HIGHEST

def matmul(left_side, right_side):
    return jnp.matmul(left_side, right_side, precision=highest)

def layer_norm(values, gain_vec, shift_vec):
    center = values - lax.optimization_barrier(jnp.mean(values, axis=-1, keepdims=True))
    spread = lax.optimization_barrier(jnp.mean(center * center, axis=-1, keepdims=True))
    return center * lax.rsqrt(spread + norm_eps) * gain_vec + shift_vec

def both_round(values):
    return low_back(low(values))

def attend_row(inputs):
    query_rows, key_rows, value_rows, segment = inputs
    length = query_rows.shape[0]
    head_count = query_rows.shape[1] // HEAD_DIM
    score_scale = HEAD_DIM ** (-0.5)
    query_heads = query_rows.reshape(length, head_count, HEAD_DIM)
    key_heads = key_rows.reshape(length, head_count, HEAD_DIM)
    value_heads = value_rows.reshape(length, head_count, HEAD_DIM)
    scores = low_back(jnp.einsum('qhd,khd->hqk', query_heads, key_heads, precision=highest) * score_scale)
    same_segment = (segment[:, None] == segment[None, :])[None]
    scores = jnp.where(same_segment, scores, -1000000000.0)
    row_best = lax.optimization_barrier(jnp.max(scores, axis=-1, keepdims=True))
    weights = jnp.exp(scores - row_best)
    probability = weights / lax.optimization_barrier(jnp.sum(weights, axis=-1, keepdims=True))
    context = jnp.einsum('hqk,khd->qhd', low(probability), value_heads, precision=highest)
    return both_round(context.reshape(length, head_count * HEAD_DIM))

def forward(tokens, w_qkv, b_qv, w_out, b_out, norm1_gain, norm1_shift, w_in, b_in, w_back, b_back, norm2_gain, norm2_shift, segment_ids, pair_ids):
    row_count = segment_ids.shape[0]
    model_width = tokens.shape[1]
    group_width = model_width // N_MP
    unit_width = w_in.shape[1] // N_MP
    attn_total = jnp.zeros_like(tokens)
    for member in range(N_MP):
        columns = slice(member * group_width, (member + 1) * group_width)
        seen = low_back(tokens)
        query_rows = both_round(matmul(seen, w_qkv[0][:, columns]) + b_qv[0, columns])
        key_rows = both_round(matmul(seen, w_qkv[1][:, columns]))
        value_rows = both_round(matmul(seen, w_qkv[2][:, columns]) + b_qv[1, columns])
        context = lax.map(jax.checkpoint(attend_row), (query_rows.reshape(row_count, ROW_LEN, group_width), key_rows.reshape(row_count, ROW_LEN, group_width), value_rows.reshape(row_count, ROW_LEN, group_width), segment_ids))
        attn_total = attn_total + low(matmul(context.reshape(-1, group_width), w_out[columns, :]))
    resid1 = tokens + low_back(attn_total) + b_out
    normed1 = layer_norm(resid1, norm1_gain, norm1_shift)
    rounded1 = low(normed1)
    ffn_total = jnp.zeros_like(tokens)
    for member in range(N_MP):
        columns = slice(member * unit_width, (member + 1) * unit_width)
        seen = low_back(rounded1)
        before = low_back(matmul(seen, w_in[:, columns]) + b_in[columns])
        active = low(jax.nn.gelu(before, approximate=False))
        ffn_total = ffn_total + low(matmul(active, w_back[columns, :]))
    resid2 = normed1 + low_back(ffn_total) + b_back
    layer_out = low(layer_norm(resid2, norm2_gain, norm2_shift))
    out_rows = layer_out.reshape(row_count, ROW_LEN, model_width)
    slot_ids = jnp.arange(SEGS, dtype=jnp.int32)
    member_mask = (segment_ids[:, None, :] == slot_ids[None, :, None]).astype(jnp.float32)
    lengths = lax.optimization_barrier(jnp.sum(member_mask, axis=-1))
    pooled = jnp.einsum('rst,rtd->rsd', member_mask, out_rows, precision=highest) / lengths[..., None]
    unit_vecs = low(pooled * lax.rsqrt(lax.optimization_barrier(jnp.sum(pooled * pooled, axis=-1, keepdims=True)) + norm_eps))
    query_vecs = unit_vecs[:, 0::2].reshape(-1, model_width)
    passage_vecs = unit_vecs[:, 1::2].reshape(-1, model_width)
    similarity = low_back(matmul(query_vecs, passage_vecs.T)) * inv_temp
    row_best = lax.optimization_barrier(jnp.max(similarity, axis=1, keepdims=True))
    total_log = row_best[:, 0] + jnp.log(lax.optimization_barrier(jnp.sum(jnp.exp(similarity - row_best), axis=1)))
    positive = jnp.take_along_axis(similarity, pair_ids.reshape(-1, 1).astype(jnp.int32), axis=1)[:, 0]
    per_query = total_log - positive
    return (loss_scale * jnp.sum(per_query), (jnp.mean(per_query), layer_out))

def reference(tokens, w_qkv, b_qv, w_out, b_out, norm1_gain, norm1_shift, w_in, b_in, w_back, b_back, norm2_gain, norm2_shift, segment_ids, pair_ids):
    params = (tokens.astype(jnp.float32), w_qkv.astype(jnp.float32), b_qv.astype(jnp.float32), w_out.astype(jnp.float32), b_out.astype(jnp.float32), norm1_gain.astype(jnp.float32), norm1_shift.astype(jnp.float32), w_in.astype(jnp.float32), b_in.astype(jnp.float32), w_back.astype(jnp.float32), b_back.astype(jnp.float32), norm2_gain.astype(jnp.float32), norm2_shift.astype(jnp.float32))

    def objective(*inputs):
        return forward(*inputs, segment_ids, pair_ids)
    scaled, pullback, extras = jax.vjp(objective, *params, has_aux=True)
    grads = pullback(jnp.ones_like(scaled))
    loss, layer_out = extras
    return (loss, layer_out.astype(jnp.bfloat16), grads[0].astype(jnp.bfloat16), grads[1], grads[2], grads[3], grads[4], grads[5], grads[6], grads[7], grads[8], grads[9], grads[10], grads[11], grads[12])
```

```python
import functools

import jax
import jax.numpy as jnp
from jax import lax
from jax.experimental import pallas as pl
from jax.experimental.pallas import tpu as pltpu
from jax.sharding import PartitionSpec as P

HEAD_DIM = 64
Q_BLOCK = 128
K_WINDOW = 256
LANES = 128
TILE = 256
ROW_TILE = 64
VEC_ROWS = 64
VMEM_BYTES = 56 * 1024 * 1024

norm_eps = 1e-06
inv_temp = 50.0
loss_scale = 8.0
masked_score = -1000000000.0

f32 = jnp.float32
bf16 = jnp.bfloat16


def product(left_side, right_side):
    return jnp.dot(left_side, right_side, preferred_element_type=f32)


def product_t(left_side, right_side):
    return lax.dot_general(
        left_side, right_side, (((0,), (0,)), ((), ())), preferred_element_type=f32
    )


def product_nt(left_side, right_side):
    return lax.dot_general(
        left_side, right_side, (((1,), (1,)), ((), ())), preferred_element_type=f32
    )


def window_start(block, length):
    return min(max(block * Q_BLOCK - HEAD_DIM, 0), length - K_WINDOW)


def gelu_and_slope(values):
    bell = jnp.exp(values * values * -0.5)
    t = 1.0 / (1.0 + (0.3275911 * 0.7071067811865476) * jnp.abs(values))
    poly = 1.061405429 * t - 1.453152027
    poly = poly * t + 1.421413741
    poly = poly * t - 0.284496736
    poly = poly * t + 0.254829592
    tail = (0.5 * t) * (poly * bell)
    phi = jnp.where(values >= 0.0, 1.0 - tail, tail)
    return values * phi, phi + (values * 0.3989422804014327) * bell


def head_lanes(pair, which):
    lane = lax.broadcasted_iota(jnp.int32, pair.shape, 1)
    keep = (lane < HEAD_DIM) if which == 0 else (lane >= HEAD_DIM)
    return jnp.where(keep, pair, jnp.zeros_like(pair))


def columns(array, first, count):
    return array[:, first : first + count]


def head_parts(array, local_width):
    parts = []
    for head in range(local_width // HEAD_DIM):
        first = head // 2 * LANES
        width = min(LANES, local_width - first)
        part = columns(array, first, width)
        parts.append(part if width < LANES else head_lanes(part, head % 2))
    return parts


def merge_heads(results, local_width):
    pieces = []
    for first in range(0, local_width, LANES):
        head = first // HEAD_DIM
        if local_width - first >= LANES:
            lane = lax.broadcasted_iota(jnp.int32, results[head].shape, 1)
            pieces.append((first, jnp.where(lane < HEAD_DIM, results[head], results[head + 1])))
        else:
            pieces.append((first, results[head]))
    return pieces


def attend_forward(m_ref, tok_ref, w_ref, b_ref, seg_ref, win_ref, qkv_ref, prob_ref, ctx_ref):
    length = tok_ref.shape[0]
    width = w_ref.shape[2]
    heads = width // HEAD_DIM
    tok = tok_ref[...]
    q = ((product(tok, w_ref[0]) + b_ref[0:1, :]).astype(bf16) * HEAD_DIM**-0.5).astype(bf16)
    k = product(tok, w_ref[1]).astype(bf16)
    v = (product(tok, w_ref[2]) + b_ref[1:2, :]).astype(bf16)
    qkv_ref[0, 0] = q
    qkv_ref[0, 1] = k
    qkv_ref[0, 2] = v
    q_parts = head_parts(q, width)
    slot = lax.broadcasted_iota(jnp.int32, (16, 1), 0)
    own = (seg_ref[0] == slot).astype(f32).astype(bf16)
    for block in range(length // Q_BLOCK):
        at, start = block * Q_BLOCK, window_start(block, length)
        seen = (win_ref[0, block : block + 1, :] == slot).astype(f32).astype(bf16)
        mask = (product_t(columns(own, at, Q_BLOCK), seen) - 1.0) * -masked_score
        results = []
        for head in range(heads):
            first = head // 2 * LANES
            part = min(LANES, width - first)
            key = k[start : start + K_WINDOW, first : first + part]
            value = v[start : start + K_WINDOW, first : first + part]
            scores = product_nt(q_parts[head][at : at + Q_BLOCK], key) + mask
            weights = jnp.exp(scores - jnp.max(scores, axis=-1, keepdims=True))
            low = (weights * (1.0 / jnp.sum(weights, axis=-1, keepdims=True))).astype(bf16)
            prob_ref[0, head * (length // Q_BLOCK) + block] = low
            results.append(product(low, value))
        for first, merged in merge_heads(results, width):
            ctx_ref[0, at : at + Q_BLOCK, first : first + merged.shape[1]] = merged.astype(bf16)


def attend_backward(
    m_ref, tok_ref, w_ref, qkv_ref, prob_ref, g0_ref, g1_ref, g2_ref, g3_ref,
    dw_ref, o0_ref, o1_ref, o2_ref, o3_ref, gctx, gk_sum, gv_sum, dw_sum, vec_sum,
):
    step = pl.program_id(0)
    length = tok_ref.shape[0]
    width = w_ref.shape[2]
    heads = width // HEAD_DIM
    for piece, g_ref in enumerate((g0_ref, g1_ref, g2_ref, g3_ref)):

        @pl.when(step == piece)
        def _():
            gctx[...] = g_ref[...]

    @pl.when(step == 0)
    def _():
        dw_sum[...] = jnp.zeros_like(dw_sum)
        vec_sum[...] = jnp.zeros_like(vec_sum)

    gk_sum[...] = jnp.zeros_like(gk_sum)
    gv_sum[...] = jnp.zeros_like(gv_sum)
    q, k, v = qkv_ref[0, 0], qkv_ref[0, 1], qkv_ref[0, 2]
    q_parts = head_parts(q, width)
    g_parts = head_parts(gctx[...], width)
    gq_blocks = []
    for block in range(length // Q_BLOCK):
        at, start = block * Q_BLOCK, window_start(block, length)
        rows = slice(start, start + K_WINDOW)
        results, gk, gv = [], {}, {}
        for head in range(heads):
            first = head // 2 * LANES
            part = min(LANES, width - first)
            key, value = k[rows, first : first + part], v[rows, first : first + part]
            grad = g_parts[head][at : at + Q_BLOCK]
            low = prob_ref[0, head * (length // Q_BLOCK) + block]
            prob = low.astype(f32)
            grad_prob = product_nt(grad, value)
            inner = jnp.sum(prob * grad_prob, axis=-1, keepdims=True)
            grad_low = (prob * (grad_prob - inner)).astype(bf16)
            results.append(product(grad_low, key))
            gk_part = product_t(grad_low, q_parts[head][at : at + Q_BLOCK])
            gv_part = product_t(low, grad)
            gk[first] = gk[first] + gk_part if first in gk else gk_part
            gv[first] = gv[first] + gv_part if first in gv else gv_part
        for first in gk:
            lanes = slice(first, first + gk[first].shape[1])
            gk_sum[rows, lanes] += gk[first]
            gv_sum[rows, lanes] += gv[first]
        gq_blocks.append(merge_heads(results, width))
    gq = jnp.concatenate(
        [
            jnp.concatenate(
                [(blocks[i][1] * HEAD_DIM**-0.5).astype(bf16) for blocks in gq_blocks], axis=0
            )
            for i in range(len(gq_blocks[0]))
        ],
        axis=1,
    )
    gk, gv = gk_sum[...].astype(bf16), gv_sum[...].astype(bf16)
    tok = tok_ref[...]
    back = None
    for c, grad in enumerate((gq, gk, gv)):
        dw_sum[c * width : (c + 1) * width, :] += product_t(grad, tok)
        term = product_nt(grad, w_ref[c])
        back = term if back is None else back + term
    vec_sum[0:1, :] += jnp.sum(gq.astype(f32), axis=0, keepdims=True)
    vec_sum[1:2, :] += jnp.sum(gv.astype(f32), axis=0, keepdims=True)
    back = back.astype(bf16)
    for piece, o_ref in enumerate((o0_ref, o1_ref, o2_ref, o3_ref)):

        @pl.when(step == piece)
        def _():
            o_ref[...] = back

    @pl.when(step == pl.num_programs(0) - 1)
    def _():
        dw_ref[0 : 3 * width, :] = dw_sum[...].astype(bf16)
        vec = vec_sum[...]
        top = vec.astype(bf16)
        rest = (vec - top.astype(f32)).astype(bf16)
        dw_ref[3 * width :, :] = jnp.zeros((VEC_ROWS, dw_ref.shape[1]), bf16)
        dw_ref[3 * width : 3 * width + 16, 0:width] = jnp.concatenate([top, rest], axis=0)


def start_all(pairs, sems):
    copies = []
    for i, (source, target) in enumerate(pairs):
        copy = pltpu.make_async_copy(source, target, sems.at[i])
        copy.start()
        copies.append(copy)
    return copies


def middle_forward(
    m_ref, tok_hbm, seg_ref, pair_ref, b_out, gain1, shift1, b_in, b_back, gain2, shift2,
    c0, c1, c2, c3, wo0, wo1, wo2, wo3, wi0, wi1, wi2, wi3, wb0, wb1, wb2, wb3,
    act_hbm, slope_hbm, xhat1_ref, rstd1_ref, low1_ref, xhat2_ref, rstd2_ref, out_ref, pooled_ref, len_ref, msg_ref,
    tok_v, ctx_v, wo_v, wi_v, wb_v, act_v, slope_v, resid, sems, out_sems,
):
    length, width = tok_v.shape
    units = wi_v.shape[2]
    at = pl.multiple_of(m_ref[0] * length, length)
    copies = start_all(
        [(tok_hbm.at[pl.ds(at, length)], tok_v)]
        + [(c, ctx_v.at[r]) for r, c in enumerate((c0, c1, c2, c3))]
        + [(w, wo_v.at[r]) for r, w in enumerate((wo0, wo1, wo2, wo3))]
        + [(w, wi_v.at[r]) for r, w in enumerate((wi0, wi1, wi2, wi3))]
        + [(w, wb_v.at[r]) for r, w in enumerate((wb0, wb1, wb2, wb3))],
        sems,
    )
    for copy in copies[:9]:
        copy.wait()
    for first in range(0, width, TILE):
        cols = slice(first, first + TILE)
        total = tok_v[:, cols].astype(f32) + b_out[:, cols]
        for r in range(4):
            total = total + product(ctx_v[r], wo_v[r, :, cols])
        resid[:, cols] = total

    @pl.loop(0, length // ROW_TILE)
    def _(i):
        rows = pl.ds(pl.multiple_of(i * ROW_TILE, ROW_TILE), ROW_TILE)
        values = resid[rows, :]
        center = values - jnp.mean(values, axis=-1, keepdims=True)
        rate = lax.rsqrt(jnp.mean(center * center, axis=-1, keepdims=True) + norm_eps)
        xhat = center * rate
        xhat1_ref[rows, :] = xhat
        rstd1_ref[rows, :] = jnp.broadcast_to(rate, (ROW_TILE, LANES))
        normed = xhat * gain1[...] + shift1[...]
        resid[rows, :] = normed
        low1_ref[rows, :] = normed.astype(bf16)

    outs = []
    for r in range(4):
        copies[9 + r].wait()
        for first in range(0, units, TILE):
            cols = slice(first, first + TILE)
            before = product(low1_ref[...], wi_v[r, :, cols]) + b_in[r : r + 1, cols]
            active, slope = gelu_and_slope(before)
            act_v[r, :, cols] = active.astype(bf16)
            slope_v[r, :, cols] = slope.astype(bf16)
        outs += start_all(
            [(act_v.at[r], act_hbm.at[r]), (slope_v.at[r], slope_hbm.at[r])],
            out_sems.at[pl.ds(2 * r, 2)],
        )
    for r in range(4):
        copies[13 + r].wait()
    for first in range(0, width, TILE):
        cols = slice(first, first + TILE)
        total = resid[:, cols] + b_back[:, cols]
        for r in range(4):
            total = total + product(act_v[r], wb_v[r, :, cols])
        resid[:, cols] = total

    @pl.loop(0, length // ROW_TILE)
    def _(i):
        rows = pl.ds(pl.multiple_of(i * ROW_TILE, ROW_TILE), ROW_TILE)
        values = resid[rows, :]
        center = values - jnp.mean(values, axis=-1, keepdims=True)
        rate = lax.rsqrt(jnp.mean(center * center, axis=-1, keepdims=True) + norm_eps)
        xhat = center * rate
        xhat2_ref[rows, :] = xhat
        rstd2_ref[rows, :] = jnp.broadcast_to(rate, (ROW_TILE, LANES))
        out_ref[rows, :] = (xhat * gain2[...] + shift2[...]).astype(bf16)

    own = members(seg_ref)
    sums = product(own.astype(bf16), out_ref[...])
    count = jnp.sum(own, axis=-1, keepdims=True)
    pooled = sums / count
    rate = lax.rsqrt(jnp.sum(pooled * pooled, axis=-1, keepdims=True) + norm_eps)
    unit = (pooled * rate).astype(bf16)
    pooled_ref[...] = pooled
    len_ref[...] = jnp.broadcast_to(count, len_ref.shape)
    half = unit.astype(f32)
    msg_ref[:, 0:width] = half[0:8].astype(bf16)
    msg_ref[:, width : 2 * width] = half[8:16].astype(bf16)
    msg_ref[:, 2 * width :] = pair_ref[...].astype(bf16)
    for copy in outs:
        copy.wait()


def members(seg_ref):
    slot = lax.broadcasted_iota(jnp.int32, (16, 1), 0)
    segment = jnp.where(slot < 8, 2 * slot, 2 * slot - 15)
    return (seg_ref[...] == segment).astype(f32)


def contrast(ids_ref, all_ref, own_ref, pooled_ref, len_ref, loss_ref, grad_ref, log_v):
    width = pooled_ref.shape[1]
    count = all_ref.shape[0]
    block = min(count, 256)
    passages = all_ref[:, width : 2 * width]
    number = lax.broadcasted_iota(jnp.int32, (1, count), 1).astype(f32)

    def target(rows):
        coded = rows[:, 2 * width :].astype(f32)
        return coded[:, 0:1] * 64.0 + coded[:, 1:2]

    def statistics(rows, scores):
        best = jnp.max(scores, axis=-1, keepdims=True)
        log_total = best + jnp.log(jnp.sum(jnp.exp(scores - best), axis=-1, keepdims=True))
        return log_total, (number == target(rows)).astype(f32)

    def one_block(i, total):
        rows_at = pl.ds(pl.multiple_of(i * block, block), block)
        rows = all_ref[rows_at, :]
        scores = product_nt(rows[:, 0:width], passages) * inv_temp
        log_total, positive = statistics(rows, scores)
        log_v[rows_at, :] = jnp.broadcast_to(log_total, (block, LANES))
        return total + jnp.sum(log_total - jnp.sum(scores * positive, axis=-1, keepdims=True), keepdims=True)

    total = lax.fori_loop(0, count // block, one_block, jnp.zeros((1, 1), f32))
    loss_ref[...] = jnp.broadcast_to(total * (1.0 / count), loss_ref.shape)
    own = own_ref[...]
    scores = product_nt(own[:, 0:width], passages) * inv_temp
    log_total, positive = statistics(own, scores)
    grad_low = ((jnp.exp(scores - log_total) - positive) * (loss_scale * inv_temp)).astype(bf16)
    grad_query = product(grad_low, passages)

    everyone = all_ref[...]
    queries = everyone[:, 0:width]
    passage = jnp.concatenate(
        [own[:, width : 2 * width].astype(f32), jnp.zeros((LANES - 8, width), f32)], axis=0
    ).astype(bf16)
    lane = lax.broadcasted_iota(jnp.int32, (1, LANES), 1)
    scores = product_nt(queries, passage) * inv_temp
    number = jnp.where(lane < 8, ids_ref[0] * 8 + lane, -1).astype(f32)
    positive = (number == target(everyone)).astype(f32)
    weight = jnp.exp(scores - log_v[...]) - positive
    grad_low = (jnp.where(lane < 8, weight, 0.0) * (loss_scale * inv_temp)).astype(bf16)
    grad_passage = product_t(grad_low, queries)[0:8]

    grad_unit = jnp.concatenate([grad_query, grad_passage], axis=0)
    pooled = pooled_ref[...]
    rate = lax.rsqrt(jnp.sum(pooled * pooled, axis=-1, keepdims=True) + norm_eps)
    inner = jnp.sum(pooled * grad_unit, axis=-1, keepdims=True)
    grad = rate * grad_unit - rate * rate * rate * pooled * inner
    grad_ref[...] = grad / len_ref[:, 0:1]


def column_total(values):
    return jnp.sum(values.reshape(values.shape[0] // 8, 8, values.shape[1]), axis=0)


def back_second(
    gp_ref, seg_ref, xhat_ref, rstd_ref, gain_ref, act_hbm,
    low_ref, grad_ref, vec_ref, d0, d1, d2, d3,
    out_v, act_v, sums, sems,
):
    length, width = xhat_ref.shape
    copies = start_all([(act_hbm.at[r], act_v.at[r]) for r in range(4)], sems)
    own = members(seg_ref).astype(bf16)
    top = gp_ref[...].astype(bf16)
    rest = (gp_ref[...] - top.astype(f32)).astype(bf16)
    out_v[...] = product_t(own, top) + product_t(own, rest)
    sums[...] = jnp.zeros_like(sums)

    @pl.loop(0, length // ROW_TILE)
    def _(i):
        rows = pl.ds(pl.multiple_of(i * ROW_TILE, ROW_TILE), ROW_TILE)
        grad_out, xhat = out_v[rows, :], xhat_ref[rows, :]
        sums[0] += column_total(grad_out * xhat)
        sums[1] += column_total(grad_out)
        grad = grad_out * gain_ref[...]
        first = jnp.mean(grad, axis=-1, keepdims=True)
        second = jnp.mean(grad * xhat, axis=-1, keepdims=True)
        grad = (grad - first - xhat * second) * rstd_ref[rows, 0:1]
        sums[2] += column_total(grad)
        grad_ref[rows, :] = grad
        low_ref[rows, :] = grad.astype(bf16)

    vec_ref[...] = jnp.zeros_like(vec_ref)
    for i in range(3):
        vec_ref[i : i + 1, :] = jnp.sum(sums[i], axis=0, keepdims=True)
    for r, d_ref in ((3, d3), (2, d2), (1, d1), (0, d0)):
        copies[r].wait()
        for first in range(0, width, TILE):
            cols = slice(first, first + TILE)
            d_ref[cols, :] = product_t(act_v[r, :, cols], low_ref[...]).astype(bf16)


def back_first(
    low_ref, resid_ref, xhat_ref, rstd_ref, gain_ref, slope_hbm,
    wo0, wo1, wo2, wo3, wi0, wi1, wi2, wi3, wb0, wb1, wb2, wb3,
    gb_hbm, grad_ref, attn_ref, vec_ref, bin_ref, x0, x1, x2, x3,
    slope_v, wo_v, wi_v, wb_v, gb_v, total_v, sums, sems, out_sems,
):
    length, width = xhat_ref.shape
    units = wi_v.shape[2]
    copies = start_all(
        [p for r, w in enumerate((wb0, wb1, wb2, wb3)) for p in ((w, wb_v.at[r]), (slope_hbm.at[r], slope_v.at[r]))]
        + [(w, wi_v.at[r]) for r, w in enumerate((wi0, wi1, wi2, wi3))]
        + [(w, wo_v.at[r]) for r, w in enumerate((wo0, wo1, wo2, wo3))],
        sems,
    )
    outs = []
    for r in range(4):
        copies[2 * r].wait()
        copies[2 * r + 1].wait()
        for first in range(0, units, TILE):
            cols = slice(first, first + TILE)
            grad = product_nt(low_ref[...], wb_v[r, cols, :])
            low = (grad * slope_v[r, :, cols].astype(f32)).astype(bf16)
            gb_v[r, :, cols] = low
            bin_ref[r : r + 1, cols] = jnp.sum(column_total(low.astype(f32)), axis=0, keepdims=True)
        outs += start_all([(gb_v.at[r], gb_hbm.at[r])], out_sems.at[pl.ds(r, 1)])
    for copy in copies[8:]:
        copy.wait()
    for first in range(0, width, TILE):
        cols = slice(first, first + TILE)
        total = resid_ref[:, cols]
        for r in range(4):
            total = total + product_nt(gb_v[r], wi_v[r, cols, :])
        total_v[:, cols] = total
    sums[...] = jnp.zeros_like(sums)

    @pl.loop(0, length // ROW_TILE)
    def _(i):
        rows = pl.ds(pl.multiple_of(i * ROW_TILE, ROW_TILE), ROW_TILE)
        grad_out, xhat = total_v[rows, :], xhat_ref[rows, :]
        sums[0] += column_total(grad_out * xhat)
        sums[1] += column_total(grad_out)
        grad = grad_out * gain_ref[...]
        first = jnp.mean(grad, axis=-1, keepdims=True)
        second = jnp.mean(grad * xhat, axis=-1, keepdims=True)
        grad = (grad - first - xhat * second) * rstd_ref[rows, 0:1]
        sums[2] += column_total(grad)
        grad_ref[rows, :] = grad
        attn_ref[rows, :] = grad.astype(bf16)

    vec_ref[...] = jnp.zeros_like(vec_ref)
    for i in range(3):
        vec_ref[i : i + 1, :] = jnp.sum(sums[i], axis=0, keepdims=True)
    for r, x_ref in enumerate((x0, x1, x2, x3)):
        x_ref[...] = product_nt(attn_ref[...], wo_v[r]).astype(bf16)
    for copy in outs:
        copy.wait()


def weight_grads(
    low1_ref, attn_ref, vec1_ref, vec2_ref, bin_ref, c0, c1, c2, c3, gb_hbm,
    d0, d1, d2, d3,
    gb_v, sems,
):
    length, width = low1_ref.shape
    units = gb_v.shape[2]
    local = c0.shape[1]
    copies = start_all([(gb_hbm.at[r], gb_v.at[r]) for r in range(4)], sems)
    for r, d_ref, c_ref in ((3, d3, c3), (2, d2, c2), (1, d1, c1), (0, d0, c0)):
        copies[r].wait()
        for first in range(0, width, TILE):
            cols = slice(first, first + TILE)
            d_ref[cols, :] = product_t(low1_ref[:, cols], gb_v[r]).astype(bf16)
        d_ref[width : width + local, :] = product_t(c_ref[...], attn_ref[...]).astype(bf16)
        rows = jnp.concatenate(
            [vec1_ref[0:3, :], vec2_ref[0:3, :], bin_ref[r : r + 1, :], jnp.zeros((1, units), f32)],
            axis=0,
        )
        top = rows.astype(bf16)
        rest = (rows - top.astype(f32)).astype(bf16)
        at = width + local
        d_ref[at : at + 16, :] = jnp.concatenate([top, rest], axis=0)
        d_ref[at + 16 : at + VEC_ROWS, :] = jnp.zeros((VEC_ROWS - 16, units), bf16)


def whole(array, memory=pltpu.VMEM):
    return pl.BlockSpec(memory_space=memory)


def hop(array, axis, flip):
    size = lax.axis_size(axis)
    return lax.ppermute(array, axis, [(i, i ^ flip) for i in range(size)])


def bit_of(axis, flip):
    return (lax.axis_index(axis) // flip) % 2


def ordered(bit, mine, other, axis):
    low_first = jnp.concatenate([mine, other], axis=axis)
    high_first = jnp.concatenate([other, mine], axis=axis)
    return jnp.where(bit == 0, low_first, high_first)


def bits_below(size):
    flips, flip = [], 1
    while flip < size:
        flips.append(flip)
        flip *= 2
    return flips


def gather_parts(mine):
    near = hop(mine, "mp", 1)
    far = hop(mine, "mp", 2)
    return [mine, near, far, hop(far, "mp", 1)]


def add_low(left_side, right_side):
    return (left_side.astype(f32) + right_side.astype(f32)).astype(bf16)


def scatter_parts(parts):
    far = add_low(parts[2], hop(parts[3], "mp", 1))
    near = add_low(parts[0], hop(parts[1], "mp", 1))
    return add_low(near, hop(far, "mp", 2))


def sum_over_rows(array):
    flips = bits_below(lax.axis_size("dp"))
    for flip in flips:
        half = array.shape[0] // 2
        bit = bit_of("dp", flip)
        send = lax.dynamic_slice_in_dim(array, (1 - bit) * half, half)
        keep = lax.dynamic_slice_in_dim(array, bit * half, half)
        array = add_low(keep, hop(send, "dp", flip))
    for flip in reversed(flips):
        array = ordered(bit_of("dp", flip), array, hop(array, "dp", flip), 0)
    return array


def params(cost=None, **more):
    return dict(
        compiler_params=pltpu.CompilerParams(vmem_limit_bytes=VMEM_BYTES, **more), cost_estimate=cost
    )


def cost(flops, moved, exps=0):
    return pl.CostEstimate(flops=int(flops), bytes_accessed=int(moved), transcendentals=int(exps))


def shape(dims, dtype=bf16):
    return jax.ShapeDtypeStruct(dims, dtype)


def shards(
    tokens, w_qkv, b_qv, w_out, b_out, norm1_gain, norm1_shift, w_in, b_in, w_back, b_back,
    norm2_gain, norm2_shift, segment_ids, pair_ids,
):
    row_count, length = segment_ids.shape
    width = tokens.shape[1]
    local = w_out.shape[0]
    units = w_in.shape[1]
    heads = local // HEAD_DIM
    blocks = length // Q_BLOCK
    member = lax.axis_index("mp")
    own_row = lax.axis_index("dp") * row_count + member
    m_arr = member.astype(jnp.int32).reshape(1)
    any_spec = pl.BlockSpec(memory_space=pl.ANY)
    vmem_spec = pl.BlockSpec(memory_space=pltpu.VMEM)
    smem_spec = pl.BlockSpec(memory_space=pltpu.SMEM)
    dma = pltpu.SemaphoreType.DMA

    out_parts = gather_parts(w_out)
    in_parts = gather_parts(w_in)
    back_parts = gather_parts(w_back)
    bias_parts = jnp.concatenate(gather_parts(b_in[None, :]), axis=0)

    windows = jnp.stack(
        [segment_ids[:, window_start(i, length) :][:, :K_WINDOW] for i in range(blocks)], axis=1
    )
    seg_rows = segment_ids[:, None, :]
    pick = lambda r, m: (r ^ m[0], 0, 0)
    qkv, probs, ctx = pl.pallas_call(
        attend_forward,
        grid_spec=pltpu.PrefetchScalarGridSpec(
            num_scalar_prefetch=1,
            grid=(row_count,),
            in_specs=[
                pl.BlockSpec((length, width), lambda r, m: (r ^ m[0], 0)),
                pl.BlockSpec(w_qkv.shape, lambda r, m: (0, 0, 0)),
                pl.BlockSpec(b_qv.shape, lambda r, m: (0, 0)),
                pl.BlockSpec((1, 1, length), pick),
                pl.BlockSpec((1, blocks, K_WINDOW), pick),
            ],
            out_specs=[
                pl.BlockSpec((1, 3, length, local), lambda r, m: (r, 0, 0, 0)),
                pl.BlockSpec((1, heads * blocks, Q_BLOCK, K_WINDOW), lambda r, m: (r, 0, 0, 0)),
                pl.BlockSpec((1, length, local), lambda r, m: (r, 0, 0)),
            ],
        ),
        out_shape=[
            shape((row_count, 3, length, local)),
            shape((row_count, heads * blocks, Q_BLOCK, K_WINDOW)),
            shape((row_count, length, local)),
        ],
        name="attend_forward",
        **params(cost(6 * row_count * length * width * local, 8e6, row_count * heads * length * K_WINDOW)),
    )(m_arr, tokens, w_qkv, b_qv, seg_rows, windows)

    ctx_parts = [ctx[0]] + [hop(ctx[r], "mp", r) for r in range(1, 4)]
    seg_own = lax.dynamic_slice_in_dim(segment_ids, member, 1)
    pair_own = lax.dynamic_slice_in_dim(pair_ids, member, 1).reshape(-1, 1)
    pair_code = jnp.concatenate(
        [pair_own // 64, pair_own % 64, jnp.zeros((pair_own.shape[0], LANES - 2), jnp.int32)], axis=1
    ).astype(f32)
    row = lambda vector: vector[None, :]
    act, slope, xhat1, rstd1, low1, xhat2, rstd2, out_own, pooled, lengths, msg = pl.pallas_call(
        middle_forward,
        in_specs=[smem_spec, any_spec] + [vmem_spec] * 9 + [any_spec] * 16,
        out_specs=[any_spec] * 2 + [vmem_spec] * 9,
        out_shape=[
            shape((4, length, units)), shape((4, length, units)),
            shape((length, width), f32), shape((length, LANES), f32), shape((length, width)),
            shape((length, width), f32), shape((length, LANES), f32), shape((length, width)),
            shape((16, width), f32), shape((16, LANES), f32), shape((8, 2 * width + LANES)),
        ],
        scratch_shapes=[
            pltpu.VMEM((length, width), bf16), pltpu.VMEM((4, length, local), bf16),
            pltpu.VMEM((4, local, width), bf16), pltpu.VMEM((4, width, units), bf16),
            pltpu.VMEM((4, units, width), bf16), pltpu.VMEM((4, length, units), bf16),
            pltpu.VMEM((4, length, units), bf16), pltpu.VMEM((length, width), f32),
            dma((17,)), dma((8,)),
        ],
        name="middle_forward",
        **params(cost(2 * length * width * (width + 8 * units), 25e6, 4 * length * units)),
    )(
        m_arr, tokens, seg_own, pair_code, row(b_out), row(norm1_gain), row(norm1_shift), bias_parts,
        row(b_back), row(norm2_gain), row(norm2_shift), *ctx_parts, *out_parts, *in_parts, *back_parts,
    )

    everyone = msg[None]
    for flip in reversed(bits_below(lax.axis_size("dp"))):
        everyone = both_ways("dp", flip, everyone)
    for flip in reversed(bits_below(lax.axis_size("mp"))):
        everyone = both_ways("mp", flip, everyone)
    everyone = everyone.reshape(-1, msg.shape[1])

    loss, grad_pooled = pl.pallas_call(
        contrast,
        in_specs=[smem_spec] + [vmem_spec] * 4,
        out_specs=[vmem_spec] * 2,
        out_shape=[shape((8, LANES), f32), shape((16, width), f32)],
        scratch_shapes=[pltpu.VMEM((everyone.shape[0], LANES), f32)],
        name="contrast",
        **params(cost(4e8, 2e6, 1e5)),
    )(own_row.astype(jnp.int32).reshape(1), everyone, msg, pooled, lengths)

    grad_low2, grad_resid2, vec2, *d_back = pl.pallas_call(
        back_second,
        in_specs=[vmem_spec] * 5 + [any_spec],
        out_specs=[vmem_spec] * 7,
        out_shape=[
            shape((length, width)), shape((length, width), f32), shape((8, width), f32),
            *[shape((units, width))] * 4,
        ],
        scratch_shapes=[
            pltpu.VMEM((length, width), f32), pltpu.VMEM((4, length, units), bf16),
            pltpu.VMEM((3, 8, width), f32), dma((4,)),
        ],
        name="back_second",
        **params(cost(8 * length * width * units, 14e6)),
    )(grad_pooled, seg_own, xhat2, rstd2, row(norm2_gain), act)

    gb, grad_resid1, attn_low, vec1, d_bin, *ctx_grads = pl.pallas_call(
        back_first,
        in_specs=[vmem_spec] * 5 + [any_spec] * 13,
        out_specs=[any_spec] + [vmem_spec] * 8,
        out_shape=[
            shape((4, length, units)), shape((length, width), f32), shape((length, width)),
            shape((8, width), f32), shape((4, units), f32), *[shape((length, local))] * 4,
        ],
        scratch_shapes=[
            pltpu.VMEM((4, length, units), bf16), pltpu.VMEM((4, local, width), bf16),
            pltpu.VMEM((4, width, units), bf16), pltpu.VMEM((4, units, width), bf16),
            pltpu.VMEM((4, length, units), bf16), pltpu.VMEM((length, width), f32),
            pltpu.VMEM((3, 8, width), f32), dma((16,)), dma((4,)),
        ],
        name="back_first",
        **params(cost(2 * length * width * (width + 8 * units), 25e6)),
    )(
        grad_low2, grad_resid2, xhat1, rstd1, row(norm1_gain), slope, *out_parts, *in_parts, *back_parts,
    )

    grads_here = [ctx_grads[0]] + [hop(ctx_grads[r], "mp", r) for r in range(1, 4)]

    d_first = pl.pallas_call(
        weight_grads,
        in_specs=[vmem_spec] * 9 + [any_spec],
        out_specs=[vmem_spec] * 4,
        out_shape=[shape((width + local + VEC_ROWS, units))] * 4,
        scratch_shapes=[pltpu.VMEM((4, length, units), bf16), dma((4,))],
        name="weight_grads",
        **params(cost(8 * length * width * (units + local), 12e6)),
    )(low1, attn_low, vec1, vec2, d_bin, *ctx_parts, gb)

    same = lambda r, m: (0, 0)
    d_qkv, *backs = pl.pallas_call(
        attend_backward,
        grid_spec=pltpu.PrefetchScalarGridSpec(
            num_scalar_prefetch=1,
            grid=(row_count,),
            in_specs=[
                pl.BlockSpec((length, width), lambda r, m: (r ^ m[0], 0)),
                pl.BlockSpec(w_qkv.shape, lambda r, m: (0, 0, 0)),
                pl.BlockSpec((1, 3, length, local), lambda r, m: (r, 0, 0, 0)),
                pl.BlockSpec((1, heads * blocks, Q_BLOCK, K_WINDOW), lambda r, m: (r, 0, 0, 0)),
            ]
            + [pl.BlockSpec((length, local), same)] * 4,
            out_specs=[pl.BlockSpec((3 * local + VEC_ROWS, width), same)]
            + [pl.BlockSpec((length, width), same)] * 4,
            scratch_shapes=[
                pltpu.VMEM((length, local), bf16), pltpu.VMEM((length, local), f32),
                pltpu.VMEM((length, local), f32), pltpu.VMEM((3 * local, width), f32),
                pltpu.VMEM((8, local), f32),
            ],
        ),
        out_shape=[shape((3 * local + VEC_ROWS, width))] + [shape((length, width))] * 4,
        name="attend_backward",
        **params(cost(12 * row_count * length * width * local, 16e6)),
    )(m_arr, tokens, w_qkv, qkv, probs, *grads_here)

    layer_out = rows_of_all(out_own, row_count)
    near = add_low(backs[0].astype(f32) + grad_resid1, hop(backs[1], "mp", 1))
    far = add_low(backs[2], hop(backs[3], "mp", 1))
    d_tokens = rows_of_all(add_low(near, hop(far, "mp", 2)), row_count)

    sum_back = sum_over_rows(scatter_parts(d_back))
    sum_first = sum_over_rows(scatter_parts(d_first))
    sum_qkv = sum_over_rows(d_qkv)

    at = width + local
    vectors = sum_first[at : at + 8].astype(f32) + sum_first[at + 8 : at + 16].astype(f32)
    shares = lax.dynamic_slice_in_dim(vectors[0:6], member * local, local, axis=1)
    at = 3 * local
    d_bqv = sum_qkv[at : at + 2, 0:local].astype(f32) + sum_qkv[at + 8 : at + 10, 0:local].astype(f32)
    d_wqkv = jnp.swapaxes(sum_qkv[0:at].reshape(3, local, width), 1, 2).astype(f32)
    return (
        loss[0, 0],
        layer_out,
        d_tokens,
        d_wqkv,
        d_bqv,
        sum_first[width : width + local].astype(f32),
        shares[2],
        shares[0],
        shares[1],
        sum_first[0:width].astype(f32),
        vectors[6],
        sum_back.astype(f32),
        shares[5],
        shares[3],
        shares[4],
    )


def both_ways(axis, flip, array):
    other = hop(array, axis, flip)
    low_first = jnp.stack([array, other], axis=1)
    high_first = jnp.stack([other, array], axis=1)
    joined = jnp.where(bit_of(axis, flip) == 0, low_first, high_first)
    return joined.reshape(-1, *array.shape[1:])


def rows_of_all(mine, row_count):
    pair = ordered(bit_of("mp", 2), mine[None], hop(mine, "mp", 2)[None], 0)
    other = hop(pair, "mp", 1)
    low_first = jnp.stack([pair, other], axis=1)
    high_first = jnp.stack([other, pair], axis=1)
    joined = jnp.where(bit_of("mp", 1) == 0, low_first, high_first)
    return joined.reshape(row_count * mine.shape[0], mine.shape[1])


def solution(mesh):
    return jax.shard_map(
        shards,
        mesh=mesh,
        in_specs=(
            P("dp", None),
            P(None, None, "mp"),
            P(None, "mp"),
            P("mp", None),
            P(),
            P(),
            P(),
            P(None, "mp"),
            P("mp"),
            P("mp", None),
            P(),
            P(),
            P(),
            P("dp", None),
            P("dp", None),
        ),
        out_specs=(
            P(),
            P("dp", None),
            P("dp", None),
            P(None, None, "mp"),
            P(None, "mp"),
            P("mp", None),
            P("mp"),
            P("mp"),
            P("mp"),
            P(None, "mp"),
            P("mp"),
            P("mp", None),
            P("mp"),
            P("mp"),
            P("mp"),
        ),
        check_vma=False,
    )
```

```python
import functools

import jax
import jax.numpy as jnp
from jax import lax
from jax.experimental import pallas as pl
from jax.experimental.pallas import tpu as pltpu
from jax.sharding import PartitionSpec as P

HEAD_DIM = 64
Q_BLOCK = 128
K_WINDOW = 256
LANES = 128
TILE = 256
ROW_TILE = 64
VEC_ROWS = 64
VMEM_BYTES = 56 * 1024 * 1024

norm_eps = 1e-06
inv_temp = 50.0
loss_scale = 8.0
masked_score = -1000000000.0

f32 = jnp.float32
bf16 = jnp.bfloat16


def product(left_side, right_side):
    return jnp.dot(left_side, right_side, preferred_element_type=f32)


def product_t(left_side, right_side):
    return lax.dot_general(
        left_side, right_side, (((0,), (0,)), ((), ())), preferred_element_type=f32
    )


def product_nt(left_side, right_side):
    return lax.dot_general(
        left_side, right_side, (((1,), (1,)), ((), ())), preferred_element_type=f32
    )


def window_start(block, length):
    return min(max(block * Q_BLOCK - HEAD_DIM, 0), length - K_WINDOW)


def gelu_and_slope(values):
    bell = jnp.exp(values * values * -0.5)
    t = 1.0 / (1.0 + (0.3275911 * 0.7071067811865476) * jnp.abs(values))
    poly = 1.061405429 * t - 1.453152027
    poly = poly * t + 1.421413741
    poly = poly * t - 0.284496736
    poly = poly * t + 0.254829592
    tail = (0.5 * t) * (poly * bell)
    phi = jnp.where(values >= 0.0, 1.0 - tail, tail)
    return values * phi, phi + (values * 0.3989422804014327) * bell


def head_lanes(pair, which):
    lane = lax.broadcasted_iota(jnp.int32, pair.shape, 1)
    keep = (lane < HEAD_DIM) if which == 0 else (lane >= HEAD_DIM)
    return jnp.where(keep, pair, jnp.zeros_like(pair))


def columns(array, first, count):
    return array[:, first : first + count]


def head_parts(array, local_width):
    parts = []
    for head in range(local_width // HEAD_DIM):
        first = head // 2 * LANES
        width = min(LANES, local_width - first)
        part = columns(array, first, width)
        parts.append(part if width < LANES else head_lanes(part, head % 2))
    return parts


def merge_heads(results, local_width):
    pieces = []
    for first in range(0, local_width, LANES):
        head = first // HEAD_DIM
        if local_width - first >= LANES:
            lane = lax.broadcasted_iota(jnp.int32, results[head].shape, 1)
            pieces.append((first, jnp.where(lane < HEAD_DIM, results[head], results[head + 1])))
        else:
            pieces.append((first, results[head]))
    return pieces


def attend_forward(m_ref, tok_ref, w_ref, b_ref, seg_ref, win_ref, qkv_ref, prob_ref, *refs):
    ctx_refs, ctx_v = refs[:-1], refs[-1]
    length = tok_ref.shape[0]
    width = w_ref.shape[1]
    heads = width // HEAD_DIM
    tok = tok_ref[...]
    q = ((product_nt(tok, w_ref[0]) + b_ref[0:1, :]).astype(bf16) * HEAD_DIM**-0.5).astype(bf16)
    k = product_nt(tok, w_ref[1]).astype(bf16)
    v = (product_nt(tok, w_ref[2]) + b_ref[1:2, :]).astype(bf16)
    qkv_ref[0, 0] = q
    qkv_ref[0, 1] = k
    qkv_ref[0, 2] = v
    q_parts = head_parts(q, width)
    slot = lax.broadcasted_iota(jnp.int32, (16, 1), 0)
    own = (seg_ref[0] == slot).astype(f32).astype(bf16)
    for block in range(length // Q_BLOCK):
        at, start = block * Q_BLOCK, window_start(block, length)
        seen = (win_ref[0, block : block + 1, :] == slot).astype(f32).astype(bf16)
        mask = (product_t(columns(own, at, Q_BLOCK), seen) - 1.0) * -masked_score
        results = []
        for head in range(heads):
            first = head // 2 * LANES
            part = min(LANES, width - first)
            key = k[start : start + K_WINDOW, first : first + part]
            value = v[start : start + K_WINDOW, first : first + part]
            scores = product_nt(q_parts[head][at : at + Q_BLOCK], key) + mask
            weights = jnp.exp(scores - jnp.max(scores, axis=-1, keepdims=True))
            low = (weights * (1.0 / jnp.sum(weights, axis=-1, keepdims=True))).astype(bf16)
            prob_ref[0, head * (length // Q_BLOCK) + block] = low
            results.append(product(low, value))
        for first, merged in merge_heads(results, width):
            ctx_v[at : at + Q_BLOCK, first : first + merged.shape[1]] = merged.astype(bf16)
    for piece, ctx_ref in enumerate(ctx_refs):

        @pl.when(pl.program_id(0) == piece)
        def _():
            ctx_ref[...] = ctx_v[...]


def attend_backward(count, first, last, m_ref, tok_ref, w_ref, qkv_ref, prob_ref, *refs):
    g_refs, refs = refs[:count], refs[count:]
    if not first:
        before_ref, vec_before_ref, *refs = refs
    o_refs, refs = refs[:count], refs[count:]
    if last:
        dw_ref, gctx, gk_sum, gv_sum, dw_sum, vec_sum = refs
    else:
        dw_ref, vec_ref, gctx, gk_sum, gv_sum, dw_sum, vec_sum = refs
    step = pl.program_id(0)
    length = tok_ref.shape[0]
    width = w_ref.shape[1]
    heads = width // HEAD_DIM
    for piece, g_ref in enumerate(g_refs):

        @pl.when(step == piece)
        def _():
            gctx[...] = g_ref[...]

    @pl.when(step == 0)
    def _():
        dw_sum[...] = jnp.zeros_like(dw_sum) if first else before_ref[...]
        vec_sum[...] = jnp.zeros_like(vec_sum) if first else vec_before_ref[...]

    gk_sum[...] = jnp.zeros_like(gk_sum)
    gv_sum[...] = jnp.zeros_like(gv_sum)
    q, k, v = qkv_ref[0, 0], qkv_ref[0, 1], qkv_ref[0, 2]
    q_parts = head_parts(q, width)
    g_parts = head_parts(gctx[...], width)
    gq_blocks = []
    for block in range(length // Q_BLOCK):
        at, start = block * Q_BLOCK, window_start(block, length)
        rows = slice(start, start + K_WINDOW)
        results, gk, gv = [], {}, {}
        for head in range(heads):
            first = head // 2 * LANES
            part = min(LANES, width - first)
            key, value = k[rows, first : first + part], v[rows, first : first + part]
            grad = g_parts[head][at : at + Q_BLOCK]
            low = prob_ref[0, head * (length // Q_BLOCK) + block]
            prob = low.astype(f32)
            grad_prob = product_nt(grad, value)
            inner = jnp.sum(prob * grad_prob, axis=-1, keepdims=True)
            grad_low = (prob * (grad_prob - inner)).astype(bf16)
            results.append(product(grad_low, key))
            gk_part = product_t(grad_low, q_parts[head][at : at + Q_BLOCK])
            gv_part = product_t(low, grad)
            gk[first] = gk[first] + gk_part if first in gk else gk_part
            gv[first] = gv[first] + gv_part if first in gv else gv_part
        for first in gk:
            lanes = slice(first, first + gk[first].shape[1])
            gk_sum[rows, lanes] += gk[first]
            gv_sum[rows, lanes] += gv[first]
        gq_blocks.append(merge_heads(results, width))
    gq = jnp.concatenate(
        [
            jnp.concatenate(
                [(blocks[i][1] * HEAD_DIM**-0.5).astype(bf16) for blocks in gq_blocks], axis=0
            )
            for i in range(len(gq_blocks[0]))
        ],
        axis=1,
    )
    gk, gv = gk_sum[...].astype(bf16), gv_sum[...].astype(bf16)
    tok = tok_ref[...]
    back = None
    for c, grad in enumerate((gq, gk, gv)):
        dw_sum[c * width : (c + 1) * width, :] += product_t(grad, tok)
        term = product(grad, w_ref[c])
        back = term if back is None else back + term
    vec_sum[0:1, :] += jnp.sum(gq.astype(f32), axis=0, keepdims=True)
    vec_sum[1:2, :] += jnp.sum(gv.astype(f32), axis=0, keepdims=True)
    back = back.astype(bf16)
    for piece, o_ref in enumerate(o_refs):

        @pl.when(step == piece)
        def _():
            o_ref[...] = back

    @pl.when(step == count - 1)
    def _():
        if not last:
            dw_ref[...] = dw_sum[...]
            vec_ref[...] = vec_sum[...]
            return
        dw_ref[0 : 3 * width, :] = dw_sum[...].astype(bf16)
        vec = vec_sum[...]
        top = vec.astype(bf16)
        rest = (vec - top.astype(f32)).astype(bf16)
        dw_ref[3 * width :, :] = jnp.zeros((VEC_ROWS, dw_ref.shape[1]), bf16)
        dw_ref[3 * width : 3 * width + 16, 0:width] = jnp.concatenate([top, rest], axis=0)


def row_of(ref):
    return jnp.concatenate([ref[i : i + 1, :] for i in range(ref.shape[0])], axis=1)


def start_all(pairs, sems):
    copies = []
    for i, (source, target) in enumerate(pairs):
        copy = pltpu.make_async_copy(source, target, sems.at[i])
        copy.start()
        copies.append(copy)
    return copies


def prepare(bits_ref, bias_ref, out_ref, in_hbm, back_hbm, pack_ref, in_ref, back_ref, sems):
    quarter = in_ref.shape[0]
    in_at = pl.multiple_of(bits_ref[0] * quarter, quarter)
    back_at = pl.multiple_of(bits_ref[1] * quarter, quarter)
    copies = start_all(
        [(in_hbm.at[pl.ds(in_at, quarter)], in_ref), (back_hbm.at[pl.ds(back_at, quarter)], back_ref)], sems
    )
    local = out_ref.shape[0]
    bias = row_of(bias_ref)
    high = bias.astype(bf16)
    rest = bias - high.astype(f32)
    middle = rest.astype(bf16)
    low = (rest - middle.astype(f32)).astype(bf16)
    slot = lax.broadcasted_iota(jnp.int32, (16, 1), 0)
    rows = jnp.where(slot == 0, high.astype(f32), 0.0)
    rows = jnp.where(slot == 1, middle.astype(f32), rows)
    rows = jnp.where(slot == 2, low.astype(f32), rows)
    pack_ref[0:local, :] = out_ref[...]
    pack_ref[local : local + 16, :] = rows.astype(bf16)
    for copy in copies:
        copy.wait()


def feed(r, low_ref, wi_v, b_in, act_v, slope_v):
    for first in range(0, wi_v.shape[2], TILE):
        cols = slice(first, first + TILE)
        before = product(low_ref[...], wi_v[r, :, cols]) + b_in[:, cols]
        active, slope = gelu_and_slope(before)
        act_v[r, :, cols] = active.astype(bf16)
        slope_v[r, :, cols] = slope.astype(bf16)


def middle_first(
    m_ref, tok_hbm, bias_ref, gain_ref, shift_ref, c0, c1, c2, c3, wo0, wo1, wo2, wo3, wi0, wi1, wb0, wb1,
    act_hbm, slope_hbm, xhat1_ref, rstd1_ref, low1_ref, total_ref,
    tok_v, ctx_v, wo_v, wi_v, wb_v, act_v, slope_v, sems, out_sems,
):
    length, width = tok_v.shape
    local = ctx_v.shape[2]
    b_out, gain1, shift1 = row_of(bias_ref), row_of(gain_ref), row_of(shift_ref)
    at = pl.multiple_of(m_ref[0] * length, length)
    copies = start_all(
        [(tok_hbm.at[pl.ds(at, length)], tok_v)]
        + [(c, ctx_v.at[r]) for r, c in enumerate((c0, c1, c2, c3))]
        + [(w, wo_v.at[r]) for r, w in enumerate((wo0, wo1, wo2, wo3))]
        + [(w, wi_v.at[r]) for r, w in enumerate((wi0, wi1))]
        + [(w, wb_v.at[r]) for r, w in enumerate((wb0, wb1))],
        sems,
    )
    for copy in copies[:9]:
        copy.wait()
    for first in range(0, width, TILE):
        cols = slice(first, first + TILE)
        total = tok_v[:, cols].astype(f32) + b_out[:, cols]
        for r in range(4):
            total = total + product(ctx_v[r], wo_v[r, 0:local, cols])
        total_ref[:, cols] = total

    @pl.loop(0, length // ROW_TILE)
    def _(i):
        rows = pl.ds(pl.multiple_of(i * ROW_TILE, ROW_TILE), ROW_TILE)
        values = total_ref[rows, :]
        center = values - jnp.mean(values, axis=-1, keepdims=True)
        rate = lax.rsqrt(jnp.mean(center * center, axis=-1, keepdims=True) + norm_eps)
        xhat = center * rate
        xhat1_ref[rows, :] = xhat
        rstd1_ref[rows, :] = jnp.broadcast_to(rate, (ROW_TILE, LANES))
        normed = xhat * gain1 + shift1
        total_ref[rows, :] = normed
        low1_ref[rows, :] = normed.astype(bf16)

    outs = []
    for r in range(2):
        copies[9 + r].wait()
        b_in = jnp.sum(wo_v[r, local : local + 16, :].astype(f32), axis=0, keepdims=True)
        feed(r, low1_ref, wi_v, b_in, act_v, slope_v)
        outs += start_all(
            [(act_v.at[r], act_hbm.at[r]), (slope_v.at[r], slope_hbm.at[r])],
            out_sems.at[pl.ds(2 * r, 2)],
        )
    for copy in copies[11:]:
        copy.wait()
    for first in range(0, width, TILE):
        cols = slice(first, first + TILE)
        total_ref[:, cols] += product(act_v[0], wb_v[0, :, cols]) + product(act_v[1], wb_v[1, :, cols])
    for copy in outs:
        copy.wait()


def middle_second(
    seg_ref, pair_ref, bias_ref, gain_ref, shift_ref, low1_ref, total_hbm, wo2, wo3, wi2, wi3, wb2, wb3,
    act_hbm, slope_hbm, xhat2_ref, rstd2_ref, out_ref, pooled_ref, len_ref, msg_ref,
    wi_v, wb_v, act_v, slope_v, resid, sems, out_sems,
):
    length, width = resid.shape
    local = wo2.shape[0] - 16
    b_back, gain2, shift2 = row_of(bias_ref), row_of(gain_ref), row_of(shift_ref)
    copies = start_all(
        [(w, wi_v.at[r]) for r, w in enumerate((wi2, wi3))]
        + [(total_hbm, resid)]
        + [(w, wb_v.at[r]) for r, w in enumerate((wb2, wb3))],
        sems,
    )
    outs = []
    for r in range(2):
        copies[r].wait()
        b_in = jnp.sum((wo2, wo3)[r][local : local + 16, :].astype(f32), axis=0, keepdims=True)
        feed(r, low1_ref, wi_v, b_in, act_v, slope_v)
        outs += start_all(
            [(act_v.at[r], act_hbm.at[r]), (slope_v.at[r], slope_hbm.at[r])],
            out_sems.at[pl.ds(2 * r, 2)],
        )
    for copy in copies[2:]:
        copy.wait()
    for first in range(0, width, TILE):
        cols = slice(first, first + TILE)
        total = resid[:, cols] + b_back[:, cols]
        resid[:, cols] = total + product(act_v[0], wb_v[0, :, cols]) + product(act_v[1], wb_v[1, :, cols])

    @pl.loop(0, length // ROW_TILE)
    def _(i):
        rows = pl.ds(pl.multiple_of(i * ROW_TILE, ROW_TILE), ROW_TILE)
        values = resid[rows, :]
        center = values - jnp.mean(values, axis=-1, keepdims=True)
        rate = lax.rsqrt(jnp.mean(center * center, axis=-1, keepdims=True) + norm_eps)
        xhat = center * rate
        xhat2_ref[rows, :] = xhat
        rstd2_ref[rows, :] = jnp.broadcast_to(rate, (ROW_TILE, LANES))
        out_ref[rows, :] = (xhat * gain2 + shift2).astype(bf16)

    own = members(seg_ref)
    sums = product(own.astype(bf16), out_ref[...])
    count = jnp.sum(own, axis=-1, keepdims=True)
    pooled = sums / count
    rate = lax.rsqrt(jnp.sum(pooled * pooled, axis=-1, keepdims=True) + norm_eps)
    unit = (pooled * rate).astype(bf16)
    pooled_ref[...] = pooled
    len_ref[...] = jnp.broadcast_to(count, len_ref.shape)
    half = unit.astype(f32)
    msg_ref[:, 0:width] = half[0:8].astype(bf16)
    msg_ref[:, width : 2 * width] = half[8:16].astype(bf16)
    msg_ref[:, 2 * width :] = pair_ref[...].astype(bf16)
    for copy in outs:
        copy.wait()


def members(seg_ref):
    slot = lax.broadcasted_iota(jnp.int32, (16, 1), 0)
    segment = jnp.where(slot < 8, 2 * slot, 2 * slot - 15)
    return (seg_ref[...] == segment).astype(f32)


def contrast(ids_ref, all_ref, own_ref, pooled_ref, len_ref, loss_ref, grad_ref, log_v):
    width = pooled_ref.shape[1]
    count = all_ref.shape[0]
    block = min(count, 256)
    passages = all_ref[:, width : 2 * width]
    number = lax.broadcasted_iota(jnp.int32, (1, count), 1).astype(f32)

    def target(rows):
        coded = rows[:, 2 * width :].astype(f32)
        return coded[:, 0:1] * 64.0 + coded[:, 1:2]

    def statistics(rows, scores):
        best = jnp.max(scores, axis=-1, keepdims=True)
        log_total = best + jnp.log(jnp.sum(jnp.exp(scores - best), axis=-1, keepdims=True))
        return log_total, (number == target(rows)).astype(f32)

    def one_block(i, total):
        rows_at = pl.ds(pl.multiple_of(i * block, block), block)
        rows = all_ref[rows_at, :]
        scores = product_nt(rows[:, 0:width], passages) * inv_temp
        log_total, positive = statistics(rows, scores)
        log_v[rows_at, :] = jnp.broadcast_to(log_total, (block, LANES))
        return total + jnp.sum(log_total - jnp.sum(scores * positive, axis=-1, keepdims=True), keepdims=True)

    total = lax.fori_loop(0, count // block, one_block, jnp.zeros((1, 1), f32))
    loss_ref[...] = jnp.broadcast_to(total * (1.0 / count), loss_ref.shape)
    own = own_ref[...]
    scores = product_nt(own[:, 0:width], passages) * inv_temp
    log_total, positive = statistics(own, scores)
    grad_low = ((jnp.exp(scores - log_total) - positive) * (loss_scale * inv_temp)).astype(bf16)
    grad_query = product(grad_low, passages)

    everyone = all_ref[...]
    queries = everyone[:, 0:width]
    passage = jnp.concatenate(
        [own[:, width : 2 * width].astype(f32), jnp.zeros((LANES - 8, width), f32)], axis=0
    ).astype(bf16)
    lane = lax.broadcasted_iota(jnp.int32, (1, LANES), 1)
    scores = product_nt(queries, passage) * inv_temp
    number = jnp.where(lane < 8, ids_ref[0] * 8 + lane, -1).astype(f32)
    positive = (number == target(everyone)).astype(f32)
    weight = jnp.exp(scores - log_v[...]) - positive
    grad_low = (jnp.where(lane < 8, weight, 0.0) * (loss_scale * inv_temp)).astype(bf16)
    grad_passage = product_t(grad_low, queries)[0:8]

    grad_unit = jnp.concatenate([grad_query, grad_passage], axis=0)
    pooled = pooled_ref[...]
    rate = lax.rsqrt(jnp.sum(pooled * pooled, axis=-1, keepdims=True) + norm_eps)
    inner = jnp.sum(pooled * grad_unit, axis=-1, keepdims=True)
    grad = rate * grad_unit - rate * rate * rate * pooled * inner
    grad_ref[...] = grad / len_ref[:, 0:1]


def column_total(values):
    return jnp.sum(values.reshape(values.shape[0] // 8, 8, values.shape[1]), axis=0)


def back_second(
    gp_ref, seg_ref, xhat_ref, rstd_ref, gain_ref, act01_hbm, act23_hbm,
    low_ref, grad_ref, vec_ref, d_ref,
    out_v, act_v, sums, sems,
):
    length, width = xhat_ref.shape
    gain = row_of(gain_ref)
    copies = start_all([(act23_hbm.at[1], act_v.at[0]), (act01_hbm.at[1], act_v.at[1])], sems)
    own = members(seg_ref).astype(bf16)
    top = gp_ref[...].astype(bf16)
    rest = (gp_ref[...] - top.astype(f32)).astype(bf16)
    out_v[...] = product_t(own, top) + product_t(own, rest)
    sums[...] = jnp.zeros_like(sums)

    @pl.loop(0, length // ROW_TILE)
    def _(i):
        rows = pl.ds(pl.multiple_of(i * ROW_TILE, ROW_TILE), ROW_TILE)
        grad_out, xhat = out_v[rows, :], xhat_ref[rows, :]
        sums[0] += column_total(grad_out * xhat)
        sums[1] += column_total(grad_out)
        grad = grad_out * gain
        first = jnp.mean(grad, axis=-1, keepdims=True)
        second = jnp.mean(grad * xhat, axis=-1, keepdims=True)
        grad = (grad - first - xhat * second) * rstd_ref[rows, 0:1]
        sums[2] += column_total(grad)
        grad_ref[rows, :] = grad
        low_ref[rows, :] = grad.astype(bf16)

    vec_ref[...] = jnp.zeros_like(vec_ref)
    for i in range(3):
        vec_ref[i : i + 1, :] = jnp.sum(sums[i], axis=0, keepdims=True)
    back_products(copies, act_v, low_ref, d_ref)


def back_products(copies, act_v, low_ref, d_ref):
    for i, copy in enumerate(copies):
        copy.wait()
        for first in range(0, act_v.shape[2], TILE):
            cols = slice(first, first + TILE)
            d_ref[i, cols, :] = product_t(act_v[i, :, cols], low_ref[...]).astype(bf16)


def back_outer(low_ref, act01_hbm, act23_hbm, d_ref, act_v, sems):
    copies = start_all([(act23_hbm.at[0], act_v.at[0]), (act01_hbm.at[0], act_v.at[1])], sems)
    back_products(copies, act_v, low_ref, d_ref)


def back_first(
    low_ref, resid_ref, xhat_ref, rstd_ref, gain_ref, slope01_hbm, slope23_hbm,
    wo0, wo1, wo2, wo3, wi0, wi1, wi2, wi3, wb0, wb1, wb2, wb3,
    gb_hbm, grad_ref, attn_ref, vec_ref, bin_ref, x0, x1, x2, x3,
    slope_v, wo_v, wi_v, wb_v, gb_v, total_v, sums, sems, out_sems,
):
    length, width = xhat_ref.shape
    units = wi_v.shape[2]
    gain = row_of(gain_ref)
    copies = start_all(
        [p for r, w in enumerate((wb0, wb1, wb2, wb3)) for p in ((w, wb_v.at[r]), ((slope01_hbm, slope23_hbm)[r // 2].at[r % 2], slope_v.at[r]))]
        + [(w, wi_v.at[r]) for r, w in enumerate((wi0, wi1, wi2, wi3))]
        + [(w, wo_v.at[r]) for r, w in enumerate((wo0, wo1, wo2, wo3))],
        sems,
    )
    outs = []
    for r in range(4):
        copies[2 * r].wait()
        copies[2 * r + 1].wait()
        for first in range(0, units, TILE):
            cols = slice(first, first + TILE)
            grad = product_nt(low_ref[...], wb_v[r, cols, :])
            low = (grad * slope_v[r, :, cols].astype(f32)).astype(bf16)
            gb_v[r, :, cols] = low
            bin_ref[r : r + 1, cols] = jnp.sum(column_total(low.astype(f32)), axis=0, keepdims=True)
        outs += start_all([(gb_v.at[r], gb_hbm.at[r])], out_sems.at[pl.ds(r, 1)])
    for copy in copies[8:]:
        copy.wait()
    for first in range(0, width, TILE):
        cols = slice(first, first + TILE)
        total = resid_ref[:, cols]
        for r in range(4):
            total = total + product_nt(gb_v[r], wi_v[r, cols, :])
        total_v[:, cols] = total
    sums[...] = jnp.zeros_like(sums)

    @pl.loop(0, length // ROW_TILE)
    def _(i):
        rows = pl.ds(pl.multiple_of(i * ROW_TILE, ROW_TILE), ROW_TILE)
        grad_out, xhat = total_v[rows, :], xhat_ref[rows, :]
        sums[0] += column_total(grad_out * xhat)
        sums[1] += column_total(grad_out)
        grad = grad_out * gain
        first = jnp.mean(grad, axis=-1, keepdims=True)
        second = jnp.mean(grad * xhat, axis=-1, keepdims=True)
        grad = (grad - first - xhat * second) * rstd_ref[rows, 0:1]
        sums[2] += column_total(grad)
        grad_ref[rows, :] = grad
        attn_ref[rows, :] = grad.astype(bf16)

    vec_ref[...] = jnp.zeros_like(vec_ref)
    for i in range(3):
        vec_ref[i : i + 1, :] = jnp.sum(sums[i], axis=0, keepdims=True)
    for r, x_ref in enumerate((x0, x1, x2, x3)):
        x_ref[...] = product_nt(attn_ref[...], wo_v[r, 0 : x_ref.shape[1], :]).astype(bf16)
    for copy in outs:
        copy.wait()


def weight_grads(
    pieces, low1_ref, attn_ref, vec1_ref, vec2_ref, bin_ref, ca, cb, gb_hbm,
    d_ref,
    gb_v, sems,
):
    length, width = low1_ref.shape
    units = gb_v.shape[2]
    local = ca.shape[1]
    copies = start_all([(gb_hbm.at[r], gb_v.at[i]) for i, r in enumerate(pieces)], sems)
    for i, (r, c_ref) in enumerate(zip(pieces, (ca, cb))):
        copies[i].wait()
        for first in range(0, width, TILE):
            cols = slice(first, first + TILE)
            d_ref[i, cols, :] = product_t(low1_ref[:, cols], gb_v[i]).astype(bf16)
        d_ref[i, width : width + local, :] = product_t(c_ref[...], attn_ref[...]).astype(bf16)
        rows = jnp.concatenate(
            [vec1_ref[0:3, :], vec2_ref[0:3, :], bin_ref[r : r + 1, :], jnp.zeros((1, units), f32)],
            axis=0,
        )
        top = rows.astype(bf16)
        rest = (rows - top.astype(f32)).astype(bf16)
        at = width + local
        d_ref[i, at : at + 16, :] = jnp.concatenate([top, rest], axis=0)
        d_ref[i, at + 16 : at + VEC_ROWS, :] = jnp.zeros((VEC_ROWS - 16, units), bf16)


def hop(array, axis, flip):
    size = lax.axis_size(axis)
    return lax.ppermute(array, axis, [(i, i ^ flip) for i in range(size)])


def bit_of(axis, flip):
    return (lax.axis_index(axis) // flip) % 2


def ordered(bit, mine, other, axis):
    low_first = jnp.concatenate([mine, other], axis=axis)
    high_first = jnp.concatenate([other, mine], axis=axis)
    return jnp.where(bit == 0, low_first, high_first)


def bits_below(size):
    flips, flip = [], 1
    while flip < size:
        flips.append(flip)
        flip *= 2
    return flips


def together(*arrays):
    return lax.optimization_barrier(arrays)


def late(array, *earlier):
    return lax.optimization_barrier((array, *earlier))[0]


def gather_parts(mine, first=None):
    near = hop(mine, "mp", 1)
    far = hop(mine, "mp", 2) if first is None else first
    return [mine, near, far, hop(far, "mp", 1)]


def join(part, flip):
    return ordered(bit_of("dp", flip), part, hop(part, "dp", flip), 0)


def add_low(left_side, right_side):
    return (left_side.astype(f32) + right_side.astype(f32)).astype(bf16)


class Rows:
    def __init__(self):
        self.dp, self.mp = lax.axis_size("dp"), lax.axis_size("mp")
        flips = bits_below(self.dp)
        self.orders = flips, flips[1:2] + flips[:1] + flips[2:]
        self.steps = len(flips)

    def swap(self, values, step):
        pairs = [
            (i, ((i // self.mp) ^ self.orders[i % self.mp % 2][step]) * self.mp + i % self.mp)
            for i in range(self.dp * self.mp)
        ]
        return lax.ppermute(values, ("dp", "mp"), pairs)

    def bit(self, step):
        even, odd = (bit_of("dp", order[step]) for order in self.orders)
        return jnp.where(lax.axis_index("mp") % 2 == 1, odd, even)

    def send(self, array, step):
        half = array.shape[-2] // 2
        away = lax.dynamic_slice_in_dim(array, (1 - self.bit(step)) * half, half, axis=-2)
        return self.swap(away, step)

    def keep(self, array, got, step):
        half = array.shape[-2] // 2
        return add_low(lax.dynamic_slice_in_dim(array, self.bit(step) * half, half, axis=-2), got)

    def join(self, array, got, step):
        return ordered(self.bit(step), array, got, array.ndim - 2)

    def gather(self, array, last):
        for step in reversed(range(last)):
            array = self.join(array, self.swap(array, step), step)
        return array

    def total(self, array):
        last = self.steps - 1
        for step in range(last):
            array = self.keep(array, self.send(array, step), step)
        array = add_low(array, self.swap(array, last))
        return self.gather(array, last)


class Running:
    def __init__(self, rows, array, plan):
        self.rows, self.array, self.plan = rows, array, plan

    def start(self):
        kind, step = self.plan[0]
        return self.rows.send(self.array, step) if kind == "send" else self.rows.swap(self.array, step)

    def finish(self, got):
        kind, step = self.plan.pop(0)
        if kind == "send":
            self.array = self.rows.keep(self.array, got, step)
        elif kind == "full":
            self.array = add_low(self.array, got)
        else:
            self.array = self.rows.join(self.array, got, step)


def params(cost=None, **more):
    return dict(
        compiler_params=pltpu.CompilerParams(vmem_limit_bytes=VMEM_BYTES, **more), cost_estimate=cost
    )


def cost(flops, moved, exps=0):
    return pl.CostEstimate(flops=int(flops), bytes_accessed=int(moved), transcendentals=int(exps))


def shape(dims, dtype=bf16):
    return jax.ShapeDtypeStruct(dims, dtype)


def shards(
    tokens, w_qkv, b_qv, w_out, b_out, norm1_gain, norm1_shift, w_in, b_in, w_back, b_back,
    norm2_gain, norm2_shift, segment_ids, pair_ids,
):
    row_count, length = segment_ids.shape
    width = tokens.shape[1]
    local = w_out.shape[0]
    units = w_in.shape[1]
    heads = local // HEAD_DIM
    blocks = length // Q_BLOCK
    member = lax.axis_index("mp")
    own_row = lax.axis_index("dp") * row_count + member
    m_arr = member.astype(jnp.int32).reshape(1)
    any_spec = pl.BlockSpec(memory_space=pl.ANY)
    vmem_spec = pl.BlockSpec(memory_space=pltpu.VMEM)
    smem_spec = pl.BlockSpec(memory_space=pltpu.SMEM)
    dma = pltpu.SemaphoreType.DMA

    tall = lambda vector: vector.reshape(-1, LANES)
    bit_x, bit_z = bit_of("dp", 1), bit_of("dp", 2)
    bits = jnp.stack([2 * bit_x + bit_z, 2 * bit_z + bit_x]).astype(jnp.int32)
    out_pack, in_quarter, back_quarter = pl.pallas_call(
        prepare,
        in_specs=[smem_spec] + [vmem_spec] * 2 + [any_spec] * 2,
        out_specs=[vmem_spec] * 3,
        out_shape=[
            shape((local + 16, width)), shape((width // 4, units)), shape((units // 4, width)),
        ],
        scratch_shapes=[dma((2,))],
        name="prepare",
        **params(cost(1e6, 2e6)),
    )(bits, tall(b_in), w_out, w_in, w_back)
    near_in, near_back = hop(w_in, "mp", 1), hop(w_back, "mp", 1)
    near_out = hop(out_pack, "mp", 1)
    far_out = hop(out_pack, "mp", 2)
    b_qv, near_in, near_back, near_out = together(b_qv, near_in, near_back, near_out)
    in_quarter = hop(in_quarter, "mp", 2)
    back_quarter = hop(back_quarter, "mp", 2)
    w_t = jnp.swapaxes(w_qkv, 1, 2)

    windows = jnp.stack(
        [segment_ids[:, window_start(i, length) :][:, :K_WINDOW] for i in range(blocks)], axis=1
    )
    seg_rows = segment_ids[:, None, :]

    def attend(count, source):
        return pl.pallas_call(
            attend_forward,
            grid_spec=pltpu.PrefetchScalarGridSpec(
                num_scalar_prefetch=1,
                grid=(count,),
                in_specs=[
                    pl.BlockSpec((length, width), lambda i, m: (source(i) ^ m[0], 0)),
                    pl.BlockSpec(w_t.shape, lambda i, m: (0, 0, 0)),
                    pl.BlockSpec(b_qv.shape, lambda i, m: (0, 0)),
                    pl.BlockSpec((1, 1, length), lambda i, m: (source(i) ^ m[0], 0, 0)),
                    pl.BlockSpec((1, blocks, K_WINDOW), lambda i, m: (source(i) ^ m[0], 0, 0)),
                ],
                out_specs=[
                    pl.BlockSpec((1, 3, length, local), lambda i, m: (i, 0, 0, 0)),
                    pl.BlockSpec((1, heads * blocks, Q_BLOCK, K_WINDOW), lambda i, m: (i, 0, 0, 0)),
                ]
                + [pl.BlockSpec((length, local), lambda i, m: (0, 0))] * count,
                scratch_shapes=[pltpu.VMEM((length, local), bf16)],
            ),
            out_shape=[
                shape((count, 3, length, local)),
                shape((count, heads * blocks, Q_BLOCK, K_WINDOW)),
                *[shape((length, local))] * count,
            ],
            name="attend_forward",
            **params(cost(6 * count * length * width * local, 2e6 * count, count * heads * length * K_WINDOW)),
        )(m_arr, tokens, w_t, b_qv, seg_rows, windows)

    qkv_away, probs_away, ctx3, ctx2, ctx1 = attend(3, lambda i: 3 - i)
    ctx3, ctx2, ctx1, in_quarter, back_quarter, far_out = together(
        ctx3, ctx2, ctx1, in_quarter, back_quarter, far_out
    )
    in_got, back_got = hop(in_quarter, "dp", 2), hop(back_quarter, "dp", 1)
    qkv_own, probs_own, ctx0 = attend(1, lambda i: 0)
    out_parts = [out_pack, near_out, far_out, hop(late(far_out, ctx0), "mp", 1)]
    in_half = ordered(bit_z, in_quarter, late(in_got, ctx0), 0)
    back_half = ordered(bit_x, back_quarter, late(back_got, ctx0), 0)
    ctx_parts = [ctx0, hop(ctx1, "mp", 1), hop(ctx2, "mp", 2), hop(ctx3, "mp", 3)]
    seg_own = lax.dynamic_slice_in_dim(segment_ids, member, 1)
    pair_own = lax.dynamic_slice_in_dim(pair_ids, member, 1).reshape(-1, 1)
    pair_code = jnp.concatenate(
        [pair_own // 64, pair_own % 64, jnp.zeros((pair_own.shape[0], LANES - 2), jnp.int32)], axis=1
    ).astype(f32)
    in_got, back_got = hop(in_half, "dp", 1), hop(back_half, "dp", 2)
    act01, slope01, xhat1, rstd1, low1, total = pl.pallas_call(
        middle_first,
        in_specs=[smem_spec, any_spec] + [vmem_spec] * 3 + [any_spec] * 12,
        out_specs=[any_spec] * 2 + [vmem_spec] * 4,
        out_shape=[
            shape((2, length, units)), shape((2, length, units)),
            shape((length, width), f32), shape((length, LANES), f32), shape((length, width)),
            shape((length, width), f32),
        ],
        scratch_shapes=[
            pltpu.VMEM((length, width), bf16), pltpu.VMEM((4, length, local), bf16),
            pltpu.VMEM((4, local + 16, width), bf16), pltpu.VMEM((2, width, units), bf16),
            pltpu.VMEM((2, units, width), bf16), pltpu.VMEM((2, length, units), bf16),
            pltpu.VMEM((2, length, units), bf16), dma((13,)), dma((4,)),
        ],
        name="middle_first",
        **params(cost(2 * length * width * (width + 4 * units), 18e6, 2 * length * units)),
    )(
        m_arr, tokens, tall(b_out), tall(norm1_gain), tall(norm1_shift), *ctx_parts, *out_parts,
        w_in, near_in, w_back, near_back,
    )
    in_far = ordered(bit_x, in_half, late(in_got, total), 0)
    back_far = ordered(bit_z, back_half, late(back_got, total), 0)
    in_parts = [w_in, near_in, in_far, hop(in_far, "mp", 1)]
    back_parts = [w_back, near_back, back_far, hop(back_far, "mp", 1)]
    act23, slope23, xhat2, rstd2, out_own, pooled, lengths, msg = pl.pallas_call(
        middle_second,
        in_specs=[vmem_spec] * 6 + [any_spec] + [vmem_spec] * 2 + [any_spec] * 4,
        out_specs=[any_spec] * 2 + [vmem_spec] * 6,
        out_shape=[
            shape((2, length, units)), shape((2, length, units)),
            shape((length, width), f32), shape((length, LANES), f32), shape((length, width)),
            shape((16, width), f32), shape((16, LANES), f32), shape((8, 2 * width + LANES)),
        ],
        scratch_shapes=[
            pltpu.VMEM((2, width, units), bf16), pltpu.VMEM((2, units, width), bf16),
            pltpu.VMEM((2, length, units), bf16), pltpu.VMEM((2, length, units), bf16),
            pltpu.VMEM((length, width), f32), dma((5,)), dma((4,)),
        ],
        name="middle_second",
        **params(cost(8 * length * width * units, 12e6, 2 * length * units)),
    )(
        seg_own, pair_code, tall(b_back), tall(norm2_gain), tall(norm2_shift), low1, total,
        *out_parts[2:], *in_parts[2:], *back_parts[2:],
    )

    everyone = msg[None]
    for flip in reversed(bits_below(lax.axis_size("dp"))):
        everyone = both_ways("dp", flip, everyone)
    for flip in reversed(bits_below(lax.axis_size("mp"))):
        everyone = both_ways("mp", flip, everyone)
    everyone = everyone.reshape(-1, msg.shape[1])

    loss, grad_pooled = pl.pallas_call(
        contrast,
        in_specs=[smem_spec] + [vmem_spec] * 4,
        out_specs=[vmem_spec] * 2,
        out_shape=[shape((8, LANES), f32), shape((16, width), f32)],
        scratch_shapes=[pltpu.VMEM((everyone.shape[0], LANES), f32)],
        name="contrast",
        **params(cost(4e8, 2e6, 1e5)),
    )(own_row.astype(jnp.int32).reshape(1), everyone, msg, pooled, lengths)

    rows = Rows()
    grad_low2, grad_resid2, vec2, back_send = pl.pallas_call(
        back_second,
        in_specs=[vmem_spec] * 5 + [any_spec] * 2,
        out_specs=[vmem_spec] * 4,
        out_shape=[
            shape((length, width)), shape((length, width), f32), shape((8, width), f32),
            shape((2, units, width)),
        ],
        scratch_shapes=[
            pltpu.VMEM((length, width), f32), pltpu.VMEM((2, length, units), bf16),
            pltpu.VMEM((3, 8, width), f32), dma((2,)),
        ],
        name="back_second",
        **params(cost(4 * length * width * units, 14e6)),
    )(grad_pooled, seg_own, xhat2, rstd2, tall(norm2_gain), act01, act23)
    back_got = hop(back_send, "mp", 1)
    back_keep = pl.pallas_call(
        back_outer,
        in_specs=[vmem_spec] + [any_spec] * 2,
        out_specs=vmem_spec,
        out_shape=shape((2, units, width)),
        scratch_shapes=[pltpu.VMEM((2, length, units), bf16), dma((2,))],
        name="back_outer",
        **params(cost(4 * length * width * units, 8e6)),
    )(grad_low2, act01, act23)
    back_sum = add_low(back_keep, back_got)
    grad_low2, back_sum = together(grad_low2, back_sum)
    back_got = rows.send(back_sum, 0)
    out_far = hop(late(out_own, grad_low2), "mp", 2)

    gb, grad_resid1, attn_low, vec1, d_bin, *ctx_grads = pl.pallas_call(
        back_first,
        in_specs=[vmem_spec] * 5 + [any_spec] * 14,
        out_specs=[any_spec] + [vmem_spec] * 8,
        out_shape=[
            shape((4, length, units)), shape((length, width), f32), shape((length, width)),
            shape((8, width), f32), shape((4, units), f32), *[shape((length, local))] * 4,
        ],
        scratch_shapes=[
            pltpu.VMEM((4, length, units), bf16), pltpu.VMEM((4, local + 16, width), bf16),
            pltpu.VMEM((4, width, units), bf16), pltpu.VMEM((4, units, width), bf16),
            pltpu.VMEM((4, length, units), bf16), pltpu.VMEM((length, width), f32),
            pltpu.VMEM((3, 8, width), f32), dma((16,)), dma((4,)),
        ],
        name="back_first",
        **params(cost(2 * length * width * (width + 8 * units), 25e6)),
    )(
        grad_low2, grad_resid2, xhat1, rstd1, tall(norm1_gain), slope01, slope23, *out_parts, *in_parts, *back_parts,
    )

    attn_low, back_got, out_far = together(attn_low, back_got, out_far)
    out_pair = ordered(bit_of("mp", 2), out_own[None], out_far[None], 0)
    back_sum = rows.keep(back_sum, back_got, 0)
    got3 = hop(ctx_grads[3], "mp", 3)

    def first_grads(pieces, low):
        return pl.pallas_call(
            functools.partial(weight_grads, pieces),
            in_specs=[vmem_spec] * 7 + [any_spec],
            out_specs=vmem_spec,
            out_shape=shape((2, width + local + VEC_ROWS, units)),
            scratch_shapes=[pltpu.VMEM((2, length, units), bf16), dma((2,))],
            name="weight_grads",
            **params(cost(4 * length * width * (units + local), 7e6)),
        )(low1, low, vec1, vec2, d_bin, ctx_parts[pieces[0]], ctx_parts[pieces[1]], gb)

    first_send = first_grads((3, 1), attn_low)
    got3, attn_low, first_send, out_pair = together(got3, attn_low, first_send, out_pair)
    out_other = hop(out_pair, "mp", 1)
    first_got = hop(first_send, "mp", 1)
    got2 = hop(late(ctx_grads[2], first_send), "mp", 2)
    first_keep = first_grads((2, 0), attn_low)
    first_sum = add_low(first_keep, first_got)
    own_grad, first_sum, got2, back_sum, out_other = together(
        ctx_grads[0], first_sum, got2, back_sum, out_other
    )
    first_far, first_near = first_sum[0], first_sum[1]
    cut = first_far.shape[0] // 4
    far0 = hop(first_far[:cut], "mp", 2)
    back_got = rows.send(back_sum, 1)
    got1 = hop(late(ctx_grads[1], own_grad), "mp", 1)

    def attend_back(count, source, first, qkv, probs, grads, sums):
        same = lambda i, m: (0, 0)
        last = source(0) == 1
        out_specs = [pl.BlockSpec((length, width), same)] * count
        out_shape = [shape((length, width))] * count
        if last:
            out_specs.append(pl.BlockSpec((3 * local + VEC_ROWS, width), same))
            out_shape.append(shape((3 * local + VEC_ROWS, width)))
        else:
            out_specs += [pl.BlockSpec((3 * local, width), same), pl.BlockSpec((8, local), same)]
            out_shape += [shape((3 * local, width), f32), shape((8, local), f32)]
        return pl.pallas_call(
            functools.partial(attend_backward, count, len(sums) == 0, last),
            grid_spec=pltpu.PrefetchScalarGridSpec(
                num_scalar_prefetch=1,
                grid=(count,),
                in_specs=[
                    pl.BlockSpec((length, width), lambda i, m: (source(i) ^ m[0], 0)),
                    pl.BlockSpec(w_t.shape, lambda i, m: (0, 0, 0)),
                    pl.BlockSpec((1, 3, length, local), lambda i, m: (first + i, 0, 0, 0)),
                    pl.BlockSpec(
                        (1, heads * blocks, Q_BLOCK, K_WINDOW), lambda i, m: (first + i, 0, 0, 0)
                    ),
                ]
                + [pl.BlockSpec((length, local), same)] * count
                + [pl.BlockSpec(part.shape, same) for part in sums],
                out_specs=out_specs,
                scratch_shapes=[
                    pltpu.VMEM((length, local), bf16), pltpu.VMEM((length, local), f32),
                    pltpu.VMEM((length, local), f32), pltpu.VMEM((3 * local, width), f32),
                    pltpu.VMEM((8, local), f32),
                ],
            ),
            out_shape=out_shape,
            name="attend_backward",
            **params(cost(12 * count * length * width * local, 4e6 * count)),
        )(m_arr, tokens, w_t, qkv, probs, *grads, *sums)

    back0, *sums = attend_back(1, lambda i: 0, 0, qkv_own, probs_own, [own_grad], [])
    far0, back_got, got1, *sums = together(far0, back_got, got1, *sums)
    far1 = hop(first_far[cut : 3 * cut], "mp", 2)
    back_sum = rows.keep(back_sum, back_got, 1)
    back_got = rows.send(back_sum, 2)
    back3, back2, *sums = attend_back(2, lambda i: 3 - i, 0, qkv_away, probs_away, [got3, got2], sums)
    far1, back_got, *sums = together(far1, back_got, *sums)
    far2 = hop(first_far[3 * cut :], "mp", 2)
    back_sum = rows.keep(back_sum, back_got, 2)
    for step in range(3, rows.steps):
        back_sum = rows.keep(back_sum, rows.send(back_sum, step), step)
    back_got = hop(back_sum[0], "mp", 2)
    far2, first_near, back3, *sums = together(far2, first_near, back3, *sums)
    first_sum = add_low(first_near, jnp.concatenate([far0, far1, far2], axis=0))
    first_got = rows.send(first_sum, 0)
    tok_got3 = hop(back3, "mp", 1)
    back1, d_qkv = attend_back(1, lambda i: 1, 2, qkv_away, probs_away, [got1], sums)
    last = rows.steps - 1
    d_qkv, tok_got3, back_got, first_got = together(d_qkv, tok_got3, back_got, first_got)
    back_sum = add_low(back_sum[1], back_got)
    first_sum = rows.keep(first_sum, first_got, 0)
    tok_got1 = hop(back1, "mp", 1)
    far = add_low(back2, tok_got3)
    down = [("send", step) for step in range(last)] + [("full", last)]
    up = [("join", step) for step in reversed(range(last))]
    sums = [
        Running(rows, first_sum, down[1:] + up),
        Running(rows, d_qkv, down + up),
        Running(rows, back_sum, [("join", last)] + up),
    ]
    sizes = [length // 48 * 16] * 2
    sizes.append(length - sum(sizes))
    mine, pieces, tok_totals, at, stage = None, None, [], 0, 0
    while any(part.plan for part in sums):
        parts = [part for part in sums if part.plan]
        hops = [part.start() for part in parts]
        if stage == 0:
            hops.append(tok_got1)
        elif stage <= len(sizes):
            rows_now = slice(at, at + sizes[stage - 1])
            at += sizes[stage - 1]
            hops.append(hop(jnp.stack([mine[rows_now], far[rows_now]]), "mp", 2))
        elif stage == len(sizes) + 1:
            tok_pair = jnp.concatenate(tok_totals, axis=1)
            hops.append(hop(tok_pair, "mp", 1))
        hops = list(together(*hops))
        for part in parts:
            part.finish(hops.pop(0))
        if stage == 0:
            mine = add_low(back0.astype(f32) + grad_resid1, hops[0])
        elif stage <= len(sizes):
            got = hops[0]
            tok_totals.append(
                ordered(
                    bit_of("mp", 2),
                    add_low(mine[rows_now], got[1])[None],
                    add_low(far[rows_now], got[0])[None],
                    0,
                )
            )
        elif stage == len(sizes) + 1:
            d_tokens = rows_of_all(tok_pair, hops[0])
        stage += 1
    sum_first, sum_qkv, sum_back = (part.array for part in sums)
    layer_out = rows_of_all(out_pair, out_other)

    at = width + local
    vectors = sum_first[at : at + 8].astype(f32) + sum_first[at + 8 : at + 16].astype(f32)
    shares = lax.dynamic_slice_in_dim(vectors[0:6], member * local, local, axis=1)
    at = 3 * local
    d_bqv = sum_qkv[at : at + 2, 0:local].astype(f32) + sum_qkv[at + 8 : at + 10, 0:local].astype(f32)
    d_wqkv = jnp.swapaxes(sum_qkv[0:at].reshape(3, local, width), 1, 2).astype(f32)
    return (
        loss[0, 0],
        layer_out,
        d_tokens,
        d_wqkv,
        d_bqv,
        sum_first[width : width + local].astype(f32),
        shares[2],
        shares[0],
        shares[1],
        sum_first[0:width].astype(f32),
        vectors[6],
        sum_back.astype(f32),
        shares[5],
        shares[3],
        shares[4],
    )


def both_ways(axis, flip, array):
    other = hop(array, axis, flip)
    low_first = jnp.stack([array, other], axis=1)
    high_first = jnp.stack([other, array], axis=1)
    joined = jnp.where(bit_of(axis, flip) == 0, low_first, high_first)
    return joined.reshape(-1, *array.shape[1:])


def rows_of_all(pair, other):
    low_first = jnp.stack([pair, other], axis=1)
    high_first = jnp.stack([other, pair], axis=1)
    joined = jnp.where(bit_of("mp", 1) == 0, low_first, high_first)
    return joined.reshape(-1, pair.shape[-1])


def solution(mesh):
    return jax.shard_map(
        shards,
        mesh=mesh,
        in_specs=(
            P("dp", None),
            P(None, None, "mp"),
            P(None, "mp"),
            P("mp", None),
            P(),
            P(),
            P(),
            P(None, "mp"),
            P("mp"),
            P("mp", None),
            P(),
            P(),
            P(),
            P("dp", None),
            P("dp", None),
        ),
        out_specs=(
            P(),
            P("dp", None),
            P("dp", None),
            P(None, None, "mp"),
            P(None, "mp"),
            P("mp", None),
            P("mp"),
            P("mp"),
            P("mp"),
            P(None, "mp"),
            P("mp"),
            P("mp", None),
            P("mp"),
            P("mp"),
            P("mp"),
        ),
        check_vma=False,
    )
```

```python
import functools

import jax
import jax.numpy as jnp
from jax import lax
from jax.experimental import pallas as pl
from jax.experimental.pallas import tpu as pltpu
from jax.sharding import PartitionSpec as P

HEAD_DIM = 64
Q_BLOCK = 128
K_WINDOW = 256
LANES = 128
TILE = 256
ROW_TILE = 64
VEC_ROWS = 64
VMEM_BYTES = 52 * 1024 * 1024

norm_eps = 1e-06
inv_temp = 50.0
loss_scale = 8.0
masked_score = -1000000000.0

f32 = jnp.float32
bf16 = jnp.bfloat16


def product(left_side, right_side):
    return jnp.dot(left_side, right_side, preferred_element_type=f32)


def product_t(left_side, right_side):
    return lax.dot_general(
        left_side, right_side, (((0,), (0,)), ((), ())), preferred_element_type=f32
    )


def product_nt(left_side, right_side):
    return lax.dot_general(
        left_side, right_side, (((1,), (1,)), ((), ())), preferred_element_type=f32
    )


def window_start(block, length):
    return min(max(block * Q_BLOCK - HEAD_DIM, 0), length - K_WINDOW)


def gelu_and_slope(values):
    bell = jnp.exp(values * values * -0.5)
    t = 1.0 / (1.0 + (0.3275911 * 0.7071067811865476) * jnp.abs(values))
    poly = 1.061405429 * t - 1.453152027
    poly = poly * t + 1.421413741
    poly = poly * t - 0.284496736
    poly = poly * t + 0.254829592
    tail = (0.5 * t) * (poly * bell)
    phi = jnp.where(values >= 0.0, 1.0 - tail, tail)
    return values * phi, phi + (values * 0.3989422804014327) * bell


def head_lanes(pair, which):
    lane = lax.broadcasted_iota(jnp.int32, pair.shape, 1)
    keep = (lane < HEAD_DIM) if which == 0 else (lane >= HEAD_DIM)
    return jnp.where(keep, pair, jnp.zeros_like(pair))


def columns(array, first, count):
    return array[:, first : first + count]


def head_parts(array, local_width):
    parts = []
    for head in range(local_width // HEAD_DIM):
        first = head // 2 * LANES
        width = min(LANES, local_width - first)
        part = columns(array, first, width)
        parts.append(part if width < LANES else head_lanes(part, head % 2))
    return parts


def merge_heads(results, local_width):
    pieces = []
    for first in range(0, local_width, LANES):
        head = first // HEAD_DIM
        if local_width - first >= LANES:
            lane = lax.broadcasted_iota(jnp.int32, results[head].shape, 1)
            pieces.append((first, jnp.where(lane < HEAD_DIM, results[head], results[head + 1])))
        else:
            pieces.append((first, results[head]))
    return pieces


def attend_forward(m_ref, tok_ref, w_ref, b_ref, seg_ref, win_ref, qkv_ref, prob_ref, *refs):
    ctx_refs, ctx_v = refs[:-1], refs[-1]
    length = tok_ref.shape[0]
    width = w_ref.shape[1]
    heads = width // HEAD_DIM
    tok = tok_ref[...]
    q = ((product_nt(tok, w_ref[0]) + b_ref[0:1, :]).astype(bf16) * HEAD_DIM**-0.5).astype(bf16)
    k = product_nt(tok, w_ref[1]).astype(bf16)
    v = (product_nt(tok, w_ref[2]) + b_ref[1:2, :]).astype(bf16)
    qkv_ref[0, 0] = q
    qkv_ref[0, 1] = k
    qkv_ref[0, 2] = v
    q_parts = head_parts(q, width)
    slot = lax.broadcasted_iota(jnp.int32, (16, 1), 0)
    own = (seg_ref[0] == slot).astype(f32).astype(bf16)
    for block in range(length // Q_BLOCK):
        at, start = block * Q_BLOCK, window_start(block, length)
        seen = (win_ref[0, block : block + 1, :] == slot).astype(f32).astype(bf16)
        mask = (product_t(columns(own, at, Q_BLOCK), seen) - 1.0) * -masked_score
        results = []
        for head in range(heads):
            first = head // 2 * LANES
            part = min(LANES, width - first)
            key = k[start : start + K_WINDOW, first : first + part]
            value = v[start : start + K_WINDOW, first : first + part]
            scores = product_nt(q_parts[head][at : at + Q_BLOCK], key) + mask
            weights = jnp.exp(scores - jnp.max(scores, axis=-1, keepdims=True))
            low = (weights * (1.0 / jnp.sum(weights, axis=-1, keepdims=True))).astype(bf16)
            prob_ref[0, head * (length // Q_BLOCK) + block] = low
            results.append(product(low, value))
        for first, merged in merge_heads(results, width):
            ctx_v[at : at + Q_BLOCK, first : first + merged.shape[1]] = merged.astype(bf16)
    for piece, ctx_ref in enumerate(ctx_refs):

        @pl.when(pl.program_id(0) == piece)
        def _():
            ctx_ref[...] = ctx_v[...]


def attend_backward(count, first, last, m_ref, tok_ref, w_ref, qkv_ref, prob_ref, *refs):
    g_refs, refs = refs[:count], refs[count:]
    if not first:
        before_ref, vec_before_ref, *refs = refs
    o_refs, refs = refs[:count], refs[count:]
    if last:
        dw_ref, gctx, gk_sum, gv_sum, dw_sum, vec_sum = refs
    else:
        dw_ref, vec_ref, gctx, gk_sum, gv_sum, dw_sum, vec_sum = refs
    step = pl.program_id(0)
    length = tok_ref.shape[0]
    width = w_ref.shape[1]
    heads = width // HEAD_DIM
    for piece, g_ref in enumerate(g_refs):

        @pl.when(step == piece)
        def _():
            gctx[...] = g_ref[...]

    @pl.when(step == 0)
    def _():
        dw_sum[...] = jnp.zeros_like(dw_sum) if first else before_ref[...]
        vec_sum[...] = jnp.zeros_like(vec_sum) if first else vec_before_ref[...]

    gk_sum[...] = jnp.zeros_like(gk_sum)
    gv_sum[...] = jnp.zeros_like(gv_sum)
    q, k, v = qkv_ref[0, 0], qkv_ref[0, 1], qkv_ref[0, 2]
    q_parts = head_parts(q, width)
    g_parts = head_parts(gctx[...], width)
    gq_blocks = []
    for block in range(length // Q_BLOCK):
        at, start = block * Q_BLOCK, window_start(block, length)
        rows = slice(start, start + K_WINDOW)
        results, gk, gv = [], {}, {}
        for head in range(heads):
            first = head // 2 * LANES
            part = min(LANES, width - first)
            key, value = k[rows, first : first + part], v[rows, first : first + part]
            grad = g_parts[head][at : at + Q_BLOCK]
            low = prob_ref[0, head * (length // Q_BLOCK) + block]
            prob = low.astype(f32)
            grad_prob = product_nt(grad, value)
            inner = jnp.sum(prob * grad_prob, axis=-1, keepdims=True)
            grad_low = (prob * (grad_prob - inner)).astype(bf16)
            results.append(product(grad_low, key))
            gk_part = product_t(grad_low, q_parts[head][at : at + Q_BLOCK])
            gv_part = product_t(low, grad)
            gk[first] = gk[first] + gk_part if first in gk else gk_part
            gv[first] = gv[first] + gv_part if first in gv else gv_part
        for first in gk:
            lanes = slice(first, first + gk[first].shape[1])
            gk_sum[rows, lanes] += gk[first]
            gv_sum[rows, lanes] += gv[first]
        gq_blocks.append(merge_heads(results, width))
    gq = jnp.concatenate(
        [
            jnp.concatenate(
                [(blocks[i][1] * HEAD_DIM**-0.5).astype(bf16) for blocks in gq_blocks], axis=0
            )
            for i in range(len(gq_blocks[0]))
        ],
        axis=1,
    )
    gk, gv = gk_sum[...].astype(bf16), gv_sum[...].astype(bf16)
    tok = tok_ref[...]
    back = None
    for c, grad in enumerate((gq, gk, gv)):
        dw_sum[c * width : (c + 1) * width, :] += product_t(grad, tok)
        term = product(grad, w_ref[c])
        back = term if back is None else back + term
    vec_sum[0:1, :] += jnp.sum(gq.astype(f32), axis=0, keepdims=True)
    vec_sum[1:2, :] += jnp.sum(gv.astype(f32), axis=0, keepdims=True)
    back = back.astype(bf16)
    for piece, o_ref in enumerate(o_refs):

        @pl.when(step == piece)
        def _():
            o_ref[...] = back

    @pl.when(step == count - 1)
    def _():
        if not last:
            dw_ref[...] = dw_sum[...]
            vec_ref[...] = vec_sum[...]
            return
        dw_ref[0 : 3 * width, :] = dw_sum[...].astype(bf16)
        vec = vec_sum[...]
        top = vec.astype(bf16)
        rest = (vec - top.astype(f32)).astype(bf16)
        dw_ref[3 * width :, :] = jnp.zeros((VEC_ROWS, dw_ref.shape[1]), bf16)
        dw_ref[3 * width : 3 * width + 16, 0:width] = jnp.concatenate([top, rest], axis=0)


def row_of(ref):
    return jnp.concatenate([ref[i : i + 1, :] for i in range(ref.shape[0])], axis=1)


def start_all(pairs, sems):
    copies = []
    for i, (source, target) in enumerate(pairs):
        copy = pltpu.make_async_copy(source, target, sems.at[i])
        copy.start()
        copies.append(copy)
    return copies


def prepare(bits_ref, bias_ref, out_ref, in_hbm, back_hbm, pack_ref, in_ref, back_ref, sems):
    quarter = in_ref.shape[0]
    in_at = pl.multiple_of(bits_ref[0] * quarter, quarter)
    back_at = pl.multiple_of(bits_ref[1] * quarter, quarter)
    copies = start_all(
        [(in_hbm.at[pl.ds(in_at, quarter)], in_ref), (back_hbm.at[pl.ds(back_at, quarter)], back_ref)], sems
    )
    local = out_ref.shape[0]
    bias = row_of(bias_ref)
    high = bias.astype(bf16)
    rest = bias - high.astype(f32)
    middle = rest.astype(bf16)
    low = (rest - middle.astype(f32)).astype(bf16)
    slot = lax.broadcasted_iota(jnp.int32, (16, 1), 0)
    rows = jnp.where(slot == 0, high.astype(f32), 0.0)
    rows = jnp.where(slot == 1, middle.astype(f32), rows)
    rows = jnp.where(slot == 2, low.astype(f32), rows)
    pack_ref[0:local, :] = out_ref[...]
    pack_ref[local : local + 16, :] = rows.astype(bf16)
    for copy in copies:
        copy.wait()


def feed(r, low_ref, wi_v, b_in, act_v, slope_v):
    for first in range(0, wi_v.shape[2], TILE):
        cols = slice(first, first + TILE)
        before = product(low_ref[...], wi_v[r, :, cols]) + b_in[:, cols]
        active, slope = gelu_and_slope(before)
        act_v[r, :, cols] = active.astype(bf16)
        slope_v[r, :, cols] = slope.astype(bf16)


def middle_first(
    m_ref, tok_hbm, bias_ref, gain_ref, shift_ref, c0, c1, c2, c3, wo0, wo1, wo2, wo3, wi0, wi1, wb0, wb1,
    act_hbm, slope_hbm, xhat1_ref, rstd1_ref, low1_ref, total_ref,
    tok_v, ctx_v, wo_v, wi_v, wb_v, act_v, slope_v, sems, out_sems,
):
    length, width = tok_v.shape
    local = ctx_v.shape[2]
    b_out, gain1, shift1 = row_of(bias_ref), row_of(gain_ref), row_of(shift_ref)
    at = pl.multiple_of(m_ref[0] * length, length)
    copies = start_all(
        [(tok_hbm.at[pl.ds(at, length)], tok_v)]
        + [(c, ctx_v.at[r]) for r, c in enumerate((c0, c1, c2, c3))]
        + [(w, wo_v.at[r]) for r, w in enumerate((wo0, wo1, wo2, wo3))]
        + [(w, wi_v.at[r]) for r, w in enumerate((wi0, wi1))]
        + [(w, wb_v.at[r]) for r, w in enumerate((wb0, wb1))],
        sems,
    )
    for copy in copies[:9]:
        copy.wait()
    for first in range(0, width, TILE):
        cols = slice(first, first + TILE)
        total = tok_v[:, cols].astype(f32) + b_out[:, cols]
        for r in range(4):
            total = total + product(ctx_v[r], wo_v[r, 0:local, cols])
        total_ref[:, cols] = total

    @pl.loop(0, length // ROW_TILE)
    def _(i):
        rows = pl.ds(pl.multiple_of(i * ROW_TILE, ROW_TILE), ROW_TILE)
        values = total_ref[rows, :]
        center = values - jnp.mean(values, axis=-1, keepdims=True)
        rate = lax.rsqrt(jnp.mean(center * center, axis=-1, keepdims=True) + norm_eps)
        xhat = center * rate
        xhat1_ref[rows, :] = xhat
        rstd1_ref[rows, :] = jnp.broadcast_to(rate, (ROW_TILE, LANES))
        normed = xhat * gain1 + shift1
        total_ref[rows, :] = normed
        low1_ref[rows, :] = normed.astype(bf16)

    outs = []
    for r in range(2):
        copies[9 + r].wait()
        b_in = jnp.sum(wo_v[r, local : local + 16, :].astype(f32), axis=0, keepdims=True)
        feed(r, low1_ref, wi_v, b_in, act_v, slope_v)
        outs += start_all(
            [(act_v.at[r], act_hbm.at[r]), (slope_v.at[r], slope_hbm.at[r])],
            out_sems.at[pl.ds(2 * r, 2)],
        )
    for copy in copies[11:]:
        copy.wait()
    for first in range(0, width, TILE):
        cols = slice(first, first + TILE)
        total_ref[:, cols] += product(act_v[0], wb_v[0, :, cols]) + product(act_v[1], wb_v[1, :, cols])
    for copy in outs:
        copy.wait()


def middle_second(
    seg_ref, pair_ref, bias_ref, gain_ref, shift_ref, low1_ref, total_hbm, wo2, wo3, wi2, wi3, wb2, wb3,
    act_hbm, slope_hbm, xhat2_ref, rstd2_ref, out_ref, pooled_ref, len_ref, msg_ref,
    wi_v, wb_v, act_v, slope_v, resid, sems, out_sems,
):
    length, width = resid.shape
    local = wo2.shape[0] - 16
    b_back, gain2, shift2 = row_of(bias_ref), row_of(gain_ref), row_of(shift_ref)
    copies = start_all(
        [(w, wi_v.at[r]) for r, w in enumerate((wi2, wi3))]
        + [(total_hbm, resid)]
        + [(w, wb_v.at[r]) for r, w in enumerate((wb2, wb3))],
        sems,
    )
    outs = []
    for r in range(2):
        copies[r].wait()
        b_in = jnp.sum((wo2, wo3)[r][local : local + 16, :].astype(f32), axis=0, keepdims=True)
        feed(r, low1_ref, wi_v, b_in, act_v, slope_v)
        outs += start_all(
            [(act_v.at[r], act_hbm.at[r]), (slope_v.at[r], slope_hbm.at[r])],
            out_sems.at[pl.ds(2 * r, 2)],
        )
    for copy in copies[2:]:
        copy.wait()
    for first in range(0, width, TILE):
        cols = slice(first, first + TILE)
        total = resid[:, cols] + b_back[:, cols]
        resid[:, cols] = total + product(act_v[0], wb_v[0, :, cols]) + product(act_v[1], wb_v[1, :, cols])

    @pl.loop(0, length // ROW_TILE)
    def _(i):
        rows = pl.ds(pl.multiple_of(i * ROW_TILE, ROW_TILE), ROW_TILE)
        values = resid[rows, :]
        center = values - jnp.mean(values, axis=-1, keepdims=True)
        rate = lax.rsqrt(jnp.mean(center * center, axis=-1, keepdims=True) + norm_eps)
        xhat = center * rate
        xhat2_ref[rows, :] = xhat
        rstd2_ref[rows, :] = jnp.broadcast_to(rate, (ROW_TILE, LANES))
        out_ref[rows, :] = (xhat * gain2 + shift2).astype(bf16)

    own = members(seg_ref)
    sums = product(own.astype(bf16), out_ref[...])
    count = jnp.sum(own, axis=-1, keepdims=True)
    pooled = sums / count
    rate = lax.rsqrt(jnp.sum(pooled * pooled, axis=-1, keepdims=True) + norm_eps)
    unit = (pooled * rate).astype(bf16)
    pooled_ref[...] = pooled
    len_ref[...] = jnp.broadcast_to(count, len_ref.shape)
    half = unit.astype(f32)
    msg_ref[:, 0:width] = half[0:8].astype(bf16)
    msg_ref[:, width : 2 * width] = half[8:16].astype(bf16)
    msg_ref[:, 2 * width :] = pair_ref[...].astype(bf16)
    for copy in outs:
        copy.wait()


def members(seg_ref):
    slot = lax.broadcasted_iota(jnp.int32, (16, 1), 0)
    segment = jnp.where(slot < 8, 2 * slot, 2 * slot - 15)
    return (seg_ref[...] == segment).astype(f32)


def contrast(ids_ref, all_ref, own_ref, pooled_ref, len_ref, loss_ref, grad_ref, log_v):
    width = pooled_ref.shape[1]
    count = all_ref.shape[0]
    block = min(count, 256)
    passages = all_ref[:, width : 2 * width]
    number = lax.broadcasted_iota(jnp.int32, (1, count), 1).astype(f32)

    def target(rows):
        coded = rows[:, 2 * width :].astype(f32)
        return coded[:, 0:1] * 64.0 + coded[:, 1:2]

    def statistics(rows, scores):
        best = jnp.max(scores, axis=-1, keepdims=True)
        log_total = best + jnp.log(jnp.sum(jnp.exp(scores - best), axis=-1, keepdims=True))
        return log_total, (number == target(rows)).astype(f32)

    def one_block(i, total):
        rows_at = pl.ds(pl.multiple_of(i * block, block), block)
        rows = all_ref[rows_at, :]
        scores = product_nt(rows[:, 0:width], passages) * inv_temp
        log_total, positive = statistics(rows, scores)
        log_v[rows_at, :] = jnp.broadcast_to(log_total, (block, LANES))
        return total + jnp.sum(log_total - jnp.sum(scores * positive, axis=-1, keepdims=True), keepdims=True)

    total = lax.fori_loop(0, count // block, one_block, jnp.zeros((1, 1), f32))
    loss_ref[...] = jnp.broadcast_to(total * (1.0 / count), loss_ref.shape)
    own = own_ref[...]
    scores = product_nt(own[:, 0:width], passages) * inv_temp
    log_total, positive = statistics(own, scores)
    grad_low = ((jnp.exp(scores - log_total) - positive) * (loss_scale * inv_temp)).astype(bf16)
    grad_query = product(grad_low, passages)

    everyone = all_ref[...]
    queries = everyone[:, 0:width]
    passage = jnp.concatenate(
        [own[:, width : 2 * width].astype(f32), jnp.zeros((LANES - 8, width), f32)], axis=0
    ).astype(bf16)
    lane = lax.broadcasted_iota(jnp.int32, (1, LANES), 1)
    scores = product_nt(queries, passage) * inv_temp
    number = jnp.where(lane < 8, ids_ref[0] * 8 + lane, -1).astype(f32)
    positive = (number == target(everyone)).astype(f32)
    weight = jnp.exp(scores - log_v[...]) - positive
    grad_low = (jnp.where(lane < 8, weight, 0.0) * (loss_scale * inv_temp)).astype(bf16)
    grad_passage = product_t(grad_low, queries)[0:8]

    grad_unit = jnp.concatenate([grad_query, grad_passage], axis=0)
    pooled = pooled_ref[...]
    rate = lax.rsqrt(jnp.sum(pooled * pooled, axis=-1, keepdims=True) + norm_eps)
    inner = jnp.sum(pooled * grad_unit, axis=-1, keepdims=True)
    grad = rate * grad_unit - rate * rate * rate * pooled * inner
    grad_ref[...] = grad / len_ref[:, 0:1]


def column_total(values):
    return jnp.sum(values.reshape(values.shape[0] // 8, 8, values.shape[1]), axis=0)


def back_second(
    gp_ref, seg_ref, xhat_ref, rstd_ref, gain_ref, act01_hbm, act23_hbm,
    low_ref, grad_ref, vec_ref, d_ref,
    out_v, act_v, sums, sems,
):
    length, width = xhat_ref.shape
    gain = row_of(gain_ref)
    copies = start_all([(act23_hbm.at[1], act_v.at[0]), (act01_hbm.at[1], act_v.at[1])], sems)
    own = members(seg_ref).astype(bf16)
    top = gp_ref[...].astype(bf16)
    rest = (gp_ref[...] - top.astype(f32)).astype(bf16)
    out_v[...] = product_t(own, top) + product_t(own, rest)
    sums[...] = jnp.zeros_like(sums)

    @pl.loop(0, length // ROW_TILE)
    def _(i):
        rows = pl.ds(pl.multiple_of(i * ROW_TILE, ROW_TILE), ROW_TILE)
        grad_out, xhat = out_v[rows, :], xhat_ref[rows, :]
        sums[0] += column_total(grad_out * xhat)
        sums[1] += column_total(grad_out)
        grad = grad_out * gain
        first = jnp.mean(grad, axis=-1, keepdims=True)
        second = jnp.mean(grad * xhat, axis=-1, keepdims=True)
        grad = (grad - first - xhat * second) * rstd_ref[rows, 0:1]
        sums[2] += column_total(grad)
        grad_ref[rows, :] = grad
        low_ref[rows, :] = grad.astype(bf16)

    vec_ref[...] = jnp.zeros_like(vec_ref)
    for i in range(3):
        vec_ref[i : i + 1, :] = jnp.sum(sums[i], axis=0, keepdims=True)
    back_products(copies, act_v, low_ref, d_ref)


def back_products(copies, act_v, low_ref, d_ref):
    for i, copy in enumerate(copies):
        copy.wait()
        for first in range(0, act_v.shape[2], TILE):
            cols = slice(first, first + TILE)
            d_ref[i, cols, :] = product_t(act_v[i, :, cols], low_ref[...]).astype(bf16)


def back_outer(low_ref, act01_hbm, act23_hbm, d_ref, act_v, sems):
    copies = start_all([(act23_hbm.at[0], act_v.at[0]), (act01_hbm.at[0], act_v.at[1])], sems)
    back_products(copies, act_v, low_ref, d_ref)


def back_first(
    low_ref, resid_ref, xhat_ref, rstd_ref, gain_ref, slope01_hbm, slope23_hbm,
    wo0, wo1, wo2, wo3, wi0, wi1, wi2, wi3, wb0, wb1, wb2, wb3,
    gb_hbm, grad_ref, attn_ref, vec_ref, bin_ref, x0, x1, x2, x3,
    slope_v, wo_v, wi_v, wb_v, gb_v, total_v, sums, sems, out_sems,
):
    length, width = xhat_ref.shape
    units = wi_v.shape[2]
    gain = row_of(gain_ref)
    copies = start_all(
        [p for r, w in enumerate((wb0, wb1, wb2, wb3)) for p in ((w, wb_v.at[r]), ((slope01_hbm, slope23_hbm)[r // 2].at[r % 2], slope_v.at[r]))]
        + [(w, wi_v.at[r]) for r, w in enumerate((wi0, wi1, wi2, wi3))]
        + [(w, wo_v.at[r]) for r, w in enumerate((wo0, wo1, wo2, wo3))],
        sems,
    )
    outs = []
    for r in range(4):
        copies[2 * r].wait()
        copies[2 * r + 1].wait()
        for first in range(0, units, TILE):
            cols = slice(first, first + TILE)
            grad = product_nt(low_ref[...], wb_v[r, cols, :])
            low = (grad * slope_v[r, :, cols].astype(f32)).astype(bf16)
            gb_v[r, :, cols] = low
            bin_ref[r : r + 1, cols] = jnp.sum(column_total(low.astype(f32)), axis=0, keepdims=True)
        outs += start_all([(gb_v.at[r], gb_hbm.at[r])], out_sems.at[pl.ds(r, 1)])
    for copy in copies[8:]:
        copy.wait()
    for first in range(0, width, TILE):
        cols = slice(first, first + TILE)
        total = resid_ref[:, cols]
        for r in range(4):
            total = total + product_nt(gb_v[r], wi_v[r, cols, :])
        total_v[:, cols] = total
    sums[...] = jnp.zeros_like(sums)

    @pl.loop(0, length // ROW_TILE)
    def _(i):
        rows = pl.ds(pl.multiple_of(i * ROW_TILE, ROW_TILE), ROW_TILE)
        grad_out, xhat = total_v[rows, :], xhat_ref[rows, :]
        sums[0] += column_total(grad_out * xhat)
        sums[1] += column_total(grad_out)
        grad = grad_out * gain
        first = jnp.mean(grad, axis=-1, keepdims=True)
        second = jnp.mean(grad * xhat, axis=-1, keepdims=True)
        grad = (grad - first - xhat * second) * rstd_ref[rows, 0:1]
        sums[2] += column_total(grad)
        grad_ref[rows, :] = grad
        attn_ref[rows, :] = grad.astype(bf16)

    vec_ref[...] = jnp.zeros_like(vec_ref)
    for i in range(3):
        vec_ref[i : i + 1, :] = jnp.sum(sums[i], axis=0, keepdims=True)
    for r, x_ref in enumerate((x0, x1, x2, x3)):
        x_ref[...] = product_nt(attn_ref[...], wo_v[r, 0 : x_ref.shape[1], :]).astype(bf16)
    for copy in outs:
        copy.wait()


def weight_grads(
    pieces, low1_ref, attn_ref, vec1_ref, vec2_ref, bin_ref, ca, cb, gb_hbm,
    d_ref,
    gb_v, sems,
):
    length, width = low1_ref.shape
    units = gb_v.shape[2]
    local = ca.shape[1]
    copies = start_all([(gb_hbm.at[r], gb_v.at[i]) for i, r in enumerate(pieces)], sems)
    for i, (r, c_ref) in enumerate(zip(pieces, (ca, cb))):
        copies[i].wait()
        for first in range(0, width, TILE):
            cols = slice(first, first + TILE)
            d_ref[i, cols, :] = product_t(low1_ref[:, cols], gb_v[i]).astype(bf16)
        d_ref[i, width : width + local, :] = product_t(c_ref[...], attn_ref[...]).astype(bf16)
        rows = jnp.concatenate(
            [vec1_ref[0:3, :], vec2_ref[0:3, :], bin_ref[r : r + 1, :], jnp.zeros((1, units), f32)],
            axis=0,
        )
        top = rows.astype(bf16)
        rest = (rows - top.astype(f32)).astype(bf16)
        at = width + local
        d_ref[i, at : at + 16, :] = jnp.concatenate([top, rest], axis=0)
        d_ref[i, at + 16 : at + VEC_ROWS, :] = jnp.zeros((VEC_ROWS - 16, units), bf16)


def hop(array, axis, flip):
    size = lax.axis_size(axis)
    return lax.ppermute(array, axis, [(i, i ^ flip) for i in range(size)])


def bit_of(axis, flip):
    return (lax.axis_index(axis) // flip) % 2


def ordered(bit, mine, other, axis):
    low_first = jnp.concatenate([mine, other], axis=axis)
    high_first = jnp.concatenate([other, mine], axis=axis)
    return jnp.where(bit == 0, low_first, high_first)


def bits_below(size):
    flips, flip = [], 1
    while flip < size:
        flips.append(flip)
        flip *= 2
    return flips


def together(*arrays):
    return lax.optimization_barrier(arrays)


def late(array, *earlier):
    return lax.optimization_barrier((array, *earlier))[0]


def gather_parts(mine, first=None):
    near = hop(mine, "mp", 1)
    far = hop(mine, "mp", 2) if first is None else first
    return [mine, near, far, hop(far, "mp", 1)]


def join(part, flip):
    return ordered(bit_of("dp", flip), part, hop(part, "dp", flip), 0)


def add_low(left_side, right_side):
    return (left_side.astype(f32) + right_side.astype(f32)).astype(bf16)


class Rows:
    def __init__(self):
        self.dp, self.mp = lax.axis_size("dp"), lax.axis_size("mp")
        flips = bits_below(self.dp)
        self.orders = flips, flips[1:2] + flips[:1] + flips[2:]
        self.steps = len(flips)

    def swap(self, values, step):
        pairs = [
            (i, ((i // self.mp) ^ self.orders[i % self.mp % 2][step]) * self.mp + i % self.mp)
            for i in range(self.dp * self.mp)
        ]
        return lax.ppermute(values, ("dp", "mp"), pairs)

    def bit(self, step):
        even, odd = (bit_of("dp", order[step]) for order in self.orders)
        return jnp.where(lax.axis_index("mp") % 2 == 1, odd, even)

    def send(self, array, step):
        half = array.shape[-2] // 2
        away = lax.dynamic_slice_in_dim(array, (1 - self.bit(step)) * half, half, axis=-2)
        return self.swap(away, step)

    def keep(self, array, got, step):
        half = array.shape[-2] // 2
        return add_low(lax.dynamic_slice_in_dim(array, self.bit(step) * half, half, axis=-2), got)

    def join(self, array, got, step):
        return ordered(self.bit(step), array, got, array.ndim - 2)

    def gather(self, array, last):
        for step in reversed(range(last)):
            array = self.join(array, self.swap(array, step), step)
        return array

    def total(self, array):
        last = self.steps - 1
        for step in range(last):
            array = self.keep(array, self.send(array, step), step)
        array = add_low(array, self.swap(array, last))
        return self.gather(array, last)


class Running:
    def __init__(self, rows, array, plan):
        self.rows, self.array, self.plan = rows, array, plan

    def start(self):
        kind, step = self.plan[0]
        return self.rows.send(self.array, step) if kind == "send" else self.rows.swap(self.array, step)

    def finish(self, got):
        kind, step = self.plan.pop(0)
        if kind == "send":
            self.array = self.rows.keep(self.array, got, step)
        elif kind == "full":
            self.array = add_low(self.array, got)
        else:
            self.array = self.rows.join(self.array, got, step)


def params(cost=None, **more):
    return dict(
        compiler_params=pltpu.CompilerParams(vmem_limit_bytes=VMEM_BYTES, **more), cost_estimate=cost
    )


def cost(flops, moved, exps=0):
    return pl.CostEstimate(flops=int(flops), bytes_accessed=int(moved), transcendentals=int(exps))


def shape(dims, dtype=bf16):
    return jax.ShapeDtypeStruct(dims, dtype)


def shards(
    tokens, w_qkv, b_qv, w_out, b_out, norm1_gain, norm1_shift, w_in, b_in, w_back, b_back,
    norm2_gain, norm2_shift, segment_ids, pair_ids,
):
    row_count, length = segment_ids.shape
    width = tokens.shape[1]
    local = w_out.shape[0]
    units = w_in.shape[1]
    heads = local // HEAD_DIM
    blocks = length // Q_BLOCK
    member = lax.axis_index("mp")
    own_row = lax.axis_index("dp") * row_count + member
    m_arr = member.astype(jnp.int32).reshape(1)
    any_spec = pl.BlockSpec(memory_space=pl.ANY)
    vmem_spec = pl.BlockSpec(memory_space=pltpu.VMEM)
    smem_spec = pl.BlockSpec(memory_space=pltpu.SMEM)
    dma = pltpu.SemaphoreType.DMA

    tall = lambda vector: vector.reshape(-1, LANES)
    bit_x, bit_z = bit_of("dp", 1), bit_of("dp", 2)
    bits = jnp.stack([2 * bit_x + bit_z, 2 * bit_z + bit_x]).astype(jnp.int32)
    out_pack, in_quarter, back_quarter = pl.pallas_call(
        prepare,
        in_specs=[smem_spec] + [vmem_spec] * 2 + [any_spec] * 2,
        out_specs=[vmem_spec] * 3,
        out_shape=[
            shape((local + 16, width)), shape((width // 4, units)), shape((units // 4, width)),
        ],
        scratch_shapes=[dma((2,))],
        name="prepare",
        **params(cost(1e6, 2e6)),
    )(bits, tall(b_in), w_out, w_in, w_back)
    near_in, near_back = hop(w_in, "mp", 1), hop(w_back, "mp", 1)
    near_out = hop(out_pack, "mp", 1)
    far_out = hop(out_pack, "mp", 2)
    b_qv, near_in, near_back, near_out = together(b_qv, near_in, near_back, near_out)
    in_quarter = hop(in_quarter, "mp", 2)
    back_quarter = hop(back_quarter, "mp", 2)
    w_t = jnp.swapaxes(w_qkv, 1, 2)

    windows = jnp.stack(
        [segment_ids[:, window_start(i, length) :][:, :K_WINDOW] for i in range(blocks)], axis=1
    )
    seg_rows = segment_ids[:, None, :]

    def attend(count, source):
        return pl.pallas_call(
            attend_forward,
            grid_spec=pltpu.PrefetchScalarGridSpec(
                num_scalar_prefetch=1,
                grid=(count,),
                in_specs=[
                    pl.BlockSpec((length, width), lambda i, m: (source(i) ^ m[0], 0)),
                    pl.BlockSpec(w_t.shape, lambda i, m: (0, 0, 0)),
                    pl.BlockSpec(b_qv.shape, lambda i, m: (0, 0)),
                    pl.BlockSpec((1, 1, length), lambda i, m: (source(i) ^ m[0], 0, 0)),
                    pl.BlockSpec((1, blocks, K_WINDOW), lambda i, m: (source(i) ^ m[0], 0, 0)),
                ],
                out_specs=[
                    pl.BlockSpec((1, 3, length, local), lambda i, m: (i, 0, 0, 0)),
                    pl.BlockSpec((1, heads * blocks, Q_BLOCK, K_WINDOW), lambda i, m: (i, 0, 0, 0)),
                ]
                + [pl.BlockSpec((length, local), lambda i, m: (0, 0))] * count,
                scratch_shapes=[pltpu.VMEM((length, local), bf16)],
            ),
            out_shape=[
                shape((count, 3, length, local)),
                shape((count, heads * blocks, Q_BLOCK, K_WINDOW)),
                *[shape((length, local))] * count,
            ],
            name="attend_forward",
            **params(cost(6 * count * length * width * local, 2e6 * count, count * heads * length * K_WINDOW)),
        )(m_arr, tokens, w_t, b_qv, seg_rows, windows)

    qkv_away, probs_away, ctx3, ctx2, ctx1 = attend(3, lambda i: 3 - i)
    ctx3, ctx2, ctx1, in_quarter, back_quarter, far_out = together(
        ctx3, ctx2, ctx1, in_quarter, back_quarter, far_out
    )
    in_got, back_got = hop(in_quarter, "dp", 2), hop(back_quarter, "dp", 1)
    qkv_own, probs_own, ctx0 = attend(1, lambda i: 0)
    out_parts = [out_pack, near_out, far_out, hop(late(far_out, ctx0), "mp", 1)]
    ctx_got2, ctx_got3 = hop(ctx2, "mp", 2), hop(ctx3, "mp", 3)
    in_half = ordered(bit_z, in_quarter, late(in_got, ctx0), 0)
    back_half = ordered(bit_x, back_quarter, late(back_got, ctx0), 0)
    in_half, back_half, ctx_got2, ctx_got3 = together(in_half, back_half, ctx_got2, ctx_got3)
    ctx_parts = [ctx0, hop(ctx1, "mp", 1), ctx_got2, ctx_got3]
    seg_own = lax.dynamic_slice_in_dim(segment_ids, member, 1)
    pair_own = lax.dynamic_slice_in_dim(pair_ids, member, 1).reshape(-1, 1)
    pair_code = jnp.concatenate(
        [pair_own // 64, pair_own % 64, jnp.zeros((pair_own.shape[0], LANES - 2), jnp.int32)], axis=1
    ).astype(f32)
    in_got, back_got = hop(in_half, "dp", 1), hop(back_half, "dp", 2)
    act01, slope01, xhat1, rstd1, low1, total = pl.pallas_call(
        middle_first,
        in_specs=[smem_spec, any_spec] + [vmem_spec] * 3 + [any_spec] * 12,
        out_specs=[any_spec] * 2 + [vmem_spec] * 4,
        out_shape=[
            shape((2, length, units)), shape((2, length, units)),
            shape((length, width), f32), shape((length, LANES), f32), shape((length, width)),
            shape((length, width), f32),
        ],
        scratch_shapes=[
            pltpu.VMEM((length, width), bf16), pltpu.VMEM((4, length, local), bf16),
            pltpu.VMEM((4, local + 16, width), bf16), pltpu.VMEM((2, width, units), bf16),
            pltpu.VMEM((2, units, width), bf16), pltpu.VMEM((2, length, units), bf16),
            pltpu.VMEM((2, length, units), bf16), dma((13,)), dma((4,)),
        ],
        name="middle_first",
        **params(cost(2 * length * width * (width + 4 * units), 18e6, 2 * length * units)),
    )(
        m_arr, tokens, tall(b_out), tall(norm1_gain), tall(norm1_shift), *ctx_parts, *out_parts,
        w_in, near_in, w_back, near_back,
    )
    in_far = ordered(bit_x, in_half, late(in_got, total), 0)
    back_far = ordered(bit_z, back_half, late(back_got, total), 0)
    in_parts = [w_in, near_in, in_far, hop(in_far, "mp", 1)]
    back_parts = [w_back, near_back, back_far, hop(back_far, "mp", 1)]
    act23, slope23, xhat2, rstd2, out_own, pooled, lengths, msg = pl.pallas_call(
        middle_second,
        in_specs=[vmem_spec] * 6 + [any_spec] + [vmem_spec] * 2 + [any_spec] * 4,
        out_specs=[any_spec] * 2 + [vmem_spec] * 6,
        out_shape=[
            shape((2, length, units)), shape((2, length, units)),
            shape((length, width), f32), shape((length, LANES), f32), shape((length, width)),
            shape((16, width), f32), shape((16, LANES), f32), shape((8, 2 * width + LANES)),
        ],
        scratch_shapes=[
            pltpu.VMEM((2, width, units), bf16), pltpu.VMEM((2, units, width), bf16),
            pltpu.VMEM((2, length, units), bf16), pltpu.VMEM((2, length, units), bf16),
            pltpu.VMEM((length, width), f32), dma((5,)), dma((4,)),
        ],
        name="middle_second",
        **params(cost(8 * length * width * units, 12e6, 2 * length * units)),
    )(
        seg_own, pair_code, tall(b_back), tall(norm2_gain), tall(norm2_shift), low1, total,
        *out_parts[2:], *in_parts[2:], *back_parts[2:],
    )

    everyone = msg[None]
    steps = [("dp", flip) for flip in reversed(bits_below(lax.axis_size("dp")))]
    steps += [("mp", flip) for flip in reversed(bits_below(lax.axis_size("mp")))]
    while len(steps) > 1:
        everyone = four_ways(everyone, *steps[:2])
        steps = steps[2:]
    if steps:
        everyone = both_ways(everyone, hop(everyone, *steps[0]), *steps[0])
    everyone = everyone.reshape(-1, msg.shape[1])

    loss, grad_pooled = pl.pallas_call(
        contrast,
        in_specs=[smem_spec] + [vmem_spec] * 4,
        out_specs=[vmem_spec] * 2,
        out_shape=[shape((8, LANES), f32), shape((16, width), f32)],
        scratch_shapes=[pltpu.VMEM((everyone.shape[0], LANES), f32)],
        name="contrast",
        **params(cost(4e8, 2e6, 1e5)),
    )(own_row.astype(jnp.int32).reshape(1), everyone, msg, pooled, lengths)

    rows = Rows()
    grad_low2, grad_resid2, vec2, back_send = pl.pallas_call(
        back_second,
        in_specs=[vmem_spec] * 5 + [any_spec] * 2,
        out_specs=[vmem_spec] * 4,
        out_shape=[
            shape((length, width)), shape((length, width), f32), shape((8, width), f32),
            shape((2, units, width)),
        ],
        scratch_shapes=[
            pltpu.VMEM((length, width), f32), pltpu.VMEM((2, length, units), bf16),
            pltpu.VMEM((3, 8, width), f32), dma((2,)),
        ],
        name="back_second",
        **params(cost(4 * length * width * units, 14e6)),
    )(grad_pooled, seg_own, xhat2, rstd2, tall(norm2_gain), act01, act23)
    back_got = hop(back_send, "mp", 1)
    back_keep = pl.pallas_call(
        back_outer,
        in_specs=[vmem_spec] + [any_spec] * 2,
        out_specs=vmem_spec,
        out_shape=shape((2, units, width)),
        scratch_shapes=[pltpu.VMEM((2, length, units), bf16), dma((2,))],
        name="back_outer",
        **params(cost(4 * length * width * units, 8e6)),
    )(grad_low2, act01, act23)
    back_sum = add_low(back_keep, back_got)
    grad_low2, back_sum = together(grad_low2, back_sum)
    back_got = rows.send(back_sum, 0)
    out_far = hop(late(out_own, grad_low2), "mp", 2)

    gb, grad_resid1, attn_low, vec1, d_bin, *ctx_grads = pl.pallas_call(
        back_first,
        in_specs=[vmem_spec] * 5 + [any_spec] * 14,
        out_specs=[any_spec] + [vmem_spec] * 8,
        out_shape=[
            shape((4, length, units)), shape((length, width), f32), shape((length, width)),
            shape((8, width), f32), shape((4, units), f32), *[shape((length, local))] * 4,
        ],
        scratch_shapes=[
            pltpu.VMEM((4, length, units), bf16), pltpu.VMEM((4, local + 16, width), bf16),
            pltpu.VMEM((4, width, units), bf16), pltpu.VMEM((4, units, width), bf16),
            pltpu.VMEM((4, length, units), bf16), pltpu.VMEM((length, width), f32),
            pltpu.VMEM((3, 8, width), f32), dma((16,)), dma((4,)),
        ],
        name="back_first",
        **params(cost(2 * length * width * (width + 8 * units), 25e6)),
    )(
        grad_low2, grad_resid2, xhat1, rstd1, tall(norm1_gain), slope01, slope23, *out_parts, *in_parts, *back_parts,
    )

    attn_low, back_got, out_far = together(attn_low, back_got, out_far)
    out_pair = ordered(bit_of("mp", 2), out_own[None], out_far[None], 0)
    back_sum = rows.keep(back_sum, back_got, 0)
    got3 = hop(ctx_grads[3], "mp", 3)

    def first_grads(pieces, low):
        return pl.pallas_call(
            functools.partial(weight_grads, pieces),
            in_specs=[vmem_spec] * 7 + [any_spec],
            out_specs=vmem_spec,
            out_shape=shape((2, width + local + VEC_ROWS, units)),
            scratch_shapes=[pltpu.VMEM((2, length, units), bf16), dma((2,))],
            name="weight_grads",
            **params(cost(4 * length * width * (units + local), 7e6)),
        )(low1, low, vec1, vec2, d_bin, ctx_parts[pieces[0]], ctx_parts[pieces[1]], gb)

    first_send = first_grads((3, 1), attn_low)
    got3, attn_low, first_send, out_pair = together(got3, attn_low, first_send, out_pair)
    out_other = hop(out_pair, "mp", 1)
    first_got = hop(first_send, "mp", 1)
    got2 = hop(late(ctx_grads[2], first_send), "mp", 2)
    first_keep = first_grads((2, 0), attn_low)
    own_grad, first_keep, first_got, got2, back_sum, out_other = together(
        ctx_grads[0], first_keep, first_got, got2, back_sum, out_other
    )
    first_far = hop(add_low(first_keep[0], first_got[0]), "mp", 2)
    back_got = rows.send(back_sum, 1)
    got1 = hop(late(ctx_grads[1], own_grad), "mp", 1)

    def attend_back(count, source, first, qkv, probs, grads, sums):
        same = lambda i, m: (0, 0)
        last = source(0) == 1
        out_specs = [pl.BlockSpec((length, width), same)] * count
        out_shape = [shape((length, width))] * count
        if last:
            out_specs.append(pl.BlockSpec((3 * local + VEC_ROWS, width), same))
            out_shape.append(shape((3 * local + VEC_ROWS, width)))
        else:
            out_specs += [pl.BlockSpec((3 * local, width), same), pl.BlockSpec((8, local), same)]
            out_shape += [shape((3 * local, width), f32), shape((8, local), f32)]
        return pl.pallas_call(
            functools.partial(attend_backward, count, len(sums) == 0, last),
            grid_spec=pltpu.PrefetchScalarGridSpec(
                num_scalar_prefetch=1,
                grid=(count,),
                in_specs=[
                    pl.BlockSpec((length, width), lambda i, m: (source(i) ^ m[0], 0)),
                    pl.BlockSpec(w_t.shape, lambda i, m: (0, 0, 0)),
                    pl.BlockSpec((1, 3, length, local), lambda i, m: (first + i, 0, 0, 0)),
                    pl.BlockSpec(
                        (1, heads * blocks, Q_BLOCK, K_WINDOW), lambda i, m: (first + i, 0, 0, 0)
                    ),
                ]
                + [pl.BlockSpec((length, local), same)] * count
                + [pl.BlockSpec(part.shape, same) for part in sums],
                out_specs=out_specs,
                scratch_shapes=[
                    pltpu.VMEM((length, local), bf16), pltpu.VMEM((length, local), f32),
                    pltpu.VMEM((length, local), f32), pltpu.VMEM((3 * local, width), f32),
                    pltpu.VMEM((8, local), f32),
                ],
            ),
            out_shape=out_shape,
            name="attend_backward",
            **params(cost(12 * count * length * width * local, 4e6 * count)),
        )(m_arr, tokens, w_t, qkv, probs, *grads, *sums)

    back0, *sums = attend_back(1, lambda i: 0, 0, qkv_own, probs_own, [own_grad], [])
    back_got, got1, *sums = together(back_got, got1, *sums)
    back_sum = rows.keep(back_sum, back_got, 1)
    back_got = rows.send(back_sum, 2)
    back3, back2, *sums = attend_back(2, lambda i: 3 - i, 0, qkv_away, probs_away, [got3, got2], sums)
    back_got, *sums = together(back_got, *sums)
    back_sum = rows.keep(back_sum, back_got, 2)
    for step in range(3, rows.steps):
        back_sum = rows.keep(back_sum, rows.send(back_sum, step), step)
    back_got = hop(back_sum[0], "mp", 2)
    first_far, first_keep, first_got, back3, *sums = together(
        first_far, first_keep, first_got, back3, *sums
    )
    first_sum = (first_keep[1].astype(f32) + first_got[1].astype(f32) + first_far.astype(f32)).astype(bf16)
    first_got = rows.send(first_sum, 0)
    tok_got3 = hop(back3, "mp", 1)
    back1, d_qkv = attend_back(1, lambda i: 1, 2, qkv_away, probs_away, [got1], sums)
    last = rows.steps - 1
    d_qkv, tok_got3, back_got, first_got = together(d_qkv, tok_got3, back_got, first_got)
    back_sum = add_low(back_sum[1], back_got)
    first_sum = rows.keep(first_sum, first_got, 0)
    tok_got1 = hop(back1, "mp", 1)
    far = add_low(back2, tok_got3)
    down = [("send", step) for step in range(last)] + [("full", last)]
    up = [("join", step) for step in reversed(range(last))]
    sums = [
        Running(rows, first_sum, down[1:] + up),
        Running(rows, d_qkv, down + up),
        Running(rows, back_sum, [("join", last)] + up),
    ]
    stage, extra = 0, [tok_got1, hop(far, "mp", 2)]
    while any(part.plan for part in sums):
        parts = [part for part in sums if part.plan]
        starts = [part.start() for part in parts]
        if extra:
            tied = list(together(starts[1], *extra))
            starts[1] = tied.pop(0)
        hops = starts + (tied if extra else [])
        for part in parts:
            part.finish(hops.pop(0))
        if stage == 0:
            own = back0.astype(f32) + grad_resid1 + hops[0].astype(f32) + hops[1].astype(f32)
            own = own.astype(bf16)
            extra = [hop(own, "mp", 2)]
        elif stage == 1:
            tok_pair = ordered(bit_of("mp", 2), own[None], hops[0][None], 0)
            extra = [hop(tok_pair, "mp", 1)]
        elif stage == 2:
            d_tokens = rows_of_all(tok_pair, hops[0])
            extra = []
        stage += 1
    sum_first, sum_qkv, sum_back = (part.array for part in sums)
    layer_out = rows_of_all(out_pair, out_other)

    at = width + local
    vectors = sum_first[at : at + 8].astype(f32) + sum_first[at + 8 : at + 16].astype(f32)
    shares = lax.dynamic_slice_in_dim(vectors[0:6], member * local, local, axis=1)
    at = 3 * local
    d_bqv = sum_qkv[at : at + 2, 0:local].astype(f32) + sum_qkv[at + 8 : at + 10, 0:local].astype(f32)
    d_wqkv = jnp.swapaxes(sum_qkv[0:at].reshape(3, local, width), 1, 2).astype(f32)
    return (
        loss[0, 0],
        layer_out,
        d_tokens,
        d_wqkv,
        d_bqv,
        sum_first[width : width + local].astype(f32),
        shares[2],
        shares[0],
        shares[1],
        sum_first[0:width].astype(f32),
        vectors[6],
        sum_back.astype(f32),
        shares[5],
        shares[3],
        shares[4],
    )


def both_ways(array, other, axis, flip):
    low_first = jnp.stack([array, other], axis=1)
    high_first = jnp.stack([other, array], axis=1)
    joined = jnp.where(bit_of(axis, flip) == 0, low_first, high_first)
    return joined.reshape(-1, *array.shape[1:])


def four_ways(array, first, second):
    dp, mp = lax.axis_size("dp"), lax.axis_size("mp")

    def fetch(*steps):
        flip = sum(step * (mp if axis == "dp" else 1) for axis, step in steps)
        return lax.ppermute(array, ("dp", "mp"), [(i, i ^ flip) for i in range(dp * mp)])

    far, near, corner = fetch(first), fetch(second), fetch(first, second)
    count = array.shape[0]
    mine = both_ways(array, near, *second).reshape(count, 2, *array.shape[1:])
    theirs = both_ways(far, corner, *second).reshape(count, 2, *array.shape[1:])
    return both_ways(mine, theirs, *first).reshape(-1, *array.shape[1:])


def rows_of_all(pair, other):
    low_first = jnp.stack([pair, other], axis=1)
    high_first = jnp.stack([other, pair], axis=1)
    joined = jnp.where(bit_of("mp", 1) == 0, low_first, high_first)
    return joined.reshape(-1, pair.shape[-1])


def solution(mesh):
    return jax.shard_map(
        shards,
        mesh=mesh,
        in_specs=(
            P("dp", None),
            P(None, None, "mp"),
            P(None, "mp"),
            P("mp", None),
            P(),
            P(),
            P(),
            P(None, "mp"),
            P("mp"),
            P("mp", None),
            P(),
            P(),
            P(),
            P("dp", None),
            P("dp", None),
        ),
        out_specs=(
            P(),
            P("dp", None),
            P("dp", None),
            P(None, None, "mp"),
            P(None, "mp"),
            P("mp", None),
            P("mp"),
            P("mp"),
            P("mp"),
            P(None, "mp"),
            P("mp"),
            P("mp", None),
            P("mp"),
            P("mp"),
            P("mp"),
        ),
        check_vma=False,
    )
```

```python
import functools

import jax
import jax.numpy as jnp
from jax import lax
from jax.experimental import pallas as pl
from jax.experimental.pallas import tpu as pltpu
from jax.sharding import PartitionSpec as P

HEAD_DIM = 64
Q_BLOCK = 128
K_WINDOW = 256
LANES = 128
TILE = 256
ROW_TILE = 64
VEC_ROWS = 64
VMEM_BYTES = 52 * 1024 * 1024

norm_eps = 1e-06
inv_temp = 50.0
loss_scale = 8.0
masked_score = -1000000000.0

f32 = jnp.float32
bf16 = jnp.bfloat16


def product(left_side, right_side):
    return jnp.dot(left_side, right_side, preferred_element_type=f32)


def product_t(left_side, right_side):
    return lax.dot_general(
        left_side, right_side, (((0,), (0,)), ((), ())), preferred_element_type=f32
    )


def product_nt(left_side, right_side):
    return lax.dot_general(
        left_side, right_side, (((1,), (1,)), ((), ())), preferred_element_type=f32
    )


def window_start(block, length):
    return min(max(block * Q_BLOCK - HEAD_DIM, 0), length - K_WINDOW)


def gelu_and_slope(values):
    bell = jnp.exp(values * values * -0.5)
    t = 1.0 / (1.0 + (0.3275911 * 0.7071067811865476) * jnp.abs(values))
    poly = 1.061405429 * t - 1.453152027
    poly = poly * t + 1.421413741
    poly = poly * t - 0.284496736
    poly = poly * t + 0.254829592
    tail = (0.5 * t) * (poly * bell)
    phi = jnp.where(values >= 0.0, 1.0 - tail, tail)
    return values * phi, phi + (values * 0.3989422804014327) * bell


def head_lanes(pair, which):
    lane = lax.broadcasted_iota(jnp.int32, pair.shape, 1)
    keep = (lane < HEAD_DIM) if which == 0 else (lane >= HEAD_DIM)
    return jnp.where(keep, pair, jnp.zeros_like(pair))


def columns(array, first, count):
    return array[:, first : first + count]


def head_parts(array, local_width):
    parts = []
    for head in range(local_width // HEAD_DIM):
        first = head // 2 * LANES
        width = min(LANES, local_width - first)
        part = columns(array, first, width)
        parts.append(part if width < LANES else head_lanes(part, head % 2))
    return parts


def merge_heads(results, local_width):
    pieces = []
    for first in range(0, local_width, LANES):
        head = first // HEAD_DIM
        if local_width - first >= LANES:
            lane = lax.broadcasted_iota(jnp.int32, results[head].shape, 1)
            pieces.append((first, jnp.where(lane < HEAD_DIM, results[head], results[head + 1])))
        else:
            pieces.append((first, results[head]))
    return pieces


def attend_forward(held, m_ref, tok_ref, w_ref, b_ref, seg_ref, win_ref, *refs):
    qkv_ref, prob_ref, *ctx_refs, ctx_v = refs[held:]
    length = tok_ref.shape[0]
    width = w_ref.shape[1]
    heads = width // HEAD_DIM
    tok = tok_ref[...]
    q = ((product_nt(tok, w_ref[0]) + b_ref[0:1, :]).astype(bf16) * HEAD_DIM**-0.5).astype(bf16)
    k = product_nt(tok, w_ref[1]).astype(bf16)
    v = (product_nt(tok, w_ref[2]) + b_ref[1:2, :]).astype(bf16)
    qkv_ref[0, 0] = q
    qkv_ref[0, 1] = k
    qkv_ref[0, 2] = v
    q_parts = head_parts(q, width)
    slot = lax.broadcasted_iota(jnp.int32, (16, 1), 0)
    own = (seg_ref[0] == slot).astype(f32).astype(bf16)
    for block in range(length // Q_BLOCK):
        at, start = block * Q_BLOCK, window_start(block, length)
        seen = (win_ref[0, block : block + 1, :] == slot).astype(f32).astype(bf16)
        mask = (product_t(columns(own, at, Q_BLOCK), seen) - 1.0) * -masked_score
        results = []
        for head in range(heads):
            first = head // 2 * LANES
            part = min(LANES, width - first)
            key = k[start : start + K_WINDOW, first : first + part]
            value = v[start : start + K_WINDOW, first : first + part]
            scores = product_nt(q_parts[head][at : at + Q_BLOCK], key) + mask
            weights = jnp.exp(scores - jnp.max(scores, axis=-1, keepdims=True))
            low = (weights * (1.0 / jnp.sum(weights, axis=-1, keepdims=True))).astype(bf16)
            prob_ref[0, head * (length // Q_BLOCK) + block] = low
            results.append(product(low, value))
        for first, merged in merge_heads(results, width):
            ctx_v[at : at + Q_BLOCK, first : first + merged.shape[1]] = merged.astype(bf16)
    for piece, ctx_ref in enumerate(ctx_refs):

        @pl.when(pl.program_id(0) == piece)
        def _():
            ctx_ref[...] = ctx_v[...]


def attend_backward(count, first, last, m_ref, tok_ref, w_ref, qkv_ref, prob_ref, *refs):
    g_refs, refs = refs[:count], refs[count:]
    if not first:
        before_ref, vec_before_ref, *refs = refs
    o_refs, refs = refs[:count], refs[count:]
    if last:
        dw_ref, gctx, gk_sum, gv_sum, dw_sum, vec_sum = refs
    else:
        dw_ref, vec_ref, gctx, gk_sum, gv_sum, dw_sum, vec_sum = refs
    step = pl.program_id(0)
    length = tok_ref.shape[0]
    width = w_ref.shape[1]
    heads = width // HEAD_DIM
    for piece, g_ref in enumerate(g_refs):

        @pl.when(step == piece)
        def _():
            gctx[...] = g_ref[...]

    @pl.when(step == 0)
    def _():
        dw_sum[...] = jnp.zeros_like(dw_sum) if first else before_ref[...]
        vec_sum[...] = jnp.zeros_like(vec_sum) if first else vec_before_ref[...]

    gk_sum[...] = jnp.zeros_like(gk_sum)
    gv_sum[...] = jnp.zeros_like(gv_sum)
    q, k, v = qkv_ref[0, 0], qkv_ref[0, 1], qkv_ref[0, 2]
    q_parts = head_parts(q, width)
    g_parts = head_parts(gctx[...], width)
    gq_blocks = []
    for block in range(length // Q_BLOCK):
        at, start = block * Q_BLOCK, window_start(block, length)
        rows = slice(start, start + K_WINDOW)
        results, gk, gv = [], {}, {}
        for head in range(heads):
            first = head // 2 * LANES
            part = min(LANES, width - first)
            key, value = k[rows, first : first + part], v[rows, first : first + part]
            grad = g_parts[head][at : at + Q_BLOCK]
            low = prob_ref[0, head * (length // Q_BLOCK) + block]
            prob = low.astype(f32)
            grad_prob = product_nt(grad, value)
            inner = jnp.sum(prob * grad_prob, axis=-1, keepdims=True)
            grad_low = (prob * (grad_prob - inner)).astype(bf16)
            results.append(product(grad_low, key))
            gk_part = product_t(grad_low, q_parts[head][at : at + Q_BLOCK])
            gv_part = product_t(low, grad)
            gk[first] = gk[first] + gk_part if first in gk else gk_part
            gv[first] = gv[first] + gv_part if first in gv else gv_part
        for first in gk:
            lanes = slice(first, first + gk[first].shape[1])
            gk_sum[rows, lanes] += gk[first]
            gv_sum[rows, lanes] += gv[first]
        gq_blocks.append(merge_heads(results, width))
    gq = jnp.concatenate(
        [
            jnp.concatenate(
                [(blocks[i][1] * HEAD_DIM**-0.5).astype(bf16) for blocks in gq_blocks], axis=0
            )
            for i in range(len(gq_blocks[0]))
        ],
        axis=1,
    )
    gk, gv = gk_sum[...].astype(bf16), gv_sum[...].astype(bf16)
    tok = tok_ref[...]
    back = None
    for c, grad in enumerate((gq, gk, gv)):
        dw_sum[c * width : (c + 1) * width, :] += product_t(grad, tok)
        term = product(grad, w_ref[c])
        back = term if back is None else back + term
    vec_sum[0:1, :] += jnp.sum(gq.astype(f32), axis=0, keepdims=True)
    vec_sum[1:2, :] += jnp.sum(gv.astype(f32), axis=0, keepdims=True)
    back = back.astype(bf16)
    for piece, o_ref in enumerate(o_refs):

        @pl.when(step == piece)
        def _():
            o_ref[...] = back

    @pl.when(step == count - 1)
    def _():
        if not last:
            dw_ref[...] = dw_sum[...]
            vec_ref[...] = vec_sum[...]
            return
        dw_ref[0 : 3 * width, :] = dw_sum[...].astype(bf16)
        vec = vec_sum[...]
        top = vec.astype(bf16)
        rest = (vec - top.astype(f32)).astype(bf16)
        dw_ref[3 * width :, :] = jnp.zeros((VEC_ROWS, dw_ref.shape[1]), bf16)
        dw_ref[3 * width : 3 * width + 16, 0:width] = jnp.concatenate([top, rest], axis=0)


def row_of(ref):
    return jnp.concatenate([ref[i : i + 1, :] for i in range(ref.shape[0])], axis=1)


def start_all(pairs, sems):
    copies = []
    for i, (source, target) in enumerate(pairs):
        copy = pltpu.make_async_copy(source, target, sems.at[i])
        copy.start()
        copies.append(copy)
    return copies


def prepare(bits_ref, bias_ref, out_ref, in_hbm, back_hbm, pack_ref, in_ref, back_ref, sems):
    quarter = in_ref.shape[0]
    in_at = pl.multiple_of(bits_ref[0] * quarter, quarter)
    back_at = pl.multiple_of(bits_ref[1] * quarter, quarter)
    copies = start_all(
        [(in_hbm.at[pl.ds(in_at, quarter)], in_ref), (back_hbm.at[pl.ds(back_at, quarter)], back_ref)], sems
    )
    local = out_ref.shape[0]
    bias = row_of(bias_ref)
    high = bias.astype(bf16)
    rest = bias - high.astype(f32)
    middle = rest.astype(bf16)
    low = (rest - middle.astype(f32)).astype(bf16)
    slot = lax.broadcasted_iota(jnp.int32, (16, 1), 0)
    rows = jnp.where(slot == 0, high.astype(f32), 0.0)
    rows = jnp.where(slot == 1, middle.astype(f32), rows)
    rows = jnp.where(slot == 2, low.astype(f32), rows)
    pack_ref[0:local, :] = out_ref[...]
    pack_ref[local : local + 16, :] = rows.astype(bf16)
    for copy in copies:
        copy.wait()


def feed(r, low_ref, wi_v, b_in, act_v, slope_v):
    for first in range(0, wi_v.shape[2], TILE):
        cols = slice(first, first + TILE)
        before = product(low_ref[...], wi_v[r, :, cols]) + b_in[:, cols]
        active, slope = gelu_and_slope(before)
        act_v[r, :, cols] = active.astype(bf16)
        slope_v[r, :, cols] = slope.astype(bf16)


def middle_first(
    m_ref, tok_hbm, bias_ref, gain_ref, shift_ref, c0, c1, c2, c3, wo0, wo1, wo2, wo3, wi0, wi1, wb0, wb1,
    act_hbm, slope_hbm, xhat1_ref, rstd1_ref, low1_ref, total_ref,
    tok_v, ctx_v, wo_v, wi_v, wb_v, act_v, slope_v, sems, out_sems,
):
    length, width = tok_v.shape
    local = ctx_v.shape[2]
    b_out, gain1, shift1 = row_of(bias_ref), row_of(gain_ref), row_of(shift_ref)
    at = pl.multiple_of(m_ref[0] * length, length)
    copies = start_all(
        [(tok_hbm.at[pl.ds(at, length)], tok_v)]
        + [(c, ctx_v.at[r]) for r, c in enumerate((c0, c1, c2, c3))]
        + [(w, wo_v.at[r]) for r, w in enumerate((wo0, wo1, wo2, wo3))]
        + [(w, wi_v.at[r]) for r, w in enumerate((wi0, wi1))]
        + [(w, wb_v.at[r]) for r, w in enumerate((wb0, wb1))],
        sems,
    )
    for copy in copies[:9]:
        copy.wait()
    for first in range(0, width, TILE):
        cols = slice(first, first + TILE)
        total = tok_v[:, cols].astype(f32) + b_out[:, cols]
        for r in range(4):
            total = total + product(ctx_v[r], wo_v[r, 0:local, cols])
        total_ref[:, cols] = total

    @pl.loop(0, length // ROW_TILE)
    def _(i):
        rows = pl.ds(pl.multiple_of(i * ROW_TILE, ROW_TILE), ROW_TILE)
        values = total_ref[rows, :]
        center = values - jnp.mean(values, axis=-1, keepdims=True)
        rate = lax.rsqrt(jnp.mean(center * center, axis=-1, keepdims=True) + norm_eps)
        xhat = center * rate
        xhat1_ref[rows, :] = xhat.astype(bf16)
        rstd1_ref[rows, :] = jnp.broadcast_to(rate, (ROW_TILE, LANES))
        normed = xhat * gain1 + shift1
        total_ref[rows, :] = normed
        low1_ref[rows, :] = normed.astype(bf16)

    outs = []
    for r in range(2):
        copies[9 + r].wait()
        b_in = jnp.sum(wo_v[r, local : local + 16, :].astype(f32), axis=0, keepdims=True)
        feed(r, low1_ref, wi_v, b_in, act_v, slope_v)
        outs += start_all(
            [(act_v.at[r], act_hbm.at[r]), (slope_v.at[r], slope_hbm.at[r])],
            out_sems.at[pl.ds(2 * r, 2)],
        )
    for copy in copies[11:]:
        copy.wait()
    for first in range(0, width, TILE):
        cols = slice(first, first + TILE)
        total_ref[:, cols] += product(act_v[0], wb_v[0, :, cols]) + product(act_v[1], wb_v[1, :, cols])
    for copy in outs:
        copy.wait()


def middle_second(
    seg_ref, pair_ref, bias_ref, gain_ref, shift_ref, low1_ref, total_hbm, wo2, wo3, wi2, wi3, wb2, wb3,
    act_hbm, slope_hbm, xhat2_ref, rstd2_ref, out_ref, pooled_ref, len_ref, msg_ref,
    wi_v, wb_v, act_v, slope_v, resid, sems, out_sems,
):
    length, width = resid.shape
    local = wo2.shape[0] - 16
    b_back, gain2, shift2 = row_of(bias_ref), row_of(gain_ref), row_of(shift_ref)
    copies = start_all(
        [(w, wi_v.at[r]) for r, w in enumerate((wi2, wi3))]
        + [(total_hbm, resid)]
        + [(w, wb_v.at[r]) for r, w in enumerate((wb2, wb3))],
        sems,
    )
    outs = []
    for r in range(2):
        copies[r].wait()
        b_in = jnp.sum((wo2, wo3)[r][local : local + 16, :].astype(f32), axis=0, keepdims=True)
        feed(r, low1_ref, wi_v, b_in, act_v, slope_v)
        outs += start_all(
            [(act_v.at[r], act_hbm.at[r]), (slope_v.at[r], slope_hbm.at[r])],
            out_sems.at[pl.ds(2 * r, 2)],
        )
    for copy in copies[2:]:
        copy.wait()
    for first in range(0, width, TILE):
        cols = slice(first, first + TILE)
        total = resid[:, cols] + b_back[:, cols]
        resid[:, cols] = total + product(act_v[0], wb_v[0, :, cols]) + product(act_v[1], wb_v[1, :, cols])

    @pl.loop(0, length // ROW_TILE)
    def _(i):
        rows = pl.ds(pl.multiple_of(i * ROW_TILE, ROW_TILE), ROW_TILE)
        values = resid[rows, :]
        center = values - jnp.mean(values, axis=-1, keepdims=True)
        rate = lax.rsqrt(jnp.mean(center * center, axis=-1, keepdims=True) + norm_eps)
        xhat = center * rate
        xhat2_ref[rows, :] = xhat.astype(bf16)
        rstd2_ref[rows, :] = jnp.broadcast_to(rate, (ROW_TILE, LANES))
        out_ref[rows, :] = (xhat * gain2 + shift2).astype(bf16)

    own = members(seg_ref)
    sums = product(own.astype(bf16), out_ref[...])
    count = jnp.sum(own, axis=-1, keepdims=True)
    pooled = sums / count
    rate = lax.rsqrt(jnp.sum(pooled * pooled, axis=-1, keepdims=True) + norm_eps)
    unit = (pooled * rate).astype(bf16)
    pooled_ref[...] = pooled
    len_ref[...] = jnp.broadcast_to(count, len_ref.shape)
    half = unit.astype(f32)
    msg_ref[:, 0:width] = half[0:8].astype(bf16)
    msg_ref[:, width : 2 * width] = half[8:16].astype(bf16)
    msg_ref[:, 2 * width :] = pair_ref[...].astype(bf16)
    for copy in outs:
        copy.wait()


def members(seg_ref):
    slot = lax.broadcasted_iota(jnp.int32, (16, 1), 0)
    segment = jnp.where(slot < 8, 2 * slot, 2 * slot - 15)
    return (seg_ref[...] == segment).astype(f32)


def contrast(ids_ref, all_ref, own_ref, pooled_ref, len_ref, loss_ref, grad_ref, log_v):
    width = pooled_ref.shape[1]
    count = all_ref.shape[0]
    block = min(count, 256)
    passages = all_ref[:, width : 2 * width]
    number = lax.broadcasted_iota(jnp.int32, (1, count), 1).astype(f32)

    def target(rows):
        coded = rows[:, 2 * width :].astype(f32)
        return coded[:, 0:1] * 64.0 + coded[:, 1:2]

    def statistics(rows, scores):
        best = jnp.max(scores, axis=-1, keepdims=True)
        log_total = best + jnp.log(jnp.sum(jnp.exp(scores - best), axis=-1, keepdims=True))
        return log_total, (number == target(rows)).astype(f32)

    def one_block(i, total):
        rows_at = pl.ds(pl.multiple_of(i * block, block), block)
        rows = all_ref[rows_at, :]
        scores = product_nt(rows[:, 0:width], passages) * inv_temp
        log_total, positive = statistics(rows, scores)
        log_v[rows_at, :] = jnp.broadcast_to(log_total, (block, LANES))
        return total + jnp.sum(log_total - jnp.sum(scores * positive, axis=-1, keepdims=True), keepdims=True)

    total = lax.fori_loop(0, count // block, one_block, jnp.zeros((1, 1), f32))
    loss_ref[...] = jnp.broadcast_to(total * (1.0 / count), loss_ref.shape)
    own = own_ref[...]
    scores = product_nt(own[:, 0:width], passages) * inv_temp
    log_total, positive = statistics(own, scores)
    grad_low = ((jnp.exp(scores - log_total) - positive) * (loss_scale * inv_temp)).astype(bf16)
    grad_query = product(grad_low, passages)

    everyone = all_ref[...]
    queries = everyone[:, 0:width]
    passage = jnp.concatenate(
        [own[:, width : 2 * width].astype(f32), jnp.zeros((LANES - 8, width), f32)], axis=0
    ).astype(bf16)
    lane = lax.broadcasted_iota(jnp.int32, (1, LANES), 1)
    scores = product_nt(queries, passage) * inv_temp
    number = jnp.where(lane < 8, ids_ref[0] * 8 + lane, -1).astype(f32)
    positive = (number == target(everyone)).astype(f32)
    weight = jnp.exp(scores - log_v[...]) - positive
    grad_low = (jnp.where(lane < 8, weight, 0.0) * (loss_scale * inv_temp)).astype(bf16)
    grad_passage = product_t(grad_low, queries)[0:8]

    grad_unit = jnp.concatenate([grad_query, grad_passage], axis=0)
    pooled = pooled_ref[...]
    rate = lax.rsqrt(jnp.sum(pooled * pooled, axis=-1, keepdims=True) + norm_eps)
    inner = jnp.sum(pooled * grad_unit, axis=-1, keepdims=True)
    grad = rate * grad_unit - rate * rate * rate * pooled * inner
    grad_ref[...] = grad / len_ref[:, 0:1]


def column_total(values):
    return jnp.sum(values.reshape(values.shape[0] // 8, 8, values.shape[1]), axis=0)


def back_second(
    gp_ref, seg_ref, xhat_ref, rstd_ref, gain_ref, act01_hbm, act23_hbm,
    low_ref, vec_ref, d_ref,
    out_v, act_v, sums, sems,
):
    length, width = xhat_ref.shape
    gain = row_of(gain_ref)
    copies = start_all([(act23_hbm.at[1], act_v.at[0]), (act01_hbm.at[1], act_v.at[1])], sems)
    own = members(seg_ref).astype(bf16)
    top = gp_ref[...].astype(bf16)
    rest = (gp_ref[...] - top.astype(f32)).astype(bf16)
    out_v[...] = product_t(own, top) + product_t(own, rest)
    sums[...] = jnp.zeros_like(sums)

    @pl.loop(0, length // ROW_TILE)
    def _(i):
        rows = pl.ds(pl.multiple_of(i * ROW_TILE, ROW_TILE), ROW_TILE)
        grad_out, xhat = out_v[rows, :], xhat_ref[rows, :].astype(f32)
        sums[0] += column_total(grad_out * xhat)
        sums[1] += column_total(grad_out)
        grad = grad_out * gain
        first = jnp.mean(grad, axis=-1, keepdims=True)
        second = jnp.mean(grad * xhat, axis=-1, keepdims=True)
        grad = (grad - first - xhat * second) * rstd_ref[rows, 0:1]
        sums[2] += column_total(grad)
        low_ref[rows, :] = grad.astype(bf16)

    vec_ref[...] = jnp.zeros_like(vec_ref)
    for i in range(3):
        vec_ref[i : i + 1, :] = jnp.sum(sums[i], axis=0, keepdims=True)
    back_products(copies, act_v, low_ref, d_ref)


def back_products(copies, act_v, low_ref, d_ref):
    for i, copy in enumerate(copies):
        copy.wait()
        for first in range(0, act_v.shape[2], TILE):
            cols = slice(first, first + TILE)
            d_ref[i, cols, :] = product_t(act_v[i, :, cols], low_ref[...]).astype(bf16)


def back_outer(low_ref, act01_hbm, act23_hbm, d_ref, act_v, sems):
    copies = start_all([(act23_hbm.at[0], act_v.at[0]), (act01_hbm.at[0], act_v.at[1])], sems)
    back_products(copies, act_v, low_ref, d_ref)


def back_first(
    low_ref, xhat_ref, rstd_ref, gain_ref, slope01_hbm, slope23_hbm,
    wo0, wo1, wo2, wo3, wi0, wi1, wi2, wi3, wb0, wb1, wb2, wb3,
    gb_hbm, attn_ref, vec_ref, bin_ref, x0, x1, x2, x3,
    slope_v, wo_v, wi_v, wb_v, gb_v, total_v, sums, sems, out_sems,
):
    length, width = xhat_ref.shape
    units = wi_v.shape[2]
    gain = row_of(gain_ref)
    copies = start_all(
        [p for r, w in enumerate((wb0, wb1, wb2, wb3)) for p in ((w, wb_v.at[r]), ((slope01_hbm, slope23_hbm)[r // 2].at[r % 2], slope_v.at[r]))]
        + [(w, wi_v.at[r]) for r, w in enumerate((wi0, wi1, wi2, wi3))]
        + [(w, wo_v.at[r]) for r, w in enumerate((wo0, wo1, wo2, wo3))],
        sems,
    )
    outs = []
    for r in range(4):
        copies[2 * r].wait()
        copies[2 * r + 1].wait()
        for first in range(0, units, TILE):
            cols = slice(first, first + TILE)
            grad = product_nt(low_ref[...], wb_v[r, cols, :])
            low = (grad * slope_v[r, :, cols].astype(f32)).astype(bf16)
            gb_v[r, :, cols] = low
            bin_ref[r : r + 1, cols] = jnp.sum(column_total(low.astype(f32)), axis=0, keepdims=True)
        outs += start_all([(gb_v.at[r], gb_hbm.at[r])], out_sems.at[pl.ds(r, 1)])
    for copy in copies[8:]:
        copy.wait()
    for first in range(0, width, TILE):
        cols = slice(first, first + TILE)
        total = low_ref[:, cols].astype(f32)
        for r in range(4):
            total = total + product_nt(gb_v[r], wi_v[r, cols, :])
        total_v[:, cols] = total
    sums[...] = jnp.zeros_like(sums)

    @pl.loop(0, length // ROW_TILE)
    def _(i):
        rows = pl.ds(pl.multiple_of(i * ROW_TILE, ROW_TILE), ROW_TILE)
        grad_out, xhat = total_v[rows, :], xhat_ref[rows, :].astype(f32)
        sums[0] += column_total(grad_out * xhat)
        sums[1] += column_total(grad_out)
        grad = grad_out * gain
        first = jnp.mean(grad, axis=-1, keepdims=True)
        second = jnp.mean(grad * xhat, axis=-1, keepdims=True)
        grad = (grad - first - xhat * second) * rstd_ref[rows, 0:1]
        sums[2] += column_total(grad)
        attn_ref[rows, :] = grad.astype(bf16)

    vec_ref[...] = jnp.zeros_like(vec_ref)
    for i in range(3):
        vec_ref[i : i + 1, :] = jnp.sum(sums[i], axis=0, keepdims=True)
    for r, x_ref in enumerate((x0, x1, x2, x3)):
        x_ref[...] = product_nt(attn_ref[...], wo_v[r, 0 : x_ref.shape[1], :]).astype(bf16)
    for copy in outs:
        copy.wait()


def weight_grads(
    pieces, low1_ref, attn_ref, vec1_ref, vec2_ref, bin_ref, ca, cb, gb_hbm,
    d_ref,
    gb_v, sems,
):
    length, width = low1_ref.shape
    units = gb_v.shape[2]
    local = ca.shape[1]
    copies = start_all([(gb_hbm.at[r], gb_v.at[i]) for i, r in enumerate(pieces)], sems)
    for i, (r, c_ref) in enumerate(zip(pieces, (ca, cb))):
        copies[i].wait()
        for first in range(0, width, TILE):
            cols = slice(first, first + TILE)
            d_ref[i, cols, :] = product_t(low1_ref[:, cols], gb_v[i]).astype(bf16)
        d_ref[i, width : width + local, :] = product_t(c_ref[...], attn_ref[...]).astype(bf16)
        rows = jnp.concatenate(
            [vec1_ref[0:3, :], vec2_ref[0:3, :], bin_ref[r : r + 1, :], jnp.zeros((1, units), f32)],
            axis=0,
        )
        top = rows.astype(bf16)
        rest = (rows - top.astype(f32)).astype(bf16)
        at = width + local
        d_ref[i, at : at + 16, :] = jnp.concatenate([top, rest], axis=0)
        d_ref[i, at + 16 : at + VEC_ROWS, :] = jnp.zeros((VEC_ROWS - 16, units), bf16)


def hop(array, axis, flip):
    size = lax.axis_size(axis)
    return lax.ppermute(array, axis, [(i, i ^ flip) for i in range(size)])


def bit_of(axis, flip):
    return (lax.axis_index(axis) // flip) % 2


def ordered(bit, mine, other, axis):
    low_first = jnp.concatenate([mine, other], axis=axis)
    high_first = jnp.concatenate([other, mine], axis=axis)
    return jnp.where(bit == 0, low_first, high_first)


def bits_below(size):
    flips, flip = [], 1
    while flip < size:
        flips.append(flip)
        flip *= 2
    return flips


def together(*arrays):
    return lax.optimization_barrier(arrays)


def late(array, *earlier):
    return lax.optimization_barrier((array, *earlier))[0]


def gather_parts(mine, first=None):
    near = hop(mine, "mp", 1)
    far = hop(mine, "mp", 2) if first is None else first
    return [mine, near, far, hop(far, "mp", 1)]


def join(part, flip):
    return ordered(bit_of("dp", flip), part, hop(part, "dp", flip), 0)


def add_low(left_side, right_side):
    return (left_side.astype(f32) + right_side.astype(f32)).astype(bf16)


class Rows:
    def __init__(self):
        self.dp, self.mp = lax.axis_size("dp"), lax.axis_size("mp")
        flips = bits_below(self.dp)
        self.orders = flips, flips[1:2] + flips[:1] + flips[2:]
        self.steps = len(flips)

    def swap(self, values, step):
        pairs = [
            (i, ((i // self.mp) ^ self.orders[i % self.mp % 2][step]) * self.mp + i % self.mp)
            for i in range(self.dp * self.mp)
        ]
        return lax.ppermute(values, ("dp", "mp"), pairs)

    def bit(self, step):
        even, odd = (bit_of("dp", order[step]) for order in self.orders)
        return jnp.where(lax.axis_index("mp") % 2 == 1, odd, even)

    def send(self, array, step):
        half = array.shape[-2] // 2
        away = lax.dynamic_slice_in_dim(array, (1 - self.bit(step)) * half, half, axis=-2)
        return self.swap(away, step)

    def keep(self, array, got, step):
        half = array.shape[-2] // 2
        return add_low(lax.dynamic_slice_in_dim(array, self.bit(step) * half, half, axis=-2), got)

    def join(self, array, got, step):
        return ordered(self.bit(step), array, got, array.ndim - 2)

    def gather(self, array, last):
        for step in reversed(range(last)):
            array = self.join(array, self.swap(array, step), step)
        return array

    def total(self, array):
        last = self.steps - 1
        for step in range(last):
            array = self.keep(array, self.send(array, step), step)
        array = add_low(array, self.swap(array, last))
        return self.gather(array, last)


class Running:
    def __init__(self, rows, array, plan):
        self.rows, self.array, self.plan = rows, array, plan

    def start(self):
        kind, step = self.plan[0]
        return self.rows.send(self.array, step) if kind == "send" else self.rows.swap(self.array, step)

    def finish(self, got):
        kind, step = self.plan.pop(0)
        if kind == "send":
            self.array = self.rows.keep(self.array, got, step)
        elif kind == "full":
            self.array = add_low(self.array, got)
        else:
            self.array = self.rows.join(self.array, got, step)


def params(cost=None, **more):
    return dict(
        compiler_params=pltpu.CompilerParams(vmem_limit_bytes=VMEM_BYTES, **more), cost_estimate=cost
    )


def cost(flops, moved, exps=0):
    return pl.CostEstimate(flops=int(flops), bytes_accessed=int(moved), transcendentals=int(exps))


def shape(dims, dtype=bf16):
    return jax.ShapeDtypeStruct(dims, dtype)


def shards(
    tokens, w_qkv, b_qv, w_out, b_out, norm1_gain, norm1_shift, w_in, b_in, w_back, b_back,
    norm2_gain, norm2_shift, segment_ids, pair_ids,
):
    row_count, length = segment_ids.shape
    width = tokens.shape[1]
    local = w_out.shape[0]
    units = w_in.shape[1]
    heads = local // HEAD_DIM
    blocks = length // Q_BLOCK
    member = lax.axis_index("mp")
    own_row = lax.axis_index("dp") * row_count + member
    m_arr = member.astype(jnp.int32).reshape(1)
    any_spec = pl.BlockSpec(memory_space=pl.ANY)
    vmem_spec = pl.BlockSpec(memory_space=pltpu.VMEM)
    smem_spec = pl.BlockSpec(memory_space=pltpu.SMEM)
    dma = pltpu.SemaphoreType.DMA

    tall = lambda vector: vector.reshape(-1, LANES)
    bit_x, bit_z = bit_of("dp", 1), bit_of("dp", 2)
    bits = jnp.stack([2 * bit_x + bit_z, 2 * bit_z + bit_x]).astype(jnp.int32)
    out_pack, in_quarter, back_quarter = pl.pallas_call(
        prepare,
        in_specs=[smem_spec] + [vmem_spec] * 2 + [any_spec] * 2,
        out_specs=[vmem_spec] * 3,
        out_shape=[
            shape((local + 16, width)), shape((width // 4, units)), shape((units // 4, width)),
        ],
        scratch_shapes=[dma((2,))],
        name="prepare",
        **params(cost(1e6, 2e6)),
    )(bits, tall(b_in), w_out, w_in, w_back)
    near_in, near_back = hop(w_in, "mp", 1), hop(w_back, "mp", 1)
    near_out = hop(out_pack, "mp", 1)
    far_out = hop(out_pack, "mp", 2)
    b_qv, near_in, near_back, near_out = together(b_qv, near_in, near_back, near_out)
    in_quarter = hop(in_quarter, "mp", 2)
    back_quarter = hop(back_quarter, "mp", 2)
    w_t = jnp.swapaxes(w_qkv, 1, 2)

    windows = jnp.stack(
        [segment_ids[:, window_start(i, length) :][:, :K_WINDOW] for i in range(blocks)], axis=1
    )
    seg_rows = segment_ids[:, None, :]

    def attend(count, source, place, held):
        return pl.pallas_call(
            functools.partial(attend_forward, len(held)),
            grid_spec=pltpu.PrefetchScalarGridSpec(
                num_scalar_prefetch=1,
                grid=(count,),
                in_specs=[
                    pl.BlockSpec((length, width), lambda i, m: (source(i) ^ m[0], 0)),
                    pl.BlockSpec(w_t.shape, lambda i, m: (0, 0, 0)),
                    pl.BlockSpec(b_qv.shape, lambda i, m: (0, 0)),
                    pl.BlockSpec((1, 1, length), lambda i, m: (source(i) ^ m[0], 0, 0)),
                    pl.BlockSpec((1, blocks, K_WINDOW), lambda i, m: (source(i) ^ m[0], 0, 0)),
                ]
                + [any_spec] * len(held),
                out_specs=[
                    pl.BlockSpec((1, 3, length, local), lambda i, m: (place + i, 0, 0, 0)),
                    pl.BlockSpec(
                        (1, heads * blocks, Q_BLOCK, K_WINDOW), lambda i, m: (place + i, 0, 0, 0)
                    ),
                ]
                + [pl.BlockSpec((length, local), lambda i, m: (0, 0))] * count,
                scratch_shapes=[pltpu.VMEM((length, local), bf16)],
            ),
            out_shape=[
                shape((row_count, 3, length, local)),
                shape((row_count, heads * blocks, Q_BLOCK, K_WINDOW)),
                *[shape((length, local))] * count,
            ],
            input_output_aliases={6 + i: i for i in range(len(held))},
            name="attend_forward",
            **params(cost(6 * count * length * width * local, 2e6 * count, count * heads * length * K_WINDOW)),
        )(m_arr, tokens, w_t, b_qv, seg_rows, windows, *held)

    qkv, probs, ctx3, ctx2, ctx1 = attend(3, lambda i: 3 - i, 0, ())
    ctx3, ctx2, ctx1, in_quarter, back_quarter, far_out = together(
        ctx3, ctx2, ctx1, in_quarter, back_quarter, far_out
    )
    in_got, back_got = hop(in_quarter, "dp", 2), hop(back_quarter, "dp", 1)
    qkv, probs, ctx0 = attend(1, lambda i: 0, 3, (qkv, probs))
    out_parts = [out_pack, near_out, far_out, hop(late(far_out, ctx0), "mp", 1)]
    ctx_got2, ctx_got3 = hop(ctx2, "mp", 2), hop(ctx3, "mp", 3)
    in_half = ordered(bit_z, in_quarter, late(in_got, ctx0), 0)
    back_half = ordered(bit_x, back_quarter, late(back_got, ctx0), 0)
    in_half, back_half, ctx_got2, ctx_got3 = together(in_half, back_half, ctx_got2, ctx_got3)
    ctx_parts = [ctx0, hop(ctx1, "mp", 1), ctx_got2, ctx_got3]
    seg_own = lax.dynamic_slice_in_dim(segment_ids, member, 1)
    pair_own = lax.dynamic_slice_in_dim(pair_ids, member, 1).reshape(-1, 1)
    pair_code = jnp.concatenate(
        [pair_own // 64, pair_own % 64, jnp.zeros((pair_own.shape[0], LANES - 2), jnp.int32)], axis=1
    ).astype(f32)
    in_got, back_got = hop(in_half, "dp", 1), hop(back_half, "dp", 2)
    act01, slope01, xhat1, rstd1, low1, total = pl.pallas_call(
        middle_first,
        in_specs=[smem_spec, any_spec] + [vmem_spec] * 3 + [any_spec] * 12,
        out_specs=[any_spec] * 2 + [vmem_spec] * 4,
        out_shape=[
            shape((2, length, units)), shape((2, length, units)),
            shape((length, width)), shape((length, LANES), f32), shape((length, width)),
            shape((length, width), f32),
        ],
        scratch_shapes=[
            pltpu.VMEM((length, width), bf16), pltpu.VMEM((4, length, local), bf16),
            pltpu.VMEM((4, local + 16, width), bf16), pltpu.VMEM((2, width, units), bf16),
            pltpu.VMEM((2, units, width), bf16), pltpu.VMEM((2, length, units), bf16),
            pltpu.VMEM((2, length, units), bf16), dma((13,)), dma((4,)),
        ],
        name="middle_first",
        **params(cost(2 * length * width * (width + 4 * units), 18e6, 2 * length * units)),
    )(
        m_arr, tokens, tall(b_out), tall(norm1_gain), tall(norm1_shift), *ctx_parts, *out_parts,
        w_in, near_in, w_back, near_back,
    )
    in_far = ordered(bit_x, in_half, late(in_got, total), 0)
    back_far = ordered(bit_z, back_half, late(back_got, total), 0)
    in_parts = [w_in, near_in, in_far, hop(in_far, "mp", 1)]
    back_parts = [w_back, near_back, back_far, hop(back_far, "mp", 1)]
    act23, slope23, xhat2, rstd2, out_own, pooled, lengths, msg = pl.pallas_call(
        middle_second,
        in_specs=[vmem_spec] * 6 + [any_spec] + [vmem_spec] * 2 + [any_spec] * 4,
        out_specs=[any_spec] * 2 + [vmem_spec] * 6,
        out_shape=[
            shape((2, length, units)), shape((2, length, units)),
            shape((length, width)), shape((length, LANES), f32), shape((length, width)),
            shape((16, width), f32), shape((16, LANES), f32), shape((8, 2 * width + LANES)),
        ],
        scratch_shapes=[
            pltpu.VMEM((2, width, units), bf16), pltpu.VMEM((2, units, width), bf16),
            pltpu.VMEM((2, length, units), bf16), pltpu.VMEM((2, length, units), bf16),
            pltpu.VMEM((length, width), f32), dma((5,)), dma((4,)),
        ],
        name="middle_second",
        **params(cost(8 * length * width * units, 12e6, 2 * length * units)),
    )(
        seg_own, pair_code, tall(b_back), tall(norm2_gain), tall(norm2_shift), low1, total,
        *out_parts[2:], *in_parts[2:], *back_parts[2:],
    )

    everyone = msg[None]
    steps = [("dp", flip) for flip in reversed(bits_below(lax.axis_size("dp")))]
    steps += [("mp", flip) for flip in reversed(bits_below(lax.axis_size("mp")))]
    while len(steps) > 1:
        everyone = four_ways(everyone, *steps[:2])
        steps = steps[2:]
    if steps:
        everyone = both_ways(everyone, hop(everyone, *steps[0]), *steps[0])
    everyone = everyone.reshape(-1, msg.shape[1])

    loss, grad_pooled = pl.pallas_call(
        contrast,
        in_specs=[smem_spec] + [vmem_spec] * 4,
        out_specs=[vmem_spec] * 2,
        out_shape=[shape((8, LANES), f32), shape((16, width), f32)],
        scratch_shapes=[pltpu.VMEM((everyone.shape[0], LANES), f32)],
        name="contrast",
        **params(cost(4e8, 2e6, 1e5)),
    )(own_row.astype(jnp.int32).reshape(1), everyone, msg, pooled, lengths)

    rows = Rows()
    grad_low2, vec2, back_send = pl.pallas_call(
        back_second,
        in_specs=[vmem_spec] * 5 + [any_spec] * 2,
        out_specs=[vmem_spec] * 3,
        out_shape=[
            shape((length, width)), shape((8, width), f32),
            shape((2, units, width)),
        ],
        scratch_shapes=[
            pltpu.VMEM((length, width), f32), pltpu.VMEM((2, length, units), bf16),
            pltpu.VMEM((3, 8, width), f32), dma((2,)),
        ],
        name="back_second",
        **params(cost(4 * length * width * units, 14e6)),
    )(grad_pooled, seg_own, xhat2, rstd2, tall(norm2_gain), act01, act23)
    back_got = hop(back_send, "mp", 1)
    back_keep = pl.pallas_call(
        back_outer,
        in_specs=[vmem_spec] + [any_spec] * 2,
        out_specs=vmem_spec,
        out_shape=shape((2, units, width)),
        scratch_shapes=[pltpu.VMEM((2, length, units), bf16), dma((2,))],
        name="back_outer",
        **params(cost(4 * length * width * units, 8e6)),
    )(grad_low2, act01, act23)
    back_sum = add_low(back_keep, back_got)
    grad_low2, back_sum = together(grad_low2, back_sum)
    back_got = rows.send(back_sum, 0)
    out_far = hop(late(out_own, grad_low2), "mp", 2)

    gb, attn_low, vec1, d_bin, *ctx_grads = pl.pallas_call(
        back_first,
        in_specs=[vmem_spec] * 4 + [any_spec] * 14,
        out_specs=[any_spec] + [vmem_spec] * 7,
        out_shape=[
            shape((4, length, units)), shape((length, width)),
            shape((8, width), f32), shape((4, units), f32), *[shape((length, local))] * 4,
        ],
        scratch_shapes=[
            pltpu.VMEM((4, length, units), bf16), pltpu.VMEM((4, local + 16, width), bf16),
            pltpu.VMEM((4, width, units), bf16), pltpu.VMEM((4, units, width), bf16),
            pltpu.VMEM((4, length, units), bf16), pltpu.VMEM((length, width), f32),
            pltpu.VMEM((3, 8, width), f32), dma((16,)), dma((4,)),
        ],
        name="back_first",
        **params(cost(2 * length * width * (width + 8 * units), 25e6)),
    )(
        grad_low2, xhat1, rstd1, tall(norm1_gain), slope01, slope23, *out_parts, *in_parts, *back_parts,
    )

    attn_low, back_got, out_far = together(attn_low, back_got, out_far)
    out_pair = ordered(bit_of("mp", 2), out_own[None], out_far[None], 0)
    back_sum = rows.keep(back_sum, back_got, 0)
    got3 = hop(ctx_grads[3], "mp", 3)

    def first_grads(pieces, low):
        return pl.pallas_call(
            functools.partial(weight_grads, pieces),
            in_specs=[vmem_spec] * 7 + [any_spec],
            out_specs=vmem_spec,
            out_shape=shape((2, width + local + VEC_ROWS, units)),
            scratch_shapes=[pltpu.VMEM((2, length, units), bf16), dma((2,))],
            name="weight_grads",
            **params(cost(4 * length * width * (units + local), 7e6)),
        )(low1, low, vec1, vec2, d_bin, ctx_parts[pieces[0]], ctx_parts[pieces[1]], gb)

    first_send = first_grads((3, 1), attn_low)
    got3, attn_low, first_send, out_pair = together(got3, attn_low, first_send, out_pair)
    out_other = hop(out_pair, "mp", 1)
    first_got = hop(first_send, "mp", 1)
    got2 = hop(late(ctx_grads[2], first_send), "mp", 2)
    back_sum = late(back_sum, first_send)
    back_got = rows.send(back_sum, 1)
    first_keep = first_grads((2, 0), attn_low)
    own_grad, first_keep, first_got, got2, back_got, out_other = together(
        ctx_grads[0], first_keep, first_got, got2, back_got, out_other
    )
    back_sum = rows.keep(back_sum, back_got, 1)
    first_far = hop(add_low(first_keep[0], first_got[0]), "mp", 2)
    back_got = rows.send(back_sum, 2)
    got1 = hop(late(ctx_grads[1], own_grad), "mp", 1)

    def attend_back(count, source, place, last, grads, sums):
        same = lambda i, m: (0, 0)
        out_specs = [pl.BlockSpec((length, width), same)] * count
        out_shape = [shape((length, width))] * count
        if last:
            out_specs.append(pl.BlockSpec((3 * local + VEC_ROWS, width), same))
            out_shape.append(shape((3 * local + VEC_ROWS, width)))
        else:
            out_specs += [pl.BlockSpec((3 * local, width), same), pl.BlockSpec((8, local), same)]
            out_shape += [shape((3 * local, width), f32), shape((8, local), f32)]
        return pl.pallas_call(
            functools.partial(attend_backward, count, len(sums) == 0, last),
            grid_spec=pltpu.PrefetchScalarGridSpec(
                num_scalar_prefetch=1,
                grid=(count,),
                in_specs=[
                    pl.BlockSpec((length, width), lambda i, m: (source(i) ^ m[0], 0)),
                    pl.BlockSpec(w_t.shape, lambda i, m: (0, 0, 0)),
                    pl.BlockSpec((1, 3, length, local), lambda i, m: ((place + i) % row_count, 0, 0, 0)),
                    pl.BlockSpec(
                        (1, heads * blocks, Q_BLOCK, K_WINDOW), lambda i, m: ((place + i) % row_count, 0, 0, 0)
                    ),
                ]
                + [pl.BlockSpec((length, local), same)] * count
                + [pl.BlockSpec(part.shape, same) for part in sums],
                out_specs=out_specs,
                scratch_shapes=[
                    pltpu.VMEM((length, local), bf16), pltpu.VMEM((length, local), f32),
                    pltpu.VMEM((length, local), f32), pltpu.VMEM((3 * local, width), f32),
                    pltpu.VMEM((8, local), f32),
                ],
            ),
            out_shape=out_shape,
            name="attend_backward",
            **params(cost(12 * count * length * width * local, 4e6 * count)),
        )(m_arr, tokens, w_t, qkv, probs, *grads, *sums)

    back0, back3, *sums = attend_back(2, lambda i: 3 * i, 3, False, [own_grad, got3], [])
    back_got, got1, back3, *sums = together(back_got, got1, back3, *sums)
    back_sum = rows.keep(back_sum, back_got, 2)
    for step in range(3, rows.steps):
        back_sum = rows.keep(back_sum, rows.send(back_sum, step), step)
    back_got = hop(back_sum[0], "mp", 2)
    tok_got3 = hop(back3, "mp", 1)
    back2, back1, d_qkv = attend_back(2, lambda i: 2 - i, 1, True, [got2, got1], sums)
    first_far, first_keep, first_got, back_got, _ = together(
        first_far, first_keep, first_got, back_got, d_qkv
    )
    back_sum = add_low(back_sum[1], back_got)
    first_sum = (first_keep[1].astype(f32) + first_got[1].astype(f32) + first_far.astype(f32)).astype(bf16)
    last = rows.steps - 1
    tok_got1 = hop(back1, "mp", 1)
    far = add_low(back2, tok_got3)
    down = [("send", step) for step in range(last)] + [("full", last)]
    up = [("join", step) for step in reversed(range(last))]
    sums = [
        Running(rows, first_sum, down + up),
        Running(rows, d_qkv, down + up),
        Running(rows, back_sum, [("join", last)] + up),
    ]
    stage, extra = 0, [tok_got1, hop(far, "mp", 2)]
    while any(part.plan for part in sums):
        parts = [part for part in sums if part.plan and not (part is sums[2] and stage == 1)]
        if stage == 2:
            sums[2].array = late(sums[2].array, sums[0].array)
        if stage == 2:
            sums[1].array = late(sums[1].array, sums[0].array)
        starts = [part.start() for part in parts]
        if stage == 0:
            starts[2], *extra = together(starts[2], *extra)
        hops = starts + extra
        for part in parts:
            part.finish(hops.pop(0))
        if stage == 0:
            own = back0.astype(f32) + attn_low.astype(f32) + hops[0].astype(f32) + hops[1].astype(f32)
            own = own.astype(bf16)
            extra = [hop(own, "mp", 2)]
        elif stage == 1:
            tok_pair = ordered(bit_of("mp", 2), own[None], hops[0][None], 0)
            extra = [hop(tok_pair, "mp", 1)]
        elif stage == 2:
            d_tokens = rows_of_all(tok_pair, hops[0])
            extra = []
        stage += 1
    sum_first, sum_qkv, sum_back = (part.array for part in sums)
    layer_out = rows_of_all(out_pair, out_other)

    at = width + local
    vectors = sum_first[at : at + 8].astype(f32) + sum_first[at + 8 : at + 16].astype(f32)
    shares = lax.dynamic_slice_in_dim(vectors[0:6], member * local, local, axis=1)
    at = 3 * local
    d_bqv = sum_qkv[at : at + 2, 0:local].astype(f32) + sum_qkv[at + 8 : at + 10, 0:local].astype(f32)
    d_wqkv = jnp.swapaxes(sum_qkv[0:at].reshape(3, local, width), 1, 2).astype(f32)
    return (
        loss[0, 0],
        layer_out,
        d_tokens,
        d_wqkv,
        d_bqv,
        sum_first[width : width + local].astype(f32),
        shares[2],
        shares[0],
        shares[1],
        sum_first[0:width].astype(f32),
        vectors[6],
        sum_back.astype(f32),
        shares[5],
        shares[3],
        shares[4],
    )


def both_ways(array, other, axis, flip):
    low_first = jnp.stack([array, other], axis=1)
    high_first = jnp.stack([other, array], axis=1)
    joined = jnp.where(bit_of(axis, flip) == 0, low_first, high_first)
    return joined.reshape(-1, *array.shape[1:])


def four_ways(array, first, second):
    dp, mp = lax.axis_size("dp"), lax.axis_size("mp")

    def fetch(*steps):
        flip = sum(step * (mp if axis == "dp" else 1) for axis, step in steps)
        return lax.ppermute(array, ("dp", "mp"), [(i, i ^ flip) for i in range(dp * mp)])

    far, near, corner = fetch(first), fetch(second), fetch(first, second)
    count = array.shape[0]
    mine = both_ways(array, near, *second).reshape(count, 2, *array.shape[1:])
    theirs = both_ways(far, corner, *second).reshape(count, 2, *array.shape[1:])
    return both_ways(mine, theirs, *first).reshape(-1, *array.shape[1:])


def rows_of_all(pair, other):
    low_first = jnp.stack([pair, other], axis=1)
    high_first = jnp.stack([other, pair], axis=1)
    joined = jnp.where(bit_of("mp", 1) == 0, low_first, high_first)
    return joined.reshape(-1, pair.shape[-1])


def solution(mesh):
    return jax.shard_map(
        shards,
        mesh=mesh,
        in_specs=(
            P("dp", None),
            P(None, None, "mp"),
            P(None, "mp"),
            P("mp", None),
            P(),
            P(),
            P(),
            P(None, "mp"),
            P("mp"),
            P("mp", None),
            P(),
            P(),
            P(),
            P("dp", None),
            P("dp", None),
        ),
        out_specs=(
            P(),
            P("dp", None),
            P("dp", None),
            P(None, None, "mp"),
            P(None, "mp"),
            P("mp", None),
            P("mp"),
            P("mp"),
            P("mp"),
            P(None, "mp"),
            P("mp"),
            P("mp", None),
            P("mp"),
            P("mp"),
            P("mp"),
        ),
        check_vma=False,
    )
```

```python
import functools

import jax
import jax.numpy as jnp
from jax import lax
from jax.experimental import pallas as pl
from jax.experimental.pallas import tpu as pltpu
from jax.sharding import PartitionSpec as P

HEAD_DIM = 64
Q_BLOCK = 128
K_WINDOW = 256
LANES = 128
TILE = 256
ROW_TILE = 64
VEC_ROWS = 64
VMEM_BYTES = 52 * 1024 * 1024

norm_eps = 1e-06
inv_temp = 50.0
loss_scale = 8.0
masked_score = -1000000000.0

f32 = jnp.float32
bf16 = jnp.bfloat16


def product(left_side, right_side):
    return jnp.dot(left_side, right_side, preferred_element_type=f32)


def product_t(left_side, right_side):
    return lax.dot_general(
        left_side, right_side, (((0,), (0,)), ((), ())), preferred_element_type=f32
    )


def product_nt(left_side, right_side):
    return lax.dot_general(
        left_side, right_side, (((1,), (1,)), ((), ())), preferred_element_type=f32
    )


def window_start(block, length):
    return min(max(block * Q_BLOCK - HEAD_DIM, 0), length - K_WINDOW)


def gelu_and_slope(values):
    bell = jnp.exp(values * values * -0.5)
    t = 1.0 / (1.0 + (0.3275911 * 0.7071067811865476) * jnp.abs(values))
    poly = 1.061405429 * t - 1.453152027
    poly = poly * t + 1.421413741
    poly = poly * t - 0.284496736
    poly = poly * t + 0.254829592
    tail = (0.5 * t) * (poly * bell)
    phi = jnp.where(values >= 0.0, 1.0 - tail, tail)
    return values * phi, phi + (values * 0.3989422804014327) * bell


def head_lanes(pair, which):
    lane = lax.broadcasted_iota(jnp.int32, pair.shape, 1)
    keep = (lane < HEAD_DIM) if which == 0 else (lane >= HEAD_DIM)
    return jnp.where(keep, pair, jnp.zeros_like(pair))


def columns(array, first, count):
    return array[:, first : first + count]


def head_parts(array, local_width):
    parts = []
    for head in range(local_width // HEAD_DIM):
        first = head // 2 * LANES
        width = min(LANES, local_width - first)
        part = columns(array, first, width)
        parts.append(part if width < LANES else head_lanes(part, head % 2))
    return parts


def merge_heads(results, local_width):
    pieces = []
    for first in range(0, local_width, LANES):
        head = first // HEAD_DIM
        if local_width - first >= LANES:
            lane = lax.broadcasted_iota(jnp.int32, results[head].shape, 1)
            pieces.append((first, jnp.where(lane < HEAD_DIM, results[head], results[head + 1])))
        else:
            pieces.append((first, results[head]))
    return pieces


def attend_forward(held, m_ref, tok_ref, w_ref, b_ref, seg_ref, win_ref, *refs):
    qkv_ref, prob_ref, *ctx_refs, ctx_v = refs[held:]
    length = tok_ref.shape[0]
    width = w_ref.shape[1]
    heads = width // HEAD_DIM
    tok = tok_ref[...]
    q = ((product_nt(tok, w_ref[0]) + b_ref[0:1, :]).astype(bf16) * HEAD_DIM**-0.5).astype(bf16)
    k = product_nt(tok, w_ref[1]).astype(bf16)
    v = (product_nt(tok, w_ref[2]) + b_ref[1:2, :]).astype(bf16)
    qkv_ref[0, 0] = q
    qkv_ref[0, 1] = k
    qkv_ref[0, 2] = v
    q_parts = head_parts(q, width)
    slot = lax.broadcasted_iota(jnp.int32, (16, 1), 0)
    own = (seg_ref[0] == slot).astype(f32).astype(bf16)
    for block in range(length // Q_BLOCK):
        at, start = block * Q_BLOCK, window_start(block, length)
        seen = (win_ref[0, block : block + 1, :] == slot).astype(f32).astype(bf16)
        mask = (product_t(columns(own, at, Q_BLOCK), seen) - 1.0) * -masked_score
        results = []
        for head in range(heads):
            first = head // 2 * LANES
            part = min(LANES, width - first)
            key = k[start : start + K_WINDOW, first : first + part]
            value = v[start : start + K_WINDOW, first : first + part]
            scores = product_nt(q_parts[head][at : at + Q_BLOCK], key) + mask
            weights = jnp.exp(scores - jnp.max(scores, axis=-1, keepdims=True))
            low = (weights * (1.0 / jnp.sum(weights, axis=-1, keepdims=True))).astype(bf16)
            prob_ref[0, head * (length // Q_BLOCK) + block] = low
            results.append(product(low, value))
        for first, merged in merge_heads(results, width):
            ctx_v[at : at + Q_BLOCK, first : first + merged.shape[1]] = merged.astype(bf16)
    for piece, ctx_ref in enumerate(ctx_refs):

        @pl.when(pl.program_id(0) == piece)
        def _():
            ctx_ref[...] = ctx_v[...]


def attend_backward(count, first, last, m_ref, tok_ref, w_ref, qkv_ref, prob_ref, *refs):
    g_refs, refs = refs[:count], refs[count:]
    if not first:
        before_ref, vec_before_ref, *refs = refs
    o_refs, refs = refs[:count], refs[count:]
    if last:
        dw_ref, gctx, gk_sum, gv_sum, dw_sum, vec_sum = refs
    else:
        dw_ref, vec_ref, gctx, gk_sum, gv_sum, dw_sum, vec_sum = refs
    step = pl.program_id(0)
    length = tok_ref.shape[0]
    width = w_ref.shape[1]
    heads = width // HEAD_DIM
    for piece, g_ref in enumerate(g_refs):

        @pl.when(step == piece)
        def _():
            gctx[...] = g_ref[...]

    @pl.when(step == 0)
    def _():
        dw_sum[...] = jnp.zeros_like(dw_sum) if first else before_ref[...]
        vec_sum[...] = jnp.zeros_like(vec_sum) if first else vec_before_ref[...]

    gk_sum[...] = jnp.zeros_like(gk_sum)
    gv_sum[...] = jnp.zeros_like(gv_sum)
    q, k, v = qkv_ref[0, 0], qkv_ref[0, 1], qkv_ref[0, 2]
    q_parts = head_parts(q, width)
    g_parts = head_parts(gctx[...], width)
    gq_blocks = []
    for block in range(length // Q_BLOCK):
        at, start = block * Q_BLOCK, window_start(block, length)
        rows = slice(start, start + K_WINDOW)
        results, gk, gv = [], {}, {}
        for head in range(heads):
            first = head // 2 * LANES
            part = min(LANES, width - first)
            key, value = k[rows, first : first + part], v[rows, first : first + part]
            grad = g_parts[head][at : at + Q_BLOCK]
            low = prob_ref[0, head * (length // Q_BLOCK) + block]
            prob = low.astype(f32)
            grad_prob = product_nt(grad, value)
            inner = jnp.sum(prob * grad_prob, axis=-1, keepdims=True)
            grad_low = (prob * (grad_prob - inner)).astype(bf16)
            results.append(product(grad_low, key))
            gk_part = product_t(grad_low, q_parts[head][at : at + Q_BLOCK])
            gv_part = product_t(low, grad)
            gk[first] = gk[first] + gk_part if first in gk else gk_part
            gv[first] = gv[first] + gv_part if first in gv else gv_part
        for first in gk:
            lanes = slice(first, first + gk[first].shape[1])
            gk_sum[rows, lanes] += gk[first]
            gv_sum[rows, lanes] += gv[first]
        gq_blocks.append(merge_heads(results, width))
    gq = jnp.concatenate(
        [
            jnp.concatenate(
                [(blocks[i][1] * HEAD_DIM**-0.5).astype(bf16) for blocks in gq_blocks], axis=0
            )
            for i in range(len(gq_blocks[0]))
        ],
        axis=1,
    )
    gk, gv = gk_sum[...].astype(bf16), gv_sum[...].astype(bf16)
    tok = tok_ref[...]
    back = None
    for c, grad in enumerate((gq, gk, gv)):
        dw_sum[c * width : (c + 1) * width, :] += product_t(grad, tok)
        term = product(grad, w_ref[c])
        back = term if back is None else back + term
    vec_sum[0:1, :] += jnp.sum(gq.astype(f32), axis=0, keepdims=True)
    vec_sum[1:2, :] += jnp.sum(gv.astype(f32), axis=0, keepdims=True)
    back = back.astype(bf16)
    for piece, o_ref in enumerate(o_refs):

        @pl.when(step == piece)
        def _():
            o_ref[...] = back

    @pl.when(step == count - 1)
    def _():
        if not last:
            dw_ref[...] = dw_sum[...]
            vec_ref[...] = vec_sum[...]
            return
        dw_ref[0 : 3 * width, :] = dw_sum[...].astype(bf16)
        vec = vec_sum[...]
        top = vec.astype(bf16)
        rest = (vec - top.astype(f32)).astype(bf16)
        dw_ref[3 * width :, :] = jnp.zeros((VEC_ROWS, dw_ref.shape[1]), bf16)
        dw_ref[3 * width : 3 * width + 16, 0:width] = jnp.concatenate([top, rest], axis=0)


def row_of(ref):
    return jnp.concatenate([ref[i : i + 1, :] for i in range(ref.shape[0])], axis=1)


def start_all(pairs, sems):
    copies = []
    for i, (source, target) in enumerate(pairs):
        copy = pltpu.make_async_copy(source, target, sems.at[i])
        copy.start()
        copies.append(copy)
    return copies


def prepare(bits_ref, bias_ref, out_ref, in_hbm, back_hbm, pack_ref, in_ref, back_ref, sems):
    quarter = in_ref.shape[0]
    in_at = pl.multiple_of(bits_ref[0] * quarter, quarter)
    back_at = pl.multiple_of(bits_ref[1] * quarter, quarter)
    copies = start_all(
        [(in_hbm.at[pl.ds(in_at, quarter)], in_ref), (back_hbm.at[pl.ds(back_at, quarter)], back_ref)], sems
    )
    local = out_ref.shape[0]
    bias = row_of(bias_ref)
    high = bias.astype(bf16)
    rest = bias - high.astype(f32)
    middle = rest.astype(bf16)
    low = (rest - middle.astype(f32)).astype(bf16)
    slot = lax.broadcasted_iota(jnp.int32, (16, 1), 0)
    rows = jnp.where(slot == 0, high.astype(f32), 0.0)
    rows = jnp.where(slot == 1, middle.astype(f32), rows)
    rows = jnp.where(slot == 2, low.astype(f32), rows)
    pack_ref[0:local, :] = out_ref[...]
    pack_ref[local : local + 16, :] = rows.astype(bf16)
    for copy in copies:
        copy.wait()


def feed(r, low_ref, wi_v, b_in, act_v, slope_v):
    for first in range(0, wi_v.shape[2], TILE):
        cols = slice(first, first + TILE)
        before = product(low_ref[...], wi_v[r, :, cols]) + b_in[:, cols]
        active, slope = gelu_and_slope(before)
        act_v[r, :, cols] = active.astype(bf16)
        slope_v[r, :, cols] = slope.astype(bf16)


def middle_first(
    m_ref, tok_hbm, bias_ref, gain_ref, shift_ref, c0, c1, c2, c3, wo0, wo1, wo2, wo3, wi0, wi1, wb0, wb1,
    act_hbm, slope_hbm, xhat1_ref, rstd1_ref, low1_ref, total_ref,
    tok_v, ctx_v, wo_v, wi_v, wb_v, act_v, slope_v, sems, out_sems,
):
    length, width = tok_v.shape
    local = ctx_v.shape[2]
    b_out, gain1, shift1 = row_of(bias_ref), row_of(gain_ref), row_of(shift_ref)
    at = pl.multiple_of(m_ref[0] * length, length)
    copies = start_all(
        [(tok_hbm.at[pl.ds(at, length)], tok_v)]
        + [(c, ctx_v.at[r]) for r, c in enumerate((c0, c1, c2, c3))]
        + [(w, wo_v.at[r]) for r, w in enumerate((wo0, wo1, wo2, wo3))]
        + [(w, wi_v.at[r]) for r, w in enumerate((wi0, wi1))]
        + [(w, wb_v.at[r]) for r, w in enumerate((wb0, wb1))],
        sems,
    )
    for copy in copies[:9]:
        copy.wait()
    for first in range(0, width, TILE):
        cols = slice(first, first + TILE)
        total = tok_v[:, cols].astype(f32) + b_out[:, cols]
        for r in range(4):
            total = total + product(ctx_v[r], wo_v[r, 0:local, cols])
        total_ref[:, cols] = total

    @pl.loop(0, length // ROW_TILE)
    def _(i):
        rows = pl.ds(pl.multiple_of(i * ROW_TILE, ROW_TILE), ROW_TILE)
        values = total_ref[rows, :]
        center = values - jnp.mean(values, axis=-1, keepdims=True)
        rate = lax.rsqrt(jnp.mean(center * center, axis=-1, keepdims=True) + norm_eps)
        xhat = center * rate
        xhat1_ref[rows, :] = xhat.astype(bf16)
        rstd1_ref[rows, :] = jnp.broadcast_to(rate, (ROW_TILE, LANES))
        normed = xhat * gain1 + shift1
        total_ref[rows, :] = normed
        low1_ref[rows, :] = normed.astype(bf16)

    outs = []
    for r in range(2):
        copies[9 + r].wait()
        b_in = jnp.sum(wo_v[r, local : local + 16, :].astype(f32), axis=0, keepdims=True)
        feed(r, low1_ref, wi_v, b_in, act_v, slope_v)
        outs += start_all(
            [(act_v.at[r], act_hbm.at[r]), (slope_v.at[r], slope_hbm.at[r])],
            out_sems.at[pl.ds(2 * r, 2)],
        )
    for copy in copies[11:]:
        copy.wait()
    for first in range(0, width, TILE):
        cols = slice(first, first + TILE)
        total_ref[:, cols] += product(act_v[0], wb_v[0, :, cols]) + product(act_v[1], wb_v[1, :, cols])
    for copy in outs:
        copy.wait()


def middle_second(
    seg_ref, pair_ref, bias_ref, gain_ref, shift_ref, low1_ref, total_hbm, wo2, wo3, wi2, wi3, wb2, wb3,
    act_hbm, slope_hbm, xhat2_ref, rstd2_ref, out_ref, pooled_ref, len_ref, msg_ref,
    wi_v, wb_v, act_v, slope_v, resid, sems, out_sems,
):
    length, width = resid.shape
    local = wo2.shape[0] - 16
    b_back, gain2, shift2 = row_of(bias_ref), row_of(gain_ref), row_of(shift_ref)
    copies = start_all(
        [(w, wi_v.at[r]) for r, w in enumerate((wi2, wi3))]
        + [(total_hbm, resid)]
        + [(w, wb_v.at[r]) for r, w in enumerate((wb2, wb3))],
        sems,
    )
    outs = []
    for r in range(2):
        copies[r].wait()
        b_in = jnp.sum((wo2, wo3)[r][local : local + 16, :].astype(f32), axis=0, keepdims=True)
        feed(r, low1_ref, wi_v, b_in, act_v, slope_v)
        outs += start_all(
            [(act_v.at[r], act_hbm.at[r]), (slope_v.at[r], slope_hbm.at[r])],
            out_sems.at[pl.ds(2 * r, 2)],
        )
    for copy in copies[2:]:
        copy.wait()
    for first in range(0, width, TILE):
        cols = slice(first, first + TILE)
        total = resid[:, cols] + b_back[:, cols]
        resid[:, cols] = total + product(act_v[0], wb_v[0, :, cols]) + product(act_v[1], wb_v[1, :, cols])

    @pl.loop(0, length // ROW_TILE)
    def _(i):
        rows = pl.ds(pl.multiple_of(i * ROW_TILE, ROW_TILE), ROW_TILE)
        values = resid[rows, :]
        center = values - jnp.mean(values, axis=-1, keepdims=True)
        rate = lax.rsqrt(jnp.mean(center * center, axis=-1, keepdims=True) + norm_eps)
        xhat = center * rate
        xhat2_ref[rows, :] = xhat.astype(bf16)
        rstd2_ref[rows, :] = jnp.broadcast_to(rate, (ROW_TILE, LANES))
        out_ref[rows, :] = (xhat * gain2 + shift2).astype(bf16)

    own = members(seg_ref)
    sums = product(own.astype(bf16), out_ref[...])
    count = jnp.sum(own, axis=-1, keepdims=True)
    pooled = sums / count
    rate = lax.rsqrt(jnp.sum(pooled * pooled, axis=-1, keepdims=True) + norm_eps)
    unit = (pooled * rate).astype(bf16)
    pooled_ref[...] = pooled
    len_ref[...] = jnp.broadcast_to(count, len_ref.shape)
    half = unit.astype(f32)
    msg_ref[:, 0:width] = half[0:8].astype(bf16)
    msg_ref[:, width : 2 * width] = half[8:16].astype(bf16)
    msg_ref[:, 2 * width :] = pair_ref[...].astype(bf16)
    for copy in outs:
        copy.wait()


def members(seg_ref):
    slot = lax.broadcasted_iota(jnp.int32, (16, 1), 0)
    segment = jnp.where(slot < 8, 2 * slot, 2 * slot - 15)
    return (seg_ref[...] == segment).astype(f32)


def contrast(ids_ref, all_ref, own_ref, pooled_ref, len_ref, loss_ref, grad_ref, log_v):
    width = pooled_ref.shape[1]
    count = all_ref.shape[0]
    block = min(count, 256)
    passages = all_ref[:, width : 2 * width]
    number = lax.broadcasted_iota(jnp.int32, (1, count), 1).astype(f32)

    def target(rows):
        coded = rows[:, 2 * width :].astype(f32)
        return coded[:, 0:1] * 64.0 + coded[:, 1:2]

    def statistics(rows, scores):
        best = jnp.max(scores, axis=-1, keepdims=True)
        log_total = best + jnp.log(jnp.sum(jnp.exp(scores - best), axis=-1, keepdims=True))
        return log_total, (number == target(rows)).astype(f32)

    def one_block(i, total):
        rows_at = pl.ds(pl.multiple_of(i * block, block), block)
        rows = all_ref[rows_at, :]
        scores = product_nt(rows[:, 0:width], passages) * inv_temp
        log_total, positive = statistics(rows, scores)
        log_v[rows_at, :] = jnp.broadcast_to(log_total, (block, LANES))
        return total + jnp.sum(log_total - jnp.sum(scores * positive, axis=-1, keepdims=True), keepdims=True)

    total = lax.fori_loop(0, count // block, one_block, jnp.zeros((1, 1), f32))
    loss_ref[...] = jnp.broadcast_to(total * (1.0 / count), loss_ref.shape)
    own = own_ref[...]
    scores = product_nt(own[:, 0:width], passages) * inv_temp
    log_total, positive = statistics(own, scores)
    grad_low = ((jnp.exp(scores - log_total) - positive) * (loss_scale * inv_temp)).astype(bf16)
    grad_query = product(grad_low, passages)

    everyone = all_ref[...]
    queries = everyone[:, 0:width]
    passage = jnp.concatenate(
        [own[:, width : 2 * width].astype(f32), jnp.zeros((LANES - 8, width), f32)], axis=0
    ).astype(bf16)
    lane = lax.broadcasted_iota(jnp.int32, (1, LANES), 1)
    scores = product_nt(queries, passage) * inv_temp
    number = jnp.where(lane < 8, ids_ref[0] * 8 + lane, -1).astype(f32)
    positive = (number == target(everyone)).astype(f32)
    weight = jnp.exp(scores - log_v[...]) - positive
    grad_low = (jnp.where(lane < 8, weight, 0.0) * (loss_scale * inv_temp)).astype(bf16)
    grad_passage = product_t(grad_low, queries)[0:8]

    grad_unit = jnp.concatenate([grad_query, grad_passage], axis=0)
    pooled = pooled_ref[...]
    rate = lax.rsqrt(jnp.sum(pooled * pooled, axis=-1, keepdims=True) + norm_eps)
    inner = jnp.sum(pooled * grad_unit, axis=-1, keepdims=True)
    grad = rate * grad_unit - rate * rate * rate * pooled * inner
    grad_ref[...] = grad / len_ref[:, 0:1]


def column_total(values):
    return jnp.sum(values.reshape(values.shape[0] // 8, 8, values.shape[1]), axis=0)


def back_second(
    gp_ref, seg_ref, xhat_ref, rstd_ref, gain_ref, act01_hbm, act23_hbm,
    low_ref, vec_ref, d_ref,
    out_v, act_v, sums, sems,
):
    length, width = xhat_ref.shape
    gain = row_of(gain_ref)
    copies = start_all([(act23_hbm.at[1], act_v.at[0]), (act01_hbm.at[1], act_v.at[1])], sems)
    own = members(seg_ref).astype(bf16)
    top = gp_ref[...].astype(bf16)
    rest = (gp_ref[...] - top.astype(f32)).astype(bf16)
    out_v[...] = product_t(own, top) + product_t(own, rest)
    sums[...] = jnp.zeros_like(sums)

    @pl.loop(0, length // ROW_TILE)
    def _(i):
        rows = pl.ds(pl.multiple_of(i * ROW_TILE, ROW_TILE), ROW_TILE)
        grad_out, xhat = out_v[rows, :], xhat_ref[rows, :].astype(f32)
        sums[0] += column_total(grad_out * xhat)
        sums[1] += column_total(grad_out)
        grad = grad_out * gain
        first = jnp.mean(grad, axis=-1, keepdims=True)
        second = jnp.mean(grad * xhat, axis=-1, keepdims=True)
        grad = (grad - first - xhat * second) * rstd_ref[rows, 0:1]
        sums[2] += column_total(grad)
        low_ref[rows, :] = grad.astype(bf16)

    vec_ref[...] = jnp.zeros_like(vec_ref)
    for i in range(3):
        vec_ref[i : i + 1, :] = jnp.sum(sums[i], axis=0, keepdims=True)
    back_products(copies, act_v, low_ref, d_ref)


def back_products(copies, act_v, low_ref, d_ref):
    for i, copy in enumerate(copies):
        copy.wait()
        for first in range(0, act_v.shape[2], TILE):
            cols = slice(first, first + TILE)
            d_ref[i, cols, :] = product_t(act_v[i, :, cols], low_ref[...]).astype(bf16)


def back_outer(low_ref, act01_hbm, act23_hbm, d_ref, act_v, sems):
    copies = start_all([(act23_hbm.at[0], act_v.at[0]), (act01_hbm.at[0], act_v.at[1])], sems)
    back_products(copies, act_v, low_ref, d_ref)


def back_first(
    low_ref, xhat_ref, rstd_ref, gain_ref, slope01_hbm, slope23_hbm,
    wo0, wo1, wo2, wo3, wi0, wi1, wi2, wi3, wb0, wb1, wb2, wb3,
    gb_hbm, attn_ref, vec_ref, bin_ref, x0, x1, x2, x3,
    slope_v, wo_v, wi_v, wb_v, gb_v, total_v, sums, sems, out_sems,
):
    length, width = xhat_ref.shape
    units = wi_v.shape[2]
    gain = row_of(gain_ref)
    copies = start_all(
        [p for r, w in enumerate((wb0, wb1, wb2, wb3)) for p in ((w, wb_v.at[r]), ((slope01_hbm, slope23_hbm)[r // 2].at[r % 2], slope_v.at[r]))]
        + [(w, wi_v.at[r]) for r, w in enumerate((wi0, wi1, wi2, wi3))]
        + [(w, wo_v.at[r]) for r, w in enumerate((wo0, wo1, wo2, wo3))],
        sems,
    )
    outs = []
    for r in range(4):
        copies[2 * r].wait()
        copies[2 * r + 1].wait()
        for first in range(0, units, TILE):
            cols = slice(first, first + TILE)
            grad = product_nt(low_ref[...], wb_v[r, cols, :])
            low = (grad * slope_v[r, :, cols].astype(f32)).astype(bf16)
            gb_v[r, :, cols] = low
            bin_ref[r : r + 1, cols] = jnp.sum(column_total(low.astype(f32)), axis=0, keepdims=True)
        outs += start_all([(gb_v.at[r], gb_hbm.at[r])], out_sems.at[pl.ds(r, 1)])
    for copy in copies[8:]:
        copy.wait()
    for first in range(0, width, TILE):
        cols = slice(first, first + TILE)
        total = low_ref[:, cols].astype(f32)
        for r in range(4):
            total = total + product_nt(gb_v[r], wi_v[r, cols, :])
        total_v[:, cols] = total
    sums[...] = jnp.zeros_like(sums)

    @pl.loop(0, length // ROW_TILE)
    def _(i):
        rows = pl.ds(pl.multiple_of(i * ROW_TILE, ROW_TILE), ROW_TILE)
        grad_out, xhat = total_v[rows, :], xhat_ref[rows, :].astype(f32)
        sums[0] += column_total(grad_out * xhat)
        sums[1] += column_total(grad_out)
        grad = grad_out * gain
        first = jnp.mean(grad, axis=-1, keepdims=True)
        second = jnp.mean(grad * xhat, axis=-1, keepdims=True)
        grad = (grad - first - xhat * second) * rstd_ref[rows, 0:1]
        sums[2] += column_total(grad)
        attn_ref[rows, :] = grad.astype(bf16)

    vec_ref[...] = jnp.zeros_like(vec_ref)
    for i in range(3):
        vec_ref[i : i + 1, :] = jnp.sum(sums[i], axis=0, keepdims=True)
    for r, x_ref in enumerate((x0, x1, x2, x3)):
        x_ref[...] = product_nt(attn_ref[...], wo_v[r, 0 : x_ref.shape[1], :]).astype(bf16)
    for copy in outs:
        copy.wait()


def weight_grads(
    pieces, low1_ref, attn_ref, vec1_ref, vec2_ref, bin_ref, ca, cb, gb_hbm,
    d_ref,
    gb_v, sems,
):
    length, width = low1_ref.shape
    units = gb_v.shape[2]
    local = ca.shape[1]
    copies = start_all([(gb_hbm.at[r], gb_v.at[i]) for i, r in enumerate(pieces)], sems)
    for i, (r, c_ref) in enumerate(zip(pieces, (ca, cb))):
        copies[i].wait()
        for first in range(0, width, TILE):
            cols = slice(first, first + TILE)
            d_ref[i, cols, :] = product_t(low1_ref[:, cols], gb_v[i]).astype(bf16)
        d_ref[i, width : width + local, :] = product_t(c_ref[...], attn_ref[...]).astype(bf16)
        rows = jnp.concatenate(
            [vec1_ref[0:3, :], vec2_ref[0:3, :], bin_ref[r : r + 1, :], jnp.zeros((1, units), f32)],
            axis=0,
        )
        top = rows.astype(bf16)
        rest = (rows - top.astype(f32)).astype(bf16)
        at = width + local
        d_ref[i, at : at + 16, :] = jnp.concatenate([top, rest], axis=0)
        d_ref[i, at + 16 : at + VEC_ROWS, :] = jnp.zeros((VEC_ROWS - 16, units), bf16)


def hop(array, axis, flip):
    size = lax.axis_size(axis)
    return lax.ppermute(array, axis, [(i, i ^ flip) for i in range(size)])


def bit_of(axis, flip):
    return (lax.axis_index(axis) // flip) % 2


def ordered(bit, mine, other, axis):
    low_first = jnp.concatenate([mine, other], axis=axis)
    high_first = jnp.concatenate([other, mine], axis=axis)
    return jnp.where(bit == 0, low_first, high_first)


def bits_below(size):
    flips, flip = [], 1
    while flip < size:
        flips.append(flip)
        flip *= 2
    return flips


def together(*arrays):
    return lax.optimization_barrier(arrays)


def late(array, *earlier):
    return lax.optimization_barrier((array, *earlier))[0]


def gather_parts(mine, first=None):
    near = hop(mine, "mp", 1)
    far = hop(mine, "mp", 2) if first is None else first
    return [mine, near, far, hop(far, "mp", 1)]


def join(part, flip):
    return ordered(bit_of("dp", flip), part, hop(part, "dp", flip), 0)


def add_low(left_side, right_side):
    return (left_side.astype(f32) + right_side.astype(f32)).astype(bf16)


class Rows:
    def __init__(self):
        self.dp, self.mp = lax.axis_size("dp"), lax.axis_size("mp")
        flips = bits_below(self.dp)
        self.orders = flips, flips[1:2] + flips[:1] + flips[2:]
        self.steps = len(flips)

    def swap(self, values, step):
        pairs = [
            (i, ((i // self.mp) ^ self.orders[i % self.mp % 2][step]) * self.mp + i % self.mp)
            for i in range(self.dp * self.mp)
        ]
        return lax.ppermute(values, ("dp", "mp"), pairs)

    def bit(self, step):
        even, odd = (bit_of("dp", order[step]) for order in self.orders)
        return jnp.where(lax.axis_index("mp") % 2 == 1, odd, even)

    def cut(self, array, bit):
        arrays = array if isinstance(array, tuple) else (array,)
        half = arrays[0].shape[-2] // 2
        total = None
        for part in arrays:
            piece = lax.dynamic_slice_in_dim(part, bit * half, half, axis=-2).astype(f32)
            total = piece if total is None else total + piece
        return total

    def send(self, array, step):
        return self.swap(self.cut(array, 1 - self.bit(step)).astype(bf16), step)

    def keep(self, array, got, step):
        return (self.cut(array, self.bit(step)) + got.astype(f32)).astype(bf16)

    def join(self, array, got, step):
        return ordered(self.bit(step), array, got, array.ndim - 2)

    def gather(self, array, last):
        for step in reversed(range(last)):
            array = self.join(array, self.swap(array, step), step)
        return array

    def total(self, array):
        last = self.steps - 1
        for step in range(last):
            array = self.keep(array, self.send(array, step), step)
        array = add_low(array, self.swap(array, last))
        return self.gather(array, last)


class Running:
    def __init__(self, rows, array, plan):
        self.rows, self.array, self.plan = rows, array, plan

    def start(self):
        kind, step = self.plan[0]
        return self.rows.send(self.array, step) if kind == "send" else self.rows.swap(self.array, step)

    def finish(self, got):
        kind, step = self.plan.pop(0)
        if kind == "send":
            self.array = self.rows.keep(self.array, got, step)
        elif kind == "full":
            self.array = add_low(self.array, got)
        else:
            self.array = self.rows.join(self.array, got, step)


def params(cost=None, **more):
    return dict(
        compiler_params=pltpu.CompilerParams(vmem_limit_bytes=VMEM_BYTES, **more), cost_estimate=cost
    )


def cost(flops, moved, exps=0):
    return pl.CostEstimate(flops=int(flops), bytes_accessed=int(moved), transcendentals=int(exps))


def shape(dims, dtype=bf16):
    return jax.ShapeDtypeStruct(dims, dtype)


def shards(
    tokens, w_qkv, b_qv, w_out, b_out, norm1_gain, norm1_shift, w_in, b_in, w_back, b_back,
    norm2_gain, norm2_shift, segment_ids, pair_ids,
):
    row_count, length = segment_ids.shape
    width = tokens.shape[1]
    local = w_out.shape[0]
    units = w_in.shape[1]
    heads = local // HEAD_DIM
    blocks = length // Q_BLOCK
    member = lax.axis_index("mp")
    own_row = lax.axis_index("dp") * row_count + member
    m_arr = member.astype(jnp.int32).reshape(1)
    any_spec = pl.BlockSpec(memory_space=pl.ANY)
    vmem_spec = pl.BlockSpec(memory_space=pltpu.VMEM)
    smem_spec = pl.BlockSpec(memory_space=pltpu.SMEM)
    dma = pltpu.SemaphoreType.DMA

    tall = lambda vector: vector.reshape(-1, LANES)
    bit_x, bit_z = bit_of("dp", 1), bit_of("dp", 2)
    bits = jnp.stack([2 * bit_x + bit_z, 2 * bit_z + bit_x]).astype(jnp.int32)
    out_pack, in_quarter, back_quarter = pl.pallas_call(
        prepare,
        in_specs=[smem_spec] + [vmem_spec] * 2 + [any_spec] * 2,
        out_specs=[vmem_spec] * 3,
        out_shape=[
            shape((local + 16, width)), shape((width // 4, units)), shape((units // 4, width)),
        ],
        scratch_shapes=[dma((2,))],
        name="prepare",
        **params(cost(1e6, 2e6)),
    )(bits, tall(b_in), w_out, w_in, w_back)
    near_in, near_back = hop(w_in, "mp", 1), hop(w_back, "mp", 1)
    near_out = hop(out_pack, "mp", 1)
    far_out = hop(out_pack, "mp", 2)
    b_qv, near_in, near_back, near_out = together(b_qv, near_in, near_back, near_out)
    in_quarter = hop(in_quarter, "mp", 2)
    back_quarter = hop(back_quarter, "mp", 2)
    w_t = jnp.swapaxes(w_qkv, 1, 2)

    windows = jnp.stack(
        [segment_ids[:, window_start(i, length) :][:, :K_WINDOW] for i in range(blocks)], axis=1
    )
    seg_rows = segment_ids[:, None, :]

    def attend(count, source, place, held):
        return pl.pallas_call(
            functools.partial(attend_forward, len(held)),
            grid_spec=pltpu.PrefetchScalarGridSpec(
                num_scalar_prefetch=1,
                grid=(count,),
                in_specs=[
                    pl.BlockSpec((length, width), lambda i, m: (source(i) ^ m[0], 0)),
                    pl.BlockSpec(w_t.shape, lambda i, m: (0, 0, 0)),
                    pl.BlockSpec(b_qv.shape, lambda i, m: (0, 0)),
                    pl.BlockSpec((1, 1, length), lambda i, m: (source(i) ^ m[0], 0, 0)),
                    pl.BlockSpec((1, blocks, K_WINDOW), lambda i, m: (source(i) ^ m[0], 0, 0)),
                ]
                + [any_spec] * len(held),
                out_specs=[
                    pl.BlockSpec((1, 3, length, local), lambda i, m: (place + i, 0, 0, 0)),
                    pl.BlockSpec(
                        (1, heads * blocks, Q_BLOCK, K_WINDOW), lambda i, m: (place + i, 0, 0, 0)
                    ),
                ]
                + [pl.BlockSpec((length, local), lambda i, m: (0, 0))] * count,
                scratch_shapes=[pltpu.VMEM((length, local), bf16)],
            ),
            out_shape=[
                shape((row_count, 3, length, local)),
                shape((row_count, heads * blocks, Q_BLOCK, K_WINDOW)),
                *[shape((length, local))] * count,
            ],
            input_output_aliases={6 + i: i for i in range(len(held))},
            name="attend_forward",
            **params(cost(6 * count * length * width * local, 2e6 * count, count * heads * length * K_WINDOW)),
        )(m_arr, tokens, w_t, b_qv, seg_rows, windows, *held)

    qkv, probs, ctx3, ctx2, ctx1 = attend(3, lambda i: 3 - i, 0, ())
    ctx3, ctx2, ctx1, in_quarter, back_quarter, far_out = together(
        ctx3, ctx2, ctx1, in_quarter, back_quarter, far_out
    )
    in_got, back_got = hop(in_quarter, "dp", 2), hop(back_quarter, "dp", 1)
    qkv, probs, ctx0 = attend(1, lambda i: 0, 3, (qkv, probs))
    out_parts = [out_pack, near_out, far_out, hop(late(far_out, ctx0), "mp", 1)]
    ctx_got2, ctx_got3 = hop(ctx2, "mp", 2), hop(ctx3, "mp", 3)
    in_half = ordered(bit_z, in_quarter, late(in_got, ctx0), 0)
    back_half = ordered(bit_x, back_quarter, late(back_got, ctx0), 0)
    in_half, back_half, ctx_got2, ctx_got3 = together(in_half, back_half, ctx_got2, ctx_got3)
    ctx_parts = [ctx0, hop(ctx1, "mp", 1), ctx_got2, ctx_got3]
    seg_own = lax.dynamic_slice_in_dim(segment_ids, member, 1)
    pair_own = lax.dynamic_slice_in_dim(pair_ids, member, 1).reshape(-1, 1)
    pair_code = jnp.concatenate(
        [pair_own // 64, pair_own % 64, jnp.zeros((pair_own.shape[0], LANES - 2), jnp.int32)], axis=1
    ).astype(f32)
    in_got, back_got = hop(in_half, "dp", 1), hop(back_half, "dp", 2)
    act01, slope01, xhat1, rstd1, low1, total = pl.pallas_call(
        middle_first,
        in_specs=[smem_spec, any_spec] + [vmem_spec] * 3 + [any_spec] * 12,
        out_specs=[any_spec] * 2 + [vmem_spec] * 4,
        out_shape=[
            shape((2, length, units)), shape((2, length, units)),
            shape((length, width)), shape((length, LANES), f32), shape((length, width)),
            shape((length, width), f32),
        ],
        scratch_shapes=[
            pltpu.VMEM((length, width), bf16), pltpu.VMEM((4, length, local), bf16),
            pltpu.VMEM((4, local + 16, width), bf16), pltpu.VMEM((2, width, units), bf16),
            pltpu.VMEM((2, units, width), bf16), pltpu.VMEM((2, length, units), bf16),
            pltpu.VMEM((2, length, units), bf16), dma((13,)), dma((4,)),
        ],
        name="middle_first",
        **params(cost(2 * length * width * (width + 4 * units), 18e6, 2 * length * units)),
    )(
        m_arr, tokens, tall(b_out), tall(norm1_gain), tall(norm1_shift), *ctx_parts, *out_parts,
        w_in, near_in, w_back, near_back,
    )
    in_far = ordered(bit_x, in_half, late(in_got, total), 0)
    back_far = ordered(bit_z, back_half, late(back_got, total), 0)
    in_parts = [w_in, near_in, in_far, hop(in_far, "mp", 1)]
    back_parts = [w_back, near_back, back_far, hop(back_far, "mp", 1)]
    act23, slope23, xhat2, rstd2, out_own, pooled, lengths, msg = pl.pallas_call(
        middle_second,
        in_specs=[vmem_spec] * 6 + [any_spec] + [vmem_spec] * 2 + [any_spec] * 4,
        out_specs=[any_spec] * 2 + [vmem_spec] * 6,
        out_shape=[
            shape((2, length, units)), shape((2, length, units)),
            shape((length, width)), shape((length, LANES), f32), shape((length, width)),
            shape((16, width), f32), shape((16, LANES), f32), shape((8, 2 * width + LANES)),
        ],
        scratch_shapes=[
            pltpu.VMEM((2, width, units), bf16), pltpu.VMEM((2, units, width), bf16),
            pltpu.VMEM((2, length, units), bf16), pltpu.VMEM((2, length, units), bf16),
            pltpu.VMEM((length, width), f32), dma((5,)), dma((4,)),
        ],
        name="middle_second",
        **params(cost(8 * length * width * units, 12e6, 2 * length * units)),
    )(
        seg_own, pair_code, tall(b_back), tall(norm2_gain), tall(norm2_shift), low1, total,
        *out_parts[2:], *in_parts[2:], *back_parts[2:],
    )

    everyone = msg[None]
    steps = [("dp", flip) for flip in reversed(bits_below(lax.axis_size("dp")))]
    steps += [("mp", flip) for flip in reversed(bits_below(lax.axis_size("mp")))]
    while len(steps) > 1:
        everyone = four_ways(everyone, *steps[:2])
        steps = steps[2:]
    if steps:
        everyone = both_ways(everyone, hop(everyone, *steps[0]), *steps[0])
    everyone = everyone.reshape(-1, msg.shape[1])

    loss, grad_pooled = pl.pallas_call(
        contrast,
        in_specs=[smem_spec] + [vmem_spec] * 4,
        out_specs=[vmem_spec] * 2,
        out_shape=[shape((8, LANES), f32), shape((16, width), f32)],
        scratch_shapes=[pltpu.VMEM((everyone.shape[0], LANES), f32)],
        name="contrast",
        **params(cost(4e8, 2e6, 1e5)),
    )(own_row.astype(jnp.int32).reshape(1), everyone, msg, pooled, lengths)

    rows = Rows()
    grad_low2, vec2, back_send = pl.pallas_call(
        back_second,
        in_specs=[vmem_spec] * 5 + [any_spec] * 2,
        out_specs=[vmem_spec] * 3,
        out_shape=[
            shape((length, width)), shape((8, width), f32),
            shape((2, units, width)),
        ],
        scratch_shapes=[
            pltpu.VMEM((length, width), f32), pltpu.VMEM((2, length, units), bf16),
            pltpu.VMEM((3, 8, width), f32), dma((2,)),
        ],
        name="back_second",
        **params(cost(4 * length * width * units, 14e6)),
    )(grad_pooled, seg_own, xhat2, rstd2, tall(norm2_gain), act01, act23)
    back_got = hop(back_send, "mp", 1)
    back_keep = pl.pallas_call(
        back_outer,
        in_specs=[vmem_spec] + [any_spec] * 2,
        out_specs=vmem_spec,
        out_shape=shape((2, units, width)),
        scratch_shapes=[pltpu.VMEM((2, length, units), bf16), dma((2,))],
        name="back_outer",
        **params(cost(4 * length * width * units, 8e6)),
    )(grad_low2, act01, act23)
    grad_low2, back_keep, back_got = together(grad_low2, back_keep, back_got)
    back_sum = back_keep, back_got
    back_got = rows.send(back_sum, 0)
    out_far = hop(late(out_own, grad_low2), "mp", 2)

    gb, attn_low, vec1, d_bin, *ctx_grads = pl.pallas_call(
        back_first,
        in_specs=[vmem_spec] * 4 + [any_spec] * 14,
        out_specs=[any_spec] + [vmem_spec] * 7,
        out_shape=[
            shape((4, length, units)), shape((length, width)),
            shape((8, width), f32), shape((4, units), f32), *[shape((length, local))] * 4,
        ],
        scratch_shapes=[
            pltpu.VMEM((4, length, units), bf16), pltpu.VMEM((4, local + 16, width), bf16),
            pltpu.VMEM((4, width, units), bf16), pltpu.VMEM((4, units, width), bf16),
            pltpu.VMEM((4, length, units), bf16), pltpu.VMEM((length, width), f32),
            pltpu.VMEM((3, 8, width), f32), dma((16,)), dma((4,)),
        ],
        name="back_first",
        **params(cost(2 * length * width * (width + 8 * units), 25e6)),
    )(
        grad_low2, xhat1, rstd1, tall(norm1_gain), slope01, slope23, *out_parts, *in_parts, *back_parts,
    )

    attn_low, back_got, out_far, *back_sum = together(attn_low, back_got, out_far, *back_sum)
    out_pair = ordered(bit_of("mp", 2), out_own[None], out_far[None], 0)
    back_sum = rows.keep(tuple(back_sum), back_got, 0)
    got3 = hop(ctx_grads[3], "mp", 3)

    def first_grads(pieces, low):
        return pl.pallas_call(
            functools.partial(weight_grads, pieces),
            in_specs=[vmem_spec] * 7 + [any_spec],
            out_specs=vmem_spec,
            out_shape=shape((2, width + local + VEC_ROWS, units)),
            scratch_shapes=[pltpu.VMEM((2, length, units), bf16), dma((2,))],
            name="weight_grads",
            **params(cost(4 * length * width * (units + local), 7e6)),
        )(low1, low, vec1, vec2, d_bin, ctx_parts[pieces[0]], ctx_parts[pieces[1]], gb)

    first_send = first_grads((3, 1), attn_low)
    got3, attn_low, first_send, out_pair = together(got3, attn_low, first_send, out_pair)
    out_other = hop(out_pair, "mp", 1)
    first_got = hop(first_send, "mp", 1)
    got2 = hop(late(ctx_grads[2], first_send), "mp", 2)
    back_sum = late(back_sum, first_send)
    back_got = rows.send(back_sum, 1)
    first_keep = first_grads((2, 0), attn_low)
    own_grad, first_keep, first_got, got2, back_got, out_other = together(
        ctx_grads[0], first_keep, first_got, got2, back_got, out_other
    )
    back_sum = rows.keep(back_sum, back_got, 1)
    first_far = hop(add_low(first_keep[0], first_got[0]), "mp", 2)
    back_got = rows.send(back_sum, 2)
    got1 = hop(late(ctx_grads[1], own_grad), "mp", 1)

    def attend_back(count, source, place, last, grads, sums):
        same = lambda i, m: (0, 0)
        out_specs = [pl.BlockSpec((length, width), same)] * count
        out_shape = [shape((length, width))] * count
        if last:
            out_specs.append(pl.BlockSpec((3 * local + VEC_ROWS, width), same))
            out_shape.append(shape((3 * local + VEC_ROWS, width)))
        else:
            out_specs += [pl.BlockSpec((3 * local, width), same), pl.BlockSpec((8, local), same)]
            out_shape += [shape((3 * local, width), f32), shape((8, local), f32)]
        return pl.pallas_call(
            functools.partial(attend_backward, count, len(sums) == 0, last),
            grid_spec=pltpu.PrefetchScalarGridSpec(
                num_scalar_prefetch=1,
                grid=(count,),
                in_specs=[
                    pl.BlockSpec((length, width), lambda i, m: (source(i) ^ m[0], 0)),
                    pl.BlockSpec(w_t.shape, lambda i, m: (0, 0, 0)),
                    pl.BlockSpec((1, 3, length, local), lambda i, m: ((place + i) % row_count, 0, 0, 0)),
                    pl.BlockSpec(
                        (1, heads * blocks, Q_BLOCK, K_WINDOW), lambda i, m: ((place + i) % row_count, 0, 0, 0)
                    ),
                ]
                + [pl.BlockSpec((length, local), same)] * count
                + [pl.BlockSpec(part.shape, same) for part in sums],
                out_specs=out_specs,
                scratch_shapes=[
                    pltpu.VMEM((length, local), bf16), pltpu.VMEM((length, local), f32),
                    pltpu.VMEM((length, local), f32), pltpu.VMEM((3 * local, width), f32),
                    pltpu.VMEM((8, local), f32),
                ],
            ),
            out_shape=out_shape,
            name="attend_backward",
            **params(cost(12 * count * length * width * local, 4e6 * count)),
        )(m_arr, tokens, w_t, qkv, probs, *grads, *sums)

    back0, back3, *sums = attend_back(2, lambda i: 3 * i, 3, False, [own_grad, got3], [])
    back_got, got1, back3, *sums = together(back_got, got1, back3, *sums)
    back_sum = rows.keep(back_sum, back_got, 2)
    for step in range(3, rows.steps):
        back_sum = rows.keep(back_sum, rows.send(back_sum, step), step)
    back_got = hop(back_sum[0], "mp", 2)
    tok_got3 = hop(back3, "mp", 1)
    back2, back1, d_qkv = attend_back(2, lambda i: 2 - i, 1, True, [got2, got1], sums)
    first_far, first_keep, first_got, back_got, _ = together(
        first_far, first_keep, first_got, back_got, d_qkv
    )
    back_sum = add_low(back_sum[1], back_got)
    first_sum = (first_keep[1].astype(f32) + first_got[1].astype(f32) + first_far.astype(f32)).astype(bf16)
    last = rows.steps - 1
    tok_got1 = hop(back1, "mp", 1)
    far = add_low(back2, tok_got3)
    down = [("send", step) for step in range(last)] + [("full", last)]
    up = [("join", step) for step in reversed(range(last))]
    sums = [
        Running(rows, first_sum, down + up),
        Running(rows, d_qkv, down + up),
        Running(rows, back_sum, [("join", last)] + up),
    ]
    stage, extra = 0, [tok_got1, hop(far, "mp", 2)]
    while any(part.plan for part in sums):
        parts = [part for part in sums if part.plan and not (part is sums[2] and stage == 1)]
        if stage == 2:
            sums[2].array = late(sums[2].array, sums[0].array)
        if stage == 2:
            sums[1].array = late(sums[1].array, sums[0].array)
        starts = [part.start() for part in parts]
        if stage == 0:
            starts[2], *extra = together(starts[2], *extra)
        hops = starts + extra
        for part in parts:
            part.finish(hops.pop(0))
        if stage == 0:
            own = back0.astype(f32) + attn_low.astype(f32) + hops[0].astype(f32) + hops[1].astype(f32)
            own = own.astype(bf16)
            extra = [hop(own, "mp", 2)]
        elif stage == 1:
            tok_pair = ordered(bit_of("mp", 2), own[None], hops[0][None], 0)
            extra = [hop(tok_pair, "mp", 1)]
        elif stage == 2:
            d_tokens = rows_of_all(tok_pair, hops[0])
            extra = []
        stage += 1
    sum_first, sum_qkv, sum_back = (part.array for part in sums)
    layer_out = rows_of_all(out_pair, out_other)

    at = width + local
    vectors = sum_first[at : at + 8].astype(f32) + sum_first[at + 8 : at + 16].astype(f32)
    shares = lax.dynamic_slice_in_dim(vectors[0:6], member * local, local, axis=1)
    at = 3 * local
    d_bqv = sum_qkv[at : at + 2, 0:local].astype(f32) + sum_qkv[at + 8 : at + 10, 0:local].astype(f32)
    d_wqkv = jnp.swapaxes(sum_qkv[0:at].reshape(3, local, width), 1, 2).astype(f32)
    return (
        loss[0, 0],
        layer_out,
        d_tokens,
        d_wqkv,
        d_bqv,
        sum_first[width : width + local].astype(f32),
        shares[2],
        shares[0],
        shares[1],
        sum_first[0:width].astype(f32),
        vectors[6],
        sum_back.astype(f32),
        shares[5],
        shares[3],
        shares[4],
    )


def both_ways(array, other, axis, flip):
    low_first = jnp.stack([array, other], axis=1)
    high_first = jnp.stack([other, array], axis=1)
    joined = jnp.where(bit_of(axis, flip) == 0, low_first, high_first)
    return joined.reshape(-1, *array.shape[1:])


def four_ways(array, first, second):
    dp, mp = lax.axis_size("dp"), lax.axis_size("mp")

    def fetch(*steps):
        flip = sum(step * (mp if axis == "dp" else 1) for axis, step in steps)
        return lax.ppermute(array, ("dp", "mp"), [(i, i ^ flip) for i in range(dp * mp)])

    far, near, corner = fetch(first), fetch(second), fetch(first, second)
    count = array.shape[0]
    mine = both_ways(array, near, *second).reshape(count, 2, *array.shape[1:])
    theirs = both_ways(far, corner, *second).reshape(count, 2, *array.shape[1:])
    return both_ways(mine, theirs, *first).reshape(-1, *array.shape[1:])


def rows_of_all(pair, other):
    low_first = jnp.stack([pair, other], axis=1)
    high_first = jnp.stack([other, pair], axis=1)
    joined = jnp.where(bit_of("mp", 1) == 0, low_first, high_first)
    return joined.reshape(-1, pair.shape[-1])


def solution(mesh):
    return jax.shard_map(
        shards,
        mesh=mesh,
        in_specs=(
            P("dp", None),
            P(None, None, "mp"),
            P(None, "mp"),
            P("mp", None),
            P(),
            P(),
            P(),
            P(None, "mp"),
            P("mp"),
            P("mp", None),
            P(),
            P(),
            P(),
            P("dp", None),
            P("dp", None),
        ),
        out_specs=(
            P(),
            P("dp", None),
            P("dp", None),
            P(None, None, "mp"),
            P(None, "mp"),
            P("mp", None),
            P("mp"),
            P("mp"),
            P("mp"),
            P(None, "mp"),
            P("mp"),
            P("mp", None),
            P("mp"),
            P("mp"),
            P("mp"),
        ),
        check_vma=False,
    )
```

```python
import functools

import jax
import jax.numpy as jnp
from jax import lax
from jax.experimental import pallas as pl
from jax.experimental.pallas import tpu as pltpu
from jax.sharding import PartitionSpec as P

HEAD_DIM = 64
Q_BLOCK = 128
K_WINDOW = 256
LANES = 128
TILE = 256
ROW_TILE = 128
VEC_ROWS = 64
VMEM_BYTES = 52 * 1024 * 1024

norm_eps = 1e-06
inv_temp = 50.0
loss_scale = 8.0
masked_score = -1000000000.0

f32 = jnp.float32
bf16 = jnp.bfloat16


def product(left_side, right_side):
    return jnp.dot(left_side, right_side, preferred_element_type=f32)


def product_t(left_side, right_side):
    return lax.dot_general(
        left_side, right_side, (((0,), (0,)), ((), ())), preferred_element_type=f32
    )


def product_nt(left_side, right_side):
    return lax.dot_general(
        left_side, right_side, (((1,), (1,)), ((), ())), preferred_element_type=f32
    )


def window_start(block, length):
    return min(max(block * Q_BLOCK - HEAD_DIM, 0), length - K_WINDOW)


def gelu_and_slope(values):
    bell = jnp.exp(values * values * -0.5)
    t = 1.0 / (1.0 + (0.3275911 * 0.7071067811865476) * jnp.abs(values))
    poly = 1.061405429 * t - 1.453152027
    poly = poly * t + 1.421413741
    poly = poly * t - 0.284496736
    poly = poly * t + 0.254829592
    tail = (0.5 * t) * (poly * bell)
    phi = jnp.where(values >= 0.0, 1.0 - tail, tail)
    return values * phi, phi + (values * 0.3989422804014327) * bell


def head_lanes(pair, which):
    lane = lax.broadcasted_iota(jnp.int32, pair.shape, 1)
    keep = (lane < HEAD_DIM) if which == 0 else (lane >= HEAD_DIM)
    return jnp.where(keep, pair, jnp.zeros_like(pair))


def columns(array, first, count):
    return array[:, first : first + count]


def head_parts(array, local_width):
    parts = []
    for head in range(local_width // HEAD_DIM):
        first = head // 2 * LANES
        width = min(LANES, local_width - first)
        part = columns(array, first, width)
        parts.append(part if width < LANES else head_lanes(part, head % 2))
    return parts


def merge_heads(results, local_width):
    pieces = []
    for first in range(0, local_width, LANES):
        head = first // HEAD_DIM
        if local_width - first >= LANES:
            lane = lax.broadcasted_iota(jnp.int32, results[head].shape, 1)
            pieces.append((first, jnp.where(lane < HEAD_DIM, results[head], results[head + 1])))
        else:
            pieces.append((first, results[head]))
    return pieces


def attend_forward(held, m_ref, tok_ref, w_ref, b_ref, seg_ref, win_ref, *refs):
    qkv_ref, prob_ref, *ctx_refs, ctx_v = refs[held:]
    length = tok_ref.shape[0]
    width = w_ref.shape[1]
    heads = width // HEAD_DIM
    tok = tok_ref[...]
    q = ((product_nt(tok, w_ref[0]) + b_ref[0:1, :]).astype(bf16) * HEAD_DIM**-0.5).astype(bf16)
    k = product_nt(tok, w_ref[1]).astype(bf16)
    v = (product_nt(tok, w_ref[2]) + b_ref[1:2, :]).astype(bf16)
    qkv_ref[0, 0] = q
    qkv_ref[0, 1] = k
    qkv_ref[0, 2] = v
    q_parts = head_parts(q, width)
    slot = lax.broadcasted_iota(jnp.int32, (16, 1), 0)
    own = (seg_ref[0] == slot).astype(f32).astype(bf16)
    for block in range(length // Q_BLOCK):
        at, start = block * Q_BLOCK, window_start(block, length)
        seen = (win_ref[0, block : block + 1, :] == slot).astype(f32).astype(bf16)
        mask = (product_t(columns(own, at, Q_BLOCK), seen) - 1.0) * -masked_score
        results = []
        for head in range(heads):
            first = head // 2 * LANES
            part = min(LANES, width - first)
            key = k[start : start + K_WINDOW, first : first + part]
            value = v[start : start + K_WINDOW, first : first + part]
            scores = product_nt(q_parts[head][at : at + Q_BLOCK], key) + mask
            weights = jnp.exp(scores - jnp.max(scores, axis=-1, keepdims=True))
            low = (weights * (1.0 / jnp.sum(weights, axis=-1, keepdims=True))).astype(bf16)
            prob_ref[0, head * (length // Q_BLOCK) + block] = low
            results.append(product(low, value))
        for first, merged in merge_heads(results, width):
            ctx_v[at : at + Q_BLOCK, first : first + merged.shape[1]] = merged.astype(bf16)
    for piece, ctx_ref in enumerate(ctx_refs):

        @pl.when(pl.program_id(0) == piece)
        def _():
            ctx_ref[...] = ctx_v[...]


def attend_backward(count, first, last, m_ref, tok_ref, w_ref, qkv_ref, prob_ref, *refs):
    g_refs, refs = refs[:count], refs[count:]
    if not first:
        before_ref, vec_before_ref, *refs = refs
    o_refs, refs = refs[:count], refs[count:]
    if last:
        dw_ref, gctx, gk_sum, gv_sum, dw_sum, vec_sum = refs
    else:
        dw_ref, vec_ref, gctx, gk_sum, gv_sum, dw_sum, vec_sum = refs
    step = pl.program_id(0)
    length = tok_ref.shape[0]
    width = w_ref.shape[1]
    heads = width // HEAD_DIM
    for piece, g_ref in enumerate(g_refs):

        @pl.when(step == piece)
        def _():
            gctx[...] = g_ref[...]

    @pl.when(step == 0)
    def _():
        dw_sum[...] = jnp.zeros_like(dw_sum) if first else before_ref[...]
        vec_sum[...] = jnp.zeros_like(vec_sum) if first else vec_before_ref[...]

    gk_sum[...] = jnp.zeros_like(gk_sum)
    gv_sum[...] = jnp.zeros_like(gv_sum)
    q, k, v = qkv_ref[0, 0], qkv_ref[0, 1], qkv_ref[0, 2]
    q_parts = head_parts(q, width)
    g_parts = head_parts(gctx[...], width)
    gq_blocks = []
    for block in range(length // Q_BLOCK):
        at, start = block * Q_BLOCK, window_start(block, length)
        rows = slice(start, start + K_WINDOW)
        results, gk, gv = [], {}, {}
        for head in range(heads):
            first = head // 2 * LANES
            part = min(LANES, width - first)
            key, value = k[rows, first : first + part], v[rows, first : first + part]
            grad = g_parts[head][at : at + Q_BLOCK]
            low = prob_ref[0, head * (length // Q_BLOCK) + block]
            prob = low.astype(f32)
            grad_prob = product_nt(grad, value)
            inner = jnp.sum(prob * grad_prob, axis=-1, keepdims=True)
            grad_low = (prob * (grad_prob - inner)).astype(bf16)
            results.append(product(grad_low, key))
            gk_part = product_t(grad_low, q_parts[head][at : at + Q_BLOCK])
            gv_part = product_t(low, grad)
            gk[first] = gk[first] + gk_part if first in gk else gk_part
            gv[first] = gv[first] + gv_part if first in gv else gv_part
        for first in gk:
            lanes = slice(first, first + gk[first].shape[1])
            gk_sum[rows, lanes] += gk[first]
            gv_sum[rows, lanes] += gv[first]
        gq_blocks.append(merge_heads(results, width))
    gq = jnp.concatenate(
        [
            jnp.concatenate(
                [(blocks[i][1] * HEAD_DIM**-0.5).astype(bf16) for blocks in gq_blocks], axis=0
            )
            for i in range(len(gq_blocks[0]))
        ],
        axis=1,
    )
    gk, gv = gk_sum[...].astype(bf16), gv_sum[...].astype(bf16)
    tok = tok_ref[...]
    back = None
    for c, grad in enumerate((gq, gk, gv)):
        dw_sum[c * width : (c + 1) * width, :] += product_t(grad, tok)
        term = product(grad, w_ref[c])
        back = term if back is None else back + term
    vec_sum[0:1, :] += jnp.sum(gq.astype(f32), axis=0, keepdims=True)
    vec_sum[1:2, :] += jnp.sum(gv.astype(f32), axis=0, keepdims=True)
    back = back.astype(bf16)
    for piece, o_ref in enumerate(o_refs):

        @pl.when(step == piece)
        def _():
            o_ref[...] = back

    @pl.when(step == count - 1)
    def _():
        if not last:
            dw_ref[...] = dw_sum[...]
            vec_ref[...] = vec_sum[...]
            return
        dw_ref[0 : 3 * width, :] = dw_sum[...].astype(bf16)
        vec = vec_sum[...]
        top = vec.astype(bf16)
        rest = (vec - top.astype(f32)).astype(bf16)
        dw_ref[3 * width :, :] = jnp.zeros((VEC_ROWS, dw_ref.shape[1]), bf16)
        dw_ref[3 * width : 3 * width + 16, 0:width] = jnp.concatenate([top, rest], axis=0)


def row_of(ref):
    return jnp.concatenate([ref[i : i + 1, :] for i in range(ref.shape[0])], axis=1)


def start_all(pairs, sems):
    copies = []
    for i, (source, target) in enumerate(pairs):
        copy = pltpu.make_async_copy(source, target, sems.at[i])
        copy.start()
        copies.append(copy)
    return copies


def prepare(bits_ref, bias_ref, out_ref, in_hbm, back_hbm, pack_ref, in_ref, back_ref, sems):
    quarter = in_ref.shape[0]
    in_at = pl.multiple_of(bits_ref[0] * quarter, quarter)
    back_at = pl.multiple_of(bits_ref[1] * quarter, quarter)
    copies = start_all(
        [(in_hbm.at[pl.ds(in_at, quarter)], in_ref), (back_hbm.at[pl.ds(back_at, quarter)], back_ref)], sems
    )
    local = out_ref.shape[0]
    bias = row_of(bias_ref)
    high = bias.astype(bf16)
    rest = bias - high.astype(f32)
    middle = rest.astype(bf16)
    low = (rest - middle.astype(f32)).astype(bf16)
    slot = lax.broadcasted_iota(jnp.int32, (16, 1), 0)
    rows = jnp.where(slot == 0, high.astype(f32), 0.0)
    rows = jnp.where(slot == 1, middle.astype(f32), rows)
    rows = jnp.where(slot == 2, low.astype(f32), rows)
    pack_ref[0:local, :] = out_ref[...]
    pack_ref[local : local + 16, :] = rows.astype(bf16)
    for copy in copies:
        copy.wait()


def feed(r, low_ref, wi_v, b_in, act_v, slope_v):
    for first in range(0, wi_v.shape[2], TILE):
        cols = slice(first, first + TILE)
        before = product(low_ref[...], wi_v[r, :, cols]) + b_in[:, cols]
        active, slope = gelu_and_slope(before)
        act_v[r, :, cols] = active.astype(bf16)
        slope_v[r, :, cols] = slope.astype(bf16)


def middle_first(
    m_ref, tok_hbm, bias_ref, gain_ref, shift_ref, c0, c1, c2, c3, wo0, wo1, wo2, wo3, wi0, wi1, wb0, wb1,
    act_hbm, slope_hbm, xhat1_ref, rstd1_ref, low1_ref, total_ref,
    tok_v, ctx_v, wo_v, wi_v, wb_v, act_v, slope_v, sems, out_sems,
):
    length, width = tok_v.shape
    local = ctx_v.shape[2]
    b_out, gain1, shift1 = row_of(bias_ref), row_of(gain_ref), row_of(shift_ref)
    at = pl.multiple_of(m_ref[0] * length, length)
    copies = start_all(
        [(tok_hbm.at[pl.ds(at, length)], tok_v)]
        + [(c, ctx_v.at[r]) for r, c in enumerate((c0, c1, c2, c3))]
        + [(w, wo_v.at[r]) for r, w in enumerate((wo0, wo1, wo2, wo3))]
        + [(w, wi_v.at[r]) for r, w in enumerate((wi0, wi1))]
        + [(w, wb_v.at[r]) for r, w in enumerate((wb0, wb1))],
        sems,
    )
    for copy in copies[:9]:
        copy.wait()
    for first in range(0, width, TILE):
        cols = slice(first, first + TILE)
        total = tok_v[:, cols].astype(f32) + b_out[:, cols]
        for r in range(4):
            total = total + product(ctx_v[r], wo_v[r, 0:local, cols])
        total_ref[:, cols] = total

    @pl.loop(0, length // ROW_TILE)
    def _(i):
        rows = pl.ds(pl.multiple_of(i * ROW_TILE, ROW_TILE), ROW_TILE)
        values = total_ref[rows, :]
        center = values - jnp.mean(values, axis=-1, keepdims=True)
        rate = lax.rsqrt(jnp.mean(center * center, axis=-1, keepdims=True) + norm_eps)
        xhat = center * rate
        xhat1_ref[rows, :] = xhat.astype(bf16)
        rstd1_ref[rows, :] = jnp.broadcast_to(rate, (ROW_TILE, LANES))
        normed = xhat * gain1 + shift1
        total_ref[rows, :] = normed
        low1_ref[rows, :] = normed.astype(bf16)

    outs = []
    for r in range(2):
        copies[9 + r].wait()
        b_in = jnp.sum(wo_v[r, local : local + 16, :].astype(f32), axis=0, keepdims=True)
        feed(r, low1_ref, wi_v, b_in, act_v, slope_v)
        outs += start_all(
            [(act_v.at[r], act_hbm.at[r]), (slope_v.at[r], slope_hbm.at[r])],
            out_sems.at[pl.ds(2 * r, 2)],
        )
    for copy in copies[11:]:
        copy.wait()
    for first in range(0, width, TILE):
        cols = slice(first, first + TILE)
        total_ref[:, cols] += product(act_v[0], wb_v[0, :, cols]) + product(act_v[1], wb_v[1, :, cols])
    for copy in outs:
        copy.wait()


def middle_second(
    seg_ref, pair_ref, bias_ref, gain_ref, shift_ref, low1_ref, total_hbm, wo2, wo3, wi2, wi3, wb2, wb3,
    act_hbm, slope_hbm, xhat2_ref, rstd2_ref, out_ref, pooled_ref, len_ref, msg_ref,
    wi_v, wb_v, act_v, slope_v, resid, sems, out_sems,
):
    length, width = resid.shape
    local = wo2.shape[0] - 16
    b_back, gain2, shift2 = row_of(bias_ref), row_of(gain_ref), row_of(shift_ref)
    copies = start_all(
        [(w, wi_v.at[r]) for r, w in enumerate((wi2, wi3))]
        + [(total_hbm, resid)]
        + [(w, wb_v.at[r]) for r, w in enumerate((wb2, wb3))],
        sems,
    )
    outs = []
    for r in range(2):
        copies[r].wait()
        b_in = jnp.sum((wo2, wo3)[r][local : local + 16, :].astype(f32), axis=0, keepdims=True)
        feed(r, low1_ref, wi_v, b_in, act_v, slope_v)
        outs += start_all(
            [(act_v.at[r], act_hbm.at[r]), (slope_v.at[r], slope_hbm.at[r])],
            out_sems.at[pl.ds(2 * r, 2)],
        )
    for copy in copies[2:]:
        copy.wait()
    for first in range(0, width, TILE):
        cols = slice(first, first + TILE)
        total = resid[:, cols] + b_back[:, cols]
        resid[:, cols] = total + product(act_v[0], wb_v[0, :, cols]) + product(act_v[1], wb_v[1, :, cols])

    @pl.loop(0, length // ROW_TILE)
    def _(i):
        rows = pl.ds(pl.multiple_of(i * ROW_TILE, ROW_TILE), ROW_TILE)
        values = resid[rows, :]
        center = values - jnp.mean(values, axis=-1, keepdims=True)
        rate = lax.rsqrt(jnp.mean(center * center, axis=-1, keepdims=True) + norm_eps)
        xhat = center * rate
        xhat2_ref[rows, :] = xhat.astype(bf16)
        rstd2_ref[rows, :] = jnp.broadcast_to(rate, (ROW_TILE, LANES))
        out_ref[rows, :] = (xhat * gain2 + shift2).astype(bf16)

    own = members(seg_ref)
    sums = product(own.astype(bf16), out_ref[...])
    count = jnp.sum(own, axis=-1, keepdims=True)
    pooled = sums / count
    rate = lax.rsqrt(jnp.sum(pooled * pooled, axis=-1, keepdims=True) + norm_eps)
    unit = (pooled * rate).astype(bf16)
    pooled_ref[...] = pooled
    len_ref[...] = jnp.broadcast_to(count, len_ref.shape)
    half = unit.astype(f32)
    msg_ref[:, 0:width] = half[0:8].astype(bf16)
    msg_ref[:, width : 2 * width] = half[8:16].astype(bf16)
    msg_ref[:, 2 * width :] = pair_ref[...].astype(bf16)
    for copy in outs:
        copy.wait()


def members(seg_ref):
    slot = lax.broadcasted_iota(jnp.int32, (16, 1), 0)
    segment = jnp.where(slot < 8, 2 * slot, 2 * slot - 15)
    return (seg_ref[...] == segment).astype(f32)


def contrast(ids_ref, all_ref, own_ref, pooled_ref, len_ref, loss_ref, grad_ref, log_v):
    width = pooled_ref.shape[1]
    count = all_ref.shape[0]
    block = min(count, 256)
    passages = all_ref[:, width : 2 * width]
    number = lax.broadcasted_iota(jnp.int32, (1, count), 1).astype(f32)

    def target(rows):
        coded = rows[:, 2 * width :].astype(f32)
        return coded[:, 0:1] * 64.0 + coded[:, 1:2]

    def statistics(rows, scores):
        best = jnp.max(scores, axis=-1, keepdims=True)
        log_total = best + jnp.log(jnp.sum(jnp.exp(scores - best), axis=-1, keepdims=True))
        return log_total, (number == target(rows)).astype(f32)

    def one_block(i, total):
        rows_at = pl.ds(pl.multiple_of(i * block, block), block)
        rows = all_ref[rows_at, :]
        scores = product_nt(rows[:, 0:width], passages) * inv_temp
        log_total, positive = statistics(rows, scores)
        log_v[rows_at, :] = jnp.broadcast_to(log_total, (block, LANES))
        return total + jnp.sum(log_total - jnp.sum(scores * positive, axis=-1, keepdims=True), keepdims=True)

    total = lax.fori_loop(0, count // block, one_block, jnp.zeros((1, 1), f32))
    loss_ref[...] = jnp.broadcast_to(total * (1.0 / count), loss_ref.shape)
    own = own_ref[...]
    scores = product_nt(own[:, 0:width], passages) * inv_temp
    log_total, positive = statistics(own, scores)
    grad_low = ((jnp.exp(scores - log_total) - positive) * (loss_scale * inv_temp)).astype(bf16)
    grad_query = product(grad_low, passages)

    everyone = all_ref[...]
    queries = everyone[:, 0:width]
    passage = jnp.concatenate(
        [own[:, width : 2 * width].astype(f32), jnp.zeros((LANES - 8, width), f32)], axis=0
    ).astype(bf16)
    lane = lax.broadcasted_iota(jnp.int32, (1, LANES), 1)
    scores = product_nt(queries, passage) * inv_temp
    number = jnp.where(lane < 8, ids_ref[0] * 8 + lane, -1).astype(f32)
    positive = (number == target(everyone)).astype(f32)
    weight = jnp.exp(scores - log_v[...]) - positive
    grad_low = (jnp.where(lane < 8, weight, 0.0) * (loss_scale * inv_temp)).astype(bf16)
    grad_passage = product_t(grad_low, queries)[0:8]

    grad_unit = jnp.concatenate([grad_query, grad_passage], axis=0)
    pooled = pooled_ref[...]
    rate = lax.rsqrt(jnp.sum(pooled * pooled, axis=-1, keepdims=True) + norm_eps)
    inner = jnp.sum(pooled * grad_unit, axis=-1, keepdims=True)
    grad = rate * grad_unit - rate * rate * rate * pooled * inner
    grad_ref[...] = grad / len_ref[:, 0:1]


def column_total(values):
    return jnp.sum(values.reshape(values.shape[0] // 8, 8, values.shape[1]), axis=0)


def back_second(
    gp_ref, seg_ref, xhat_ref, rstd_ref, gain_ref, act01_hbm, act23_hbm,
    low_ref, vec_ref, d_ref,
    out_v, act_v, sums, sems,
):
    length, width = xhat_ref.shape
    gain = row_of(gain_ref)
    copies = start_all([(act23_hbm.at[1], act_v.at[0]), (act01_hbm.at[1], act_v.at[1])], sems)
    own = members(seg_ref).astype(bf16)
    top = gp_ref[...].astype(bf16)
    rest = (gp_ref[...] - top.astype(f32)).astype(bf16)
    out_v[...] = product_t(own, top) + product_t(own, rest)
    sums[...] = jnp.zeros_like(sums)

    @pl.loop(0, length // ROW_TILE)
    def _(i):
        rows = pl.ds(pl.multiple_of(i * ROW_TILE, ROW_TILE), ROW_TILE)
        grad_out, xhat = out_v[rows, :], xhat_ref[rows, :].astype(f32)
        sums[0] += column_total(grad_out * xhat)
        sums[1] += column_total(grad_out)
        grad = grad_out * gain
        first = jnp.mean(grad, axis=-1, keepdims=True)
        second = jnp.mean(grad * xhat, axis=-1, keepdims=True)
        grad = (grad - first - xhat * second) * rstd_ref[rows, 0:1]
        sums[2] += column_total(grad)
        low_ref[rows, :] = grad.astype(bf16)

    vec_ref[...] = jnp.zeros_like(vec_ref)
    for i in range(3):
        vec_ref[i : i + 1, :] = jnp.sum(sums[i], axis=0, keepdims=True)
    back_products(copies, act_v, low_ref, d_ref)


def back_products(copies, act_v, low_ref, d_ref):
    for i, copy in enumerate(copies):
        copy.wait()
        for first in range(0, act_v.shape[2], TILE):
            cols = slice(first, first + TILE)
            d_ref[i, cols, :] = product_t(act_v[i, :, cols], low_ref[...]).astype(bf16)


def back_outer(low_ref, act01_hbm, act23_hbm, d_ref, act_v, sems):
    copies = start_all([(act23_hbm.at[0], act_v.at[0]), (act01_hbm.at[0], act_v.at[1])], sems)
    back_products(copies, act_v, low_ref, d_ref)


def back_first(
    low_ref, xhat_ref, rstd_ref, gain_ref, slope01_hbm, slope23_hbm,
    wo0, wo1, wo2, wo3, wi0, wi1, wi2, wi3, wb0, wb1, wb2, wb3,
    gb_hbm, attn_ref, vec_ref, bin_ref, x0, x1, x2, x3,
    slope_v, wo_v, wi_v, wb_v, gb_v, total_v, sums, sems, out_sems,
):
    length, width = xhat_ref.shape
    units = wi_v.shape[2]
    gain = row_of(gain_ref)
    copies = start_all(
        [p for r, w in enumerate((wb0, wb1, wb2, wb3)) for p in ((w, wb_v.at[r]), ((slope01_hbm, slope23_hbm)[r // 2].at[r % 2], slope_v.at[r]))]
        + [(w, wi_v.at[r]) for r, w in enumerate((wi0, wi1, wi2, wi3))]
        + [(w, wo_v.at[r]) for r, w in enumerate((wo0, wo1, wo2, wo3))],
        sems,
    )
    outs = []
    for r in range(4):
        copies[2 * r].wait()
        copies[2 * r + 1].wait()
        for first in range(0, units, TILE):
            cols = slice(first, first + TILE)
            grad = product_nt(low_ref[...], wb_v[r, cols, :])
            low = (grad * slope_v[r, :, cols].astype(f32)).astype(bf16)
            gb_v[r, :, cols] = low
            bin_ref[r : r + 1, cols] = jnp.sum(column_total(low.astype(f32)), axis=0, keepdims=True)
        outs += start_all([(gb_v.at[r], gb_hbm.at[r])], out_sems.at[pl.ds(r, 1)])
    for copy in copies[8:]:
        copy.wait()
    for first in range(0, width, TILE):
        cols = slice(first, first + TILE)
        total = low_ref[:, cols].astype(f32)
        for r in range(4):
            total = total + product_nt(gb_v[r], wi_v[r, cols, :])
        total_v[:, cols] = total
    sums[...] = jnp.zeros_like(sums)

    @pl.loop(0, length // ROW_TILE)
    def _(i):
        rows = pl.ds(pl.multiple_of(i * ROW_TILE, ROW_TILE), ROW_TILE)
        grad_out, xhat = total_v[rows, :], xhat_ref[rows, :].astype(f32)
        sums[0] += column_total(grad_out * xhat)
        sums[1] += column_total(grad_out)
        grad = grad_out * gain
        first = jnp.mean(grad, axis=-1, keepdims=True)
        second = jnp.mean(grad * xhat, axis=-1, keepdims=True)
        grad = (grad - first - xhat * second) * rstd_ref[rows, 0:1]
        sums[2] += column_total(grad)
        attn_ref[rows, :] = grad.astype(bf16)

    vec_ref[...] = jnp.zeros_like(vec_ref)
    for i in range(3):
        vec_ref[i : i + 1, :] = jnp.sum(sums[i], axis=0, keepdims=True)
    for r, x_ref in enumerate((x0, x1, x2, x3)):
        x_ref[...] = product_nt(attn_ref[...], wo_v[r, 0 : x_ref.shape[1], :]).astype(bf16)
    for copy in outs:
        copy.wait()


def weight_grads(
    pieces, low1_ref, attn_ref, vec1_ref, vec2_ref, bin_ref, ca, cb, gb_hbm,
    d_ref,
    gb_v, sems,
):
    length, width = low1_ref.shape
    units = gb_v.shape[2]
    local = ca.shape[1]
    copies = start_all([(gb_hbm.at[r], gb_v.at[i]) for i, r in enumerate(pieces)], sems)
    for i, (r, c_ref) in enumerate(zip(pieces, (ca, cb))):
        copies[i].wait()
        for first in range(0, width, TILE):
            cols = slice(first, first + TILE)
            d_ref[i, cols, :] = product_t(low1_ref[:, cols], gb_v[i]).astype(bf16)
        d_ref[i, width : width + local, :] = product_t(c_ref[...], attn_ref[...]).astype(bf16)
        rows = jnp.concatenate(
            [vec1_ref[0:3, :], vec2_ref[0:3, :], bin_ref[r : r + 1, :], jnp.zeros((1, units), f32)],
            axis=0,
        )
        top = rows.astype(bf16)
        rest = (rows - top.astype(f32)).astype(bf16)
        at = width + local
        d_ref[i, at : at + 16, :] = jnp.concatenate([top, rest], axis=0)
        d_ref[i, at + 16 : at + VEC_ROWS, :] = jnp.zeros((VEC_ROWS - 16, units), bf16)


def hop(array, axis, flip):
    size = lax.axis_size(axis)
    return lax.ppermute(array, axis, [(i, i ^ flip) for i in range(size)])


def bit_of(axis, flip):
    return (lax.axis_index(axis) // flip) % 2


def ordered(bit, mine, other, axis):
    low_first = jnp.concatenate([mine, other], axis=axis)
    high_first = jnp.concatenate([other, mine], axis=axis)
    return jnp.where(bit == 0, low_first, high_first)


def bits_below(size):
    flips, flip = [], 1
    while flip < size:
        flips.append(flip)
        flip *= 2
    return flips


def together(*arrays):
    return lax.optimization_barrier(arrays)


def late(array, *earlier):
    return lax.optimization_barrier((array, *earlier))[0]


def gather_parts(mine, first=None):
    near = hop(mine, "mp", 1)
    far = hop(mine, "mp", 2) if first is None else first
    return [mine, near, far, hop(far, "mp", 1)]


def join(part, flip):
    return ordered(bit_of("dp", flip), part, hop(part, "dp", flip), 0)


def add_low(left_side, right_side):
    return (left_side.astype(f32) + right_side.astype(f32)).astype(bf16)


class Rows:
    def __init__(self):
        self.dp, self.mp = lax.axis_size("dp"), lax.axis_size("mp")
        flips = bits_below(self.dp)
        self.orders = flips, flips[1:2] + flips[:1] + flips[2:]
        self.steps = len(flips)

    def swap(self, values, step):
        pairs = [
            (i, ((i // self.mp) ^ self.orders[i % self.mp % 2][step]) * self.mp + i % self.mp)
            for i in range(self.dp * self.mp)
        ]
        return lax.ppermute(values, ("dp", "mp"), pairs)

    def bit(self, step):
        even, odd = (bit_of("dp", order[step]) for order in self.orders)
        return jnp.where(lax.axis_index("mp") % 2 == 1, odd, even)

    def cut(self, array, bit):
        arrays = array if isinstance(array, tuple) else (array,)
        half = arrays[0].shape[-2] // 2
        total = None
        for part in arrays:
            piece = lax.dynamic_slice_in_dim(part, bit * half, half, axis=-2).astype(f32)
            total = piece if total is None else total + piece
        return total

    def send(self, array, step):
        return self.swap(self.cut(array, 1 - self.bit(step)).astype(bf16), step)

    def keep(self, array, got, step):
        return (self.cut(array, self.bit(step)) + got.astype(f32)).astype(bf16)

    def join(self, array, got, step):
        return ordered(self.bit(step), array, got, array.ndim - 2)

    def gather(self, array, last):
        for step in reversed(range(last)):
            array = self.join(array, self.swap(array, step), step)
        return array

    def total(self, array):
        last = self.steps - 1
        for step in range(last):
            array = self.keep(array, self.send(array, step), step)
        array = add_low(array, self.swap(array, last))
        return self.gather(array, last)


class Running:
    def __init__(self, rows, array, plan):
        self.rows, self.array, self.plan = rows, array, plan

    def start(self):
        kind, step = self.plan[0]
        return self.rows.send(self.array, step) if kind == "send" else self.rows.swap(self.array, step)

    def finish(self, got):
        kind, step = self.plan.pop(0)
        if kind == "send":
            self.array = self.rows.keep(self.array, got, step)
        elif kind == "full":
            self.array = add_low(self.array, got)
        else:
            self.array = self.rows.join(self.array, got, step)


def params(cost=None, **more):
    return dict(
        compiler_params=pltpu.CompilerParams(vmem_limit_bytes=VMEM_BYTES, **more), cost_estimate=cost
    )


def cost(flops, moved, exps=0):
    return pl.CostEstimate(flops=int(flops), bytes_accessed=int(moved), transcendentals=int(exps))


def shape(dims, dtype=bf16):
    return jax.ShapeDtypeStruct(dims, dtype)


def shards(
    tokens, w_qkv, b_qv, w_out, b_out, norm1_gain, norm1_shift, w_in, b_in, w_back, b_back,
    norm2_gain, norm2_shift, segment_ids, pair_ids,
):
    row_count, length = segment_ids.shape
    width = tokens.shape[1]
    local = w_out.shape[0]
    units = w_in.shape[1]
    heads = local // HEAD_DIM
    blocks = length // Q_BLOCK
    member = lax.axis_index("mp")
    own_row = lax.axis_index("dp") * row_count + member
    m_arr = member.astype(jnp.int32).reshape(1)
    any_spec = pl.BlockSpec(memory_space=pl.ANY)
    vmem_spec = pl.BlockSpec(memory_space=pltpu.VMEM)
    smem_spec = pl.BlockSpec(memory_space=pltpu.SMEM)
    dma = pltpu.SemaphoreType.DMA

    tall = lambda vector: vector.reshape(-1, LANES)
    bit_x, bit_z = bit_of("dp", 1), bit_of("dp", 2)
    bits = jnp.stack([2 * bit_x + bit_z, 2 * bit_z + bit_x]).astype(jnp.int32)
    out_pack, in_quarter, back_quarter = pl.pallas_call(
        prepare,
        in_specs=[smem_spec] + [vmem_spec] * 2 + [any_spec] * 2,
        out_specs=[vmem_spec] * 3,
        out_shape=[
            shape((local + 16, width)), shape((width // 4, units)), shape((units // 4, width)),
        ],
        scratch_shapes=[dma((2,))],
        name="prepare",
        **params(cost(1e6, 2e6)),
    )(bits, tall(b_in), w_out, w_in, w_back)
    near_in, near_back = hop(w_in, "mp", 1), hop(w_back, "mp", 1)
    near_out = hop(out_pack, "mp", 1)
    far_out = hop(out_pack, "mp", 2)
    b_qv, near_in, near_back, near_out = together(b_qv, near_in, near_back, near_out)
    in_quarter = hop(in_quarter, "mp", 2)
    back_quarter = hop(back_quarter, "mp", 2)
    w_t = jnp.swapaxes(w_qkv, 1, 2)

    windows = jnp.stack(
        [segment_ids[:, window_start(i, length) :][:, :K_WINDOW] for i in range(blocks)], axis=1
    )
    seg_rows = segment_ids[:, None, :]

    def attend(count, source, place, held):
        return pl.pallas_call(
            functools.partial(attend_forward, len(held)),
            grid_spec=pltpu.PrefetchScalarGridSpec(
                num_scalar_prefetch=1,
                grid=(count,),
                in_specs=[
                    pl.BlockSpec((length, width), lambda i, m: (source(i) ^ m[0], 0)),
                    pl.BlockSpec(w_t.shape, lambda i, m: (0, 0, 0)),
                    pl.BlockSpec(b_qv.shape, lambda i, m: (0, 0)),
                    pl.BlockSpec((1, 1, length), lambda i, m: (source(i) ^ m[0], 0, 0)),
                    pl.BlockSpec((1, blocks, K_WINDOW), lambda i, m: (source(i) ^ m[0], 0, 0)),
                ]
                + [any_spec] * len(held),
                out_specs=[
                    pl.BlockSpec((1, 3, length, local), lambda i, m: (place + i, 0, 0, 0)),
                    pl.BlockSpec(
                        (1, heads * blocks, Q_BLOCK, K_WINDOW), lambda i, m: (place + i, 0, 0, 0)
                    ),
                ]
                + [pl.BlockSpec((length, local), lambda i, m: (0, 0))] * count,
                scratch_shapes=[pltpu.VMEM((length, local), bf16)],
            ),
            out_shape=[
                shape((row_count, 3, length, local)),
                shape((row_count, heads * blocks, Q_BLOCK, K_WINDOW)),
                *[shape((length, local))] * count,
            ],
            input_output_aliases={6 + i: i for i in range(len(held))},
            name="attend_forward",
            **params(cost(6 * count * length * width * local, 2e6 * count, count * heads * length * K_WINDOW)),
        )(m_arr, tokens, w_t, b_qv, seg_rows, windows, *held)

    qkv, probs, ctx3, ctx2, ctx1 = attend(3, lambda i: 3 - i, 0, ())
    ctx3, ctx2, ctx1, in_quarter, back_quarter, far_out = together(
        ctx3, ctx2, ctx1, in_quarter, back_quarter, far_out
    )
    in_got, back_got = hop(in_quarter, "dp", 2), hop(back_quarter, "dp", 1)
    qkv, probs, ctx0 = attend(1, lambda i: 0, 3, (qkv, probs))
    out_parts = [out_pack, near_out, far_out, hop(late(far_out, ctx0), "mp", 1)]
    ctx_got2, ctx_got3 = hop(ctx2, "mp", 2), hop(ctx3, "mp", 3)
    in_half = ordered(bit_z, in_quarter, late(in_got, ctx0), 0)
    back_half = ordered(bit_x, back_quarter, late(back_got, ctx0), 0)
    in_half, back_half, ctx_got2, ctx_got3 = together(in_half, back_half, ctx_got2, ctx_got3)
    ctx_parts = [ctx0, hop(ctx1, "mp", 1), ctx_got2, ctx_got3]
    seg_own = lax.dynamic_slice_in_dim(segment_ids, member, 1)
    pair_own = lax.dynamic_slice_in_dim(pair_ids, member, 1).reshape(-1, 1)
    pair_code = jnp.concatenate(
        [pair_own // 64, pair_own % 64, jnp.zeros((pair_own.shape[0], LANES - 2), jnp.int32)], axis=1
    ).astype(f32)
    in_got, back_got = hop(in_half, "dp", 1), hop(back_half, "dp", 2)
    act01, slope01, xhat1, rstd1, low1, total = pl.pallas_call(
        middle_first,
        in_specs=[smem_spec, any_spec] + [vmem_spec] * 3 + [any_spec] * 12,
        out_specs=[any_spec] * 2 + [vmem_spec] * 4,
        out_shape=[
            shape((2, length, units)), shape((2, length, units)),
            shape((length, width)), shape((length, LANES), f32), shape((length, width)),
            shape((length, width), f32),
        ],
        scratch_shapes=[
            pltpu.VMEM((length, width), bf16), pltpu.VMEM((4, length, local), bf16),
            pltpu.VMEM((4, local + 16, width), bf16), pltpu.VMEM((2, width, units), bf16),
            pltpu.VMEM((2, units, width), bf16), pltpu.VMEM((2, length, units), bf16),
            pltpu.VMEM((2, length, units), bf16), dma((13,)), dma((4,)),
        ],
        name="middle_first",
        **params(cost(2 * length * width * (width + 4 * units), 18e6, 2 * length * units)),
    )(
        m_arr, tokens, tall(b_out), tall(norm1_gain), tall(norm1_shift), *ctx_parts, *out_parts,
        w_in, near_in, w_back, near_back,
    )
    in_far = ordered(bit_x, in_half, late(in_got, total), 0)
    back_far = ordered(bit_z, back_half, late(back_got, total), 0)
    in_parts = [w_in, near_in, in_far, hop(in_far, "mp", 1)]
    back_parts = [w_back, near_back, back_far, hop(back_far, "mp", 1)]
    act23, slope23, xhat2, rstd2, out_own, pooled, lengths, msg = pl.pallas_call(
        middle_second,
        in_specs=[vmem_spec] * 6 + [any_spec] + [vmem_spec] * 2 + [any_spec] * 4,
        out_specs=[any_spec] * 2 + [vmem_spec] * 6,
        out_shape=[
            shape((2, length, units)), shape((2, length, units)),
            shape((length, width)), shape((length, LANES), f32), shape((length, width)),
            shape((16, width), f32), shape((16, LANES), f32), shape((8, 2 * width + LANES)),
        ],
        scratch_shapes=[
            pltpu.VMEM((2, width, units), bf16), pltpu.VMEM((2, units, width), bf16),
            pltpu.VMEM((2, length, units), bf16), pltpu.VMEM((2, length, units), bf16),
            pltpu.VMEM((length, width), f32), dma((5,)), dma((4,)),
        ],
        name="middle_second",
        **params(cost(8 * length * width * units, 12e6, 2 * length * units)),
    )(
        seg_own, pair_code, tall(b_back), tall(norm2_gain), tall(norm2_shift), low1, total,
        *out_parts[2:], *in_parts[2:], *back_parts[2:],
    )

    everyone = msg[None]
    steps = [("dp", flip) for flip in reversed(bits_below(lax.axis_size("dp")))]
    steps += [("mp", flip) for flip in reversed(bits_below(lax.axis_size("mp")))]
    while len(steps) > 1:
        everyone = four_ways(everyone, *steps[:2])
        steps = steps[2:]
    if steps:
        everyone = both_ways(everyone, hop(everyone, *steps[0]), *steps[0])
    everyone = everyone.reshape(-1, msg.shape[1])

    loss, grad_pooled = pl.pallas_call(
        contrast,
        in_specs=[smem_spec] + [vmem_spec] * 4,
        out_specs=[vmem_spec] * 2,
        out_shape=[shape((8, LANES), f32), shape((16, width), f32)],
        scratch_shapes=[pltpu.VMEM((everyone.shape[0], LANES), f32)],
        name="contrast",
        **params(cost(4e8, 2e6, 1e5)),
    )(own_row.astype(jnp.int32).reshape(1), everyone, msg, pooled, lengths)

    rows = Rows()
    grad_low2, vec2, back_send = pl.pallas_call(
        back_second,
        in_specs=[vmem_spec] * 5 + [any_spec] * 2,
        out_specs=[vmem_spec] * 3,
        out_shape=[
            shape((length, width)), shape((8, width), f32),
            shape((2, units, width)),
        ],
        scratch_shapes=[
            pltpu.VMEM((length, width), f32), pltpu.VMEM((2, length, units), bf16),
            pltpu.VMEM((3, 8, width), f32), dma((2,)),
        ],
        name="back_second",
        **params(cost(4 * length * width * units, 14e6)),
    )(grad_pooled, seg_own, xhat2, rstd2, tall(norm2_gain), act01, act23)
    back_got = hop(back_send, "mp", 1)
    back_keep = pl.pallas_call(
        back_outer,
        in_specs=[vmem_spec] + [any_spec] * 2,
        out_specs=vmem_spec,
        out_shape=shape((2, units, width)),
        scratch_shapes=[pltpu.VMEM((2, length, units), bf16), dma((2,))],
        name="back_outer",
        **params(cost(4 * length * width * units, 8e6)),
    )(grad_low2, act01, act23)
    grad_low2, back_keep, back_got = together(grad_low2, back_keep, back_got)
    back_sum = back_keep, back_got
    back_got = rows.send(back_sum, 0)
    out_far = hop(late(out_own, grad_low2), "mp", 2)

    gb, attn_low, vec1, d_bin, *ctx_grads = pl.pallas_call(
        back_first,
        in_specs=[vmem_spec] * 4 + [any_spec] * 14,
        out_specs=[any_spec] + [vmem_spec] * 7,
        out_shape=[
            shape((4, length, units)), shape((length, width)),
            shape((8, width), f32), shape((4, units), f32), *[shape((length, local))] * 4,
        ],
        scratch_shapes=[
            pltpu.VMEM((4, length, units), bf16), pltpu.VMEM((4, local + 16, width), bf16),
            pltpu.VMEM((4, width, units), bf16), pltpu.VMEM((4, units, width), bf16),
            pltpu.VMEM((4, length, units), bf16), pltpu.VMEM((length, width), f32),
            pltpu.VMEM((3, 8, width), f32), dma((16,)), dma((4,)),
        ],
        name="back_first",
        **params(cost(2 * length * width * (width + 8 * units), 25e6)),
    )(
        grad_low2, xhat1, rstd1, tall(norm1_gain), slope01, slope23, *out_parts, *in_parts, *back_parts,
    )

    attn_low, back_got, out_far, *back_sum = together(attn_low, back_got, out_far, *back_sum)
    out_pair = ordered(bit_of("mp", 2), out_own[None], out_far[None], 0)
    back_sum = rows.keep(tuple(back_sum), back_got, 0)
    got3 = hop(ctx_grads[3], "mp", 3)

    def first_grads(pieces, low):
        return pl.pallas_call(
            functools.partial(weight_grads, pieces),
            in_specs=[vmem_spec] * 7 + [any_spec],
            out_specs=vmem_spec,
            out_shape=shape((2, width + local + VEC_ROWS, units)),
            scratch_shapes=[pltpu.VMEM((2, length, units), bf16), dma((2,))],
            name="weight_grads",
            **params(cost(4 * length * width * (units + local), 7e6)),
        )(low1, low, vec1, vec2, d_bin, ctx_parts[pieces[0]], ctx_parts[pieces[1]], gb)

    first_send = first_grads((3, 1), attn_low)
    got3, attn_low, first_send, out_pair = together(got3, attn_low, first_send, out_pair)
    out_other = hop(out_pair, "mp", 1)
    first_got = hop(first_send, "mp", 1)
    got2 = hop(late(ctx_grads[2], first_send), "mp", 2)
    back_sum = late(back_sum, first_send)
    back_got = rows.send(back_sum, 1)
    first_keep = first_grads((2, 0), attn_low)
    own_grad, first_keep, first_got, got2, back_got, out_other = together(
        ctx_grads[0], first_keep, first_got, got2, back_got, out_other
    )
    back_sum = rows.keep(back_sum, back_got, 1)
    first_far = hop(add_low(first_keep[0], first_got[0]), "mp", 2)
    back_got = rows.send(back_sum, 2)
    got1 = hop(late(ctx_grads[1], own_grad), "mp", 1)

    def attend_back(count, source, place, last, grads, sums):
        same = lambda i, m: (0, 0)
        out_specs = [pl.BlockSpec((length, width), same)] * count
        out_shape = [shape((length, width))] * count
        if last:
            out_specs.append(pl.BlockSpec((3 * local + VEC_ROWS, width), same))
            out_shape.append(shape((3 * local + VEC_ROWS, width)))
        else:
            out_specs += [pl.BlockSpec((3 * local, width), same), pl.BlockSpec((8, local), same)]
            out_shape += [shape((3 * local, width), f32), shape((8, local), f32)]
        return pl.pallas_call(
            functools.partial(attend_backward, count, len(sums) == 0, last),
            grid_spec=pltpu.PrefetchScalarGridSpec(
                num_scalar_prefetch=1,
                grid=(count,),
                in_specs=[
                    pl.BlockSpec((length, width), lambda i, m: (source(i) ^ m[0], 0)),
                    pl.BlockSpec(w_t.shape, lambda i, m: (0, 0, 0)),
                    pl.BlockSpec((1, 3, length, local), lambda i, m: ((place + i) % row_count, 0, 0, 0)),
                    pl.BlockSpec(
                        (1, heads * blocks, Q_BLOCK, K_WINDOW), lambda i, m: ((place + i) % row_count, 0, 0, 0)
                    ),
                ]
                + [pl.BlockSpec((length, local), same)] * count
                + [pl.BlockSpec(part.shape, same) for part in sums],
                out_specs=out_specs,
                scratch_shapes=[
                    pltpu.VMEM((length, local), bf16), pltpu.VMEM((length, local), f32),
                    pltpu.VMEM((length, local), f32), pltpu.VMEM((3 * local, width), f32),
                    pltpu.VMEM((8, local), f32),
                ],
            ),
            out_shape=out_shape,
            name="attend_backward",
            **params(cost(12 * count * length * width * local, 4e6 * count)),
        )(m_arr, tokens, w_t, qkv, probs, *grads, *sums)

    back0, back3, *sums = attend_back(2, lambda i: 3 * i, 3, False, [own_grad, got3], [])
    back_got, got1, back3, *sums = together(back_got, got1, back3, *sums)
    back_sum = rows.keep(back_sum, back_got, 2)
    for step in range(3, rows.steps):
        back_sum = rows.keep(back_sum, rows.send(back_sum, step), step)
    back_got = hop(back_sum[0], "mp", 2)
    tok_got3 = hop(back3, "mp", 1)
    back2, back1, d_qkv = attend_back(2, lambda i: 2 - i, 1, True, [got2, got1], sums)
    first_far, first_keep, first_got, back_got, _ = together(
        first_far, first_keep, first_got, back_got, d_qkv
    )
    back_sum = add_low(back_sum[1], back_got)
    first_sum = (first_keep[1].astype(f32) + first_got[1].astype(f32) + first_far.astype(f32)).astype(bf16)
    last = rows.steps - 1
    tok_got1 = hop(back1, "mp", 1)
    far = add_low(back2, tok_got3)
    down = [("send", step) for step in range(last)] + [("full", last)]
    up = [("join", step) for step in reversed(range(last))]
    sums = [
        Running(rows, first_sum, down + up),
        Running(rows, d_qkv, down + up),
        Running(rows, back_sum, [("join", last)] + up),
    ]
    stage, extra = 0, [tok_got1, hop(far, "mp", 2)]
    while any(part.plan for part in sums):
        parts = [part for part in sums if part.plan and not (part is sums[2] and stage == 1)]
        if stage == 2:
            sums[2].array = late(sums[2].array, sums[0].array)
        if stage == 2:
            sums[1].array = late(sums[1].array, sums[0].array)
        starts = [part.start() for part in parts]
        if stage == 0:
            starts[2], *extra = together(starts[2], *extra)
        hops = starts + extra
        for part in parts:
            part.finish(hops.pop(0))
        if stage == 0:
            own = back0.astype(f32) + attn_low.astype(f32) + hops[0].astype(f32) + hops[1].astype(f32)
            own = own.astype(bf16)
            extra = [hop(own, "mp", 2)]
        elif stage == 1:
            tok_pair = ordered(bit_of("mp", 2), own[None], hops[0][None], 0)
            extra = [hop(tok_pair, "mp", 1)]
        elif stage == 2:
            d_tokens = rows_of_all(tok_pair, hops[0])
            extra = []
        stage += 1
    sum_first, sum_qkv, sum_back = (part.array for part in sums)
    layer_out = rows_of_all(out_pair, out_other)

    at = width + local
    vectors = sum_first[at : at + 8].astype(f32) + sum_first[at + 8 : at + 16].astype(f32)
    shares = lax.dynamic_slice_in_dim(vectors[0:6], member * local, local, axis=1)
    at = 3 * local
    d_bqv = sum_qkv[at : at + 2, 0:local].astype(f32) + sum_qkv[at + 8 : at + 10, 0:local].astype(f32)
    d_wqkv = jnp.swapaxes(sum_qkv[0:at].reshape(3, local, width), 1, 2).astype(f32)
    return (
        loss[0, 0],
        layer_out,
        d_tokens,
        d_wqkv,
        d_bqv,
        sum_first[width : width + local].astype(f32),
        shares[2],
        shares[0],
        shares[1],
        sum_first[0:width].astype(f32),
        vectors[6],
        sum_back.astype(f32),
        shares[5],
        shares[3],
        shares[4],
    )


def both_ways(array, other, axis, flip):
    low_first = jnp.stack([array, other], axis=1)
    high_first = jnp.stack([other, array], axis=1)
    joined = jnp.where(bit_of(axis, flip) == 0, low_first, high_first)
    return joined.reshape(-1, *array.shape[1:])


def four_ways(array, first, second):
    dp, mp = lax.axis_size("dp"), lax.axis_size("mp")

    def fetch(*steps):
        flip = sum(step * (mp if axis == "dp" else 1) for axis, step in steps)
        return lax.ppermute(array, ("dp", "mp"), [(i, i ^ flip) for i in range(dp * mp)])

    far, near, corner = fetch(first), fetch(second), fetch(first, second)
    count = array.shape[0]
    mine = both_ways(array, near, *second).reshape(count, 2, *array.shape[1:])
    theirs = both_ways(far, corner, *second).reshape(count, 2, *array.shape[1:])
    return both_ways(mine, theirs, *first).reshape(-1, *array.shape[1:])


def rows_of_all(pair, other):
    low_first = jnp.stack([pair, other], axis=1)
    high_first = jnp.stack([other, pair], axis=1)
    joined = jnp.where(bit_of("mp", 1) == 0, low_first, high_first)
    return joined.reshape(-1, pair.shape[-1])


def solution(mesh):
    return jax.shard_map(
        shards,
        mesh=mesh,
        in_specs=(
            P("dp", None),
            P(None, None, "mp"),
            P(None, "mp"),
            P("mp", None),
            P(),
            P(),
            P(),
            P(None, "mp"),
            P("mp"),
            P("mp", None),
            P(),
            P(),
            P(),
            P("dp", None),
            P("dp", None),
        ),
        out_specs=(
            P(),
            P("dp", None),
            P("dp", None),
            P(None, None, "mp"),
            P(None, "mp"),
            P("mp", None),
            P("mp"),
            P("mp"),
            P("mp"),
            P(None, "mp"),
            P("mp"),
            P("mp", None),
            P("mp"),
            P("mp"),
            P("mp"),
        ),
        check_vma=False,
    )
```
